32 devices in a mesh: slab: 16 (over z, x, core), dom: 2 (over y).
Axes of the slice: x: 2, y: 2, z: 4, core: 2. Of those that a mesh axis runs over, the one named last changes fastest.
Arguments:
- positions: float32 [3, 196608], P(None, ('slab', 'dom')), may hold values from -6 to 6
- velocities: float32 [3, 196608], P(None, ('slab', 'dom')), may hold values from -6 to 6
- masses: float32 [196608], P(('slab', 'dom')), may hold values from 0.2 to 2
- owner_cell: int32 [196608, 1], P(('slab', 'dom')), may hold values from 0 to 127; in each aligned block of 6144 rows (0 to 6143, 6144 to 12287, ...) at most 64 rows name the same one
- counts: int32 [32], P(('slab', 'dom')), may hold values from 3072 to 6144, as said below
Outputs:
- state: float32 [10, 16, 128, 128], P(None, 'slab', 'dom')
- buddy: float32 [10, 16, 128, 128], P(None, 'slab', 'dom')
The draws below stay inside these ranges and needn't reach their ends.
Inputs may be any that keep to these rules, and one draw needn't show every extreme that they name: owner_cell is the partner index of the owner times 64 plus its cell; among the rows of one device no value appears more than 64 times, and some device's rows name one value exactly 64 times. `counts`: some device has all 6144 rows live.
All inputs are finite; a program needn't handle non-finite values.
Results may differ from the reference program's by a relative error of at most 0.0003.
Values sent between devices are 32-bit elements; how exact they have to be, the bound alone decides.
No kernel may reach another device: no remote copies, remote signals or barrier semaphores. Data moves between devices by JAX's collectives and lax.ppermute only.
A program may use at most 64 MiB of HBM per device.

```python
import math
import jax
import jax.numpy as jnp
import numpy as np
from jax import lax

CELLS = 64
TILE = 128
PART_DEV = 6144
SLOT = 64
NCELL = 128
GROUPS = 32
PARTICLES = 196608
N_SLAB = 16
N_DOM = 2


def draw_counts(key, part):
    values = jax.random.randint(key, (GROUPS,), PART_DEV // 2, PART_DEV + 1)
    chosen = jax.random.randint(jax.random.fold_in(key, 7), (), 0, GROUPS)
    return jnp.where(jnp.arange(GROUPS) == chosen, PART_DEV, values).astype(jnp.int32)


def block_scale(key, extent, shards, low, largest):
    loudness = 1.0
    for dim, shards_of in shards:
        draws = jax.random.uniform(jax.random.fold_in(jax.random.fold_in(key, 6), dim), (shards_of,), jnp.float32, low / len(shards), largest / len(shards))
        loudness = loudness * jnp.repeat(jnp.exp(draws), extent[dim] // shards_of).reshape((-1,) + (1,) * (len(extent) - 1 - dim))
    return loudness


def routed_block(own_key, own, number, rows, count, top, bound, lean):
    sequence = jax.random.permutation(own_key, count)
    heavy_load, usual = shares(count, rows * top, bound, lean, True), shares(count, rows * top, bound, lean, False)
    places = jnp.arange(count)

    def named(sizes, turn):
        used = int((sizes > 0).sum())
        fixed = max(1, used // 4)
        shifted = fixed + (places - fixed + turn * (used - fixed)) % max(1, count - fixed)
        return jnp.zeros((count,), jnp.int32).at[sequence[jnp.where(places < fixed, places, shifted)]].set(jnp.asarray(sizes, jnp.int32))

    sizes = jnp.where(number % 4 == 0, named(heavy_load, number // 4), named(usual, number - number // 4 - 1))
    mixed = jax.random.permutation(jax.random.fold_in(own, 3), count)
    donor, taker = mixed[0:count // 2 * 2:2], mixed[1:count // 2 * 2:2]
    margin = jnp.minimum(sizes[donor] - 1, bound - sizes[taker]) // 2
    margin = jnp.where((donor == sequence[0]) | (taker == sequence[0]) | (sizes[taker] == 0), 0, jnp.maximum(margin, 0))
    shifted = jax.random.randint(jax.random.fold_in(own, 4), (count // 2,), 0, 1 << 20) % (margin + 1)
    sizes = sizes.at[donor].add(-shifted).at[taker].add(shifted)
    members = jnp.searchsorted(jnp.cumsum(sizes), jnp.arange(rows * top), side="right").astype(jnp.int32)
    grid = members.reshape(top, rows).T
    grid = grid[jax.random.permutation(jax.random.fold_in(own, 1), rows)]
    turn = jax.random.randint(jax.random.fold_in(own, 2), (rows, 1), 0, top)
    return jnp.take_along_axis(grid, (jnp.arange(top)[None, :] + turn) % top, axis=1)


def shares(amount, total, most, skew, full):
    portions = [(1 << 20) // math.isqrt(standing ** skew) + 1 for standing in range(1, amount + 1)]
    largest = most if full else min(most, max(-(-total // amount), total * portions[0] // sum(portions)))
    least = 1 if total - largest >= amount - 1 else 0
    holding, spare = [largest] + [least] * (amount - 1), total - largest - least * (amount - 1)
    while spare > 0:
        candidates = [i for i in range(1, amount) if holding[i] < largest] or [i for i in range(1, amount) if holding[i] < most]
        whole, budget = sum([portions[i] for i in candidates]), spare
        for i in candidates:
            addition = min(most - holding[i], max(1, budget * portions[i] // whole), spare)
            holding[i] = holding[i] + addition
            spare = spare - addition
    return np.array(holding)


def normal_values(own_key, extent, deviation, bound, cuts=(), held_as=jnp.bfloat16):
    gain = block_scale(own_key, extent, cuts, -0.22, 0.18) if cuts else 1.0
    values = jax.random.normal(own_key, extent, jnp.float32) * deviation * gain
    return jnp.minimum(jnp.maximum(values, -bound), bound).astype(held_as)


def setup_inputs(seed: int = 0) -> dict:
    seeds = jax.random.split(jax.random.key(seed), 6)
    positions = normal_values(seeds[0], (3, PARTICLES), 1.0, 6.0, ((1, 32),), jnp.float32)
    velocities = normal_values(seeds[1], (3, PARTICLES), 1.0, 6.0, ((1, 32),), jnp.float32)
    masses = jnp.clip(jnp.exp(math.log(2.0) - 2.3025851 * jax.random.uniform(seeds[2], (PARTICLES,), jnp.float32) ** block_scale(seeds[2], (PARTICLES,), ((0, 32),), -0.2, 0.2)), 0.2, 2.0)
    owner_cell_keys = jax.random.split(jax.random.fold_in(seeds[3], 1), PARTICLES // PART_DEV)
    owner_cell_turns = jax.random.permutation(jax.random.fold_in(seeds[3], 3), PARTICLES // PART_DEV)
    owner_cell = jax.vmap(lambda own, number: routed_block(jax.random.fold_in(seeds[3], 2), own, number, PART_DEV, NCELL, 1, SLOT, 2))(owner_cell_keys, owner_cell_turns).reshape((PARTICLES, 1))
    counts = draw_counts(jax.random.fold_in(seeds[5], 71), 0)
    return dict(positions=positions, velocities=velocities, masses=masses, owner_cell=owner_cell, counts=counts)


drift_step = 0.5
kick_step = 0.5
soften = 0.25
reach = 4.0
coupling = 0.25

def pair_accel(centre, others):
    separation = others[:3, None, :] - centre[:3, :, None]
    distance = lax.optimization_barrier(jnp.sum(separation * separation, axis=0))
    inverse = lax.rsqrt(distance + soften)
    weight = others[3][None, :] * jnp.exp(-distance / reach) * inverse * inverse * inverse
    return coupling * lax.optimization_barrier(jnp.sum(weight[None] * separation, axis=2))

def reference(positions, velocities, masses, owner_cell, counts):
    groups = N_SLAB * N_DOM
    lanes = TILE // N_DOM
    moved = positions + drift_step * velocities
    payload = jnp.concatenate([moved, masses[None, :], velocities], axis=0)
    per_device = payload.reshape(7, groups, PART_DEV).transpose(1, 0, 2)
    targets_all = owner_cell[:, 0].reshape(groups, PART_DEV)
    targets = N_DOM * CELLS

    def pack(pieces):
        rows_here, target, limit = pieces
        active = jnp.arange(PART_DEV, dtype=jnp.int32) < limit
        hits = ((target[:, None] == jnp.arange(targets, dtype=jnp.int32)[None, :]) & active[:, None]).astype(jnp.int32)
        ranking = lax.optimization_barrier(jnp.sum(jnp.cumsum(hits, axis=0) * hits, axis=1)) - 1
        place = jnp.where(active, target * lanes + ranking, targets * lanes).astype(jnp.int32)
        buffer = jnp.zeros((7, targets * lanes), jnp.float32).at[:, place].set(rows_here, mode='drop')
        return buffer.reshape(7, N_DOM, CELLS, lanes)
    sent = lax.map(pack, (per_device, targets_all, counts))
    ncell = N_DOM * CELLS
    sorted_rows = sent.reshape(N_SLAB, N_DOM, 7, N_DOM, CELLS, lanes).transpose(2, 0, 3, 4, 1, 5).reshape(7, N_SLAB, ncell, TILE)
    padded = jnp.pad(sorted_rows[:4], ((0, 0), (1, 1), (1, 1), (0, 0)), mode='wrap')

    def cell_accel(number):
        slab_index = number // ncell
        cell_index = number % ncell
        zero = jnp.zeros((), jnp.int32)
        block = lax.dynamic_slice(padded, (zero, slab_index, cell_index, zero), (4, 3, 3, TILE)).reshape(4, 9 * TILE)
        centre = lax.dynamic_slice(padded, (zero, slab_index + 1, cell_index + 1, zero), (4, 1, 1, TILE)).reshape(4, TILE)
        return pair_accel(centre, block)
    accel = lax.map(cell_accel, jnp.arange(N_SLAB * ncell, dtype=jnp.int32), batch_size=64)
    accel = accel.reshape(N_SLAB, ncell, 3, TILE).transpose(2, 0, 1, 3)
    occupied = (sorted_rows[3:4] > 0).astype(jnp.float32)
    accel = accel * occupied
    state = jnp.concatenate([sorted_rows[:4], sorted_rows[4:7] + kick_step * accel, accel], axis=0)
    buddy = jnp.roll(state, -(N_SLAB // 2), axis=1)
    return (state, buddy)
```

```python
import functools
import math

import jax
import jax.numpy as jnp
from jax import lax
from jax.experimental import pallas as pl
from jax.experimental.pallas import tpu as pltpu
from jax.sharding import PartitionSpec as P

CELLS = 64
LANES = 128

drift_step = 0.5
kick_step = 0.5
soften = 0.25
reach = 4.0
coupling = 0.25

scale = math.log2(math.e) / reach
fold = scale**1.5 * math.exp(soften / reach)

f32 = jnp.float32
bf16 = jnp.bfloat16
NN = (((1,), (0,)), ((), ()))
NT = (((1,), (1,)), ((), ()))
TN = (((0,), (0,)), ((), ()))
FEATURES = 32
EDGES = 8


def split(value, pieces):
    parts = []
    for _ in range(pieces):
        head = value.astype(bf16).astype(f32)
        parts.append(head)
        value = value - head
    return parts


def pack_kernel(n_dom, me_ref, count_ref, pos_ref, vel_ref, mass_ref, owner_ref, *refs):
    outs, (hot_ref, rank_ref, total_ref) = refs[:-3], refs[-3:]
    rows = pos_ref.shape[1]
    targets, lanes = n_dom * CELLS, LANES // n_dom
    chunk = 256
    before = (
        lax.broadcasted_iota(jnp.int32, (chunk, chunk + LANES), 0)
        < lax.broadcasted_iota(jnp.int32, (chunk, chunk + LANES), 1)
    ).astype(f32).astype(bf16)
    carry = jnp.zeros((targets, LANES), f32)
    number = lax.broadcasted_iota(jnp.int32, (targets, chunk), 0)
    for at in range(0, rows, chunk):
        target = owner_ref[:, at : at + chunk] - me_ref[0] * CELLS
        target = jnp.where(target < 0, target + targets, target)
        place = lax.broadcasted_iota(jnp.int32, (1, chunk), 1) + at
        target = jnp.where(place < count_ref[0], target, -1)
        same = number == target
        hot = jnp.where(same, 1.0, 0.0).astype(bf16)
        hot_ref[:, at : at + chunk] = hot
        seen = lax.dot_general(hot, before, NN, preferred_element_type=f32)
        wide = jnp.concatenate([carry] * (chunk // LANES), axis=1)
        rank = jnp.sum(jnp.where(same, seen[:, :chunk] + wide, 0.0), axis=0, keepdims=True)
        rank_ref[:, at : at + chunk] = rank.astype(jnp.int32)
        carry = carry + seen[:, chunk:]
    step = 1024
    row = lax.broadcasted_iota(jnp.int32, (lanes, step), 0)
    for at in range(0, rows, step):
        span = slice(at, at + step)
        mark = jnp.where(row == rank_ref[:, span], 1.0, 0.0)
        values = [pos_ref[i : i + 1, span] + drift_step * vel_ref[i : i + 1, span] for i in range(3)]
        values += [mass_ref[:, span]]
        values += [vel_ref[i : i + 1, span] for i in range(3)]
        pieces = [split(value, 3) for value in values]
        hot = hot_ref[:, span]
        left = [
            jnp.concatenate([(mark * piece[k]).astype(bf16) for piece in pieces], axis=0)
            for k in range(3)
        ]
        part = lax.dot_general(
            jnp.concatenate(left, axis=1),
            jnp.concatenate([hot] * 3, axis=1),
            NT,
            preferred_element_type=f32,
        )
        size = 7 * lanes
        if at == 0:
            total_ref[:size] = part
            total_ref[size:] = jnp.zeros((lanes, targets), f32)
        else:
            total_ref[:size] += part
    groups = 8 * lanes // LANES
    half = groups // 2
    packed = [
        jnp.concatenate(
            [
                total_ref[g * LANES : (g + 1) * LANES, t : t + LANES].T
                for t in range(0, targets, LANES)
            ],
            axis=0,
        )
        for g in range(groups)
    ]
    for by in range(n_dom):
        low, high = by * CELLS, (by + 1) * CELLS
        edge_high, edge_low = high % targets, (low - 1) % targets
        for g in range(groups):
            edges = jnp.concatenate(
                [
                    packed[g][edge_high : edge_high + 1],
                    packed[g][edge_low : edge_low + 1],
                    jnp.zeros((EDGES - 2, LANES), f32),
                ],
                axis=0,
            )
            both = jnp.concatenate([packed[g][low:high], edges], axis=0)
            outs[by][g] = both
            if g < half:
                outs[n_dom + by][g] = both


def merged(pieces, comp, n_dom):
    lanes = LANES // n_dom
    group, inside = comp // n_dom, comp % n_dom
    plane = None
    for k, piece in enumerate(pieces):
        value = piece[group]
        shift = ((k - inside) % n_dom) * lanes
        if shift:
            value = pltpu.roll(value, shift, 1)
        if plane is None:
            plane = value
        else:
            lane = lax.broadcasted_iota(jnp.int32, value.shape, 1)
            plane = jnp.where(lane // lanes == k, value, plane)
    return plane


def put_rows(ref, slab, k, plane, stride):
    for at in range(0, CELLS, 8):
        ref[slab, pl.ds((at + 1) * stride + k, 8, stride=stride), :] = plane[at : at + 8]
    ref[slab, pl.ds((CELLS + 1) * stride + k, 1), :] = plane[CELLS : CELLS + 1]
    ref[slab, pl.ds(k, 1), :] = plane[CELLS + 1 : CELLS + 2]


def pair_kernel(n_dom, me_ref, *refs):
    n_in = 3 * n_dom
    ins, (state_ref, accel_ref) = refs[:n_in], refs[n_in : n_in + 2]
    far, near, summed, centre_rows, far_rows, sum_rows, out_rows, *work = refs[n_in + 2 :]
    dist, heavy, light = work[0:2], work[2:4], work[4:6]
    root = math.sqrt(scale)
    weight = coupling * fold / root
    own = None
    for slab in range(3):
        pieces = ins[slab * n_dom : (slab + 1) * n_dom]
        planes = [merged(pieces, comp, n_dom) for comp in range(4)]
        if slab == 1:
            own = [plane[:CELLS] for plane in planes]
        x = [plane * root for plane in planes[:3]]
        norm = x[0] * x[0] + x[1] * x[1] + x[2] * x[2]
        one, none = jnp.ones_like(norm), jnp.zeros_like(norm)
        cut = [split(value, 3) for value in x]
        far_feat, near_feat = [], []
        for h, m, l in cut:
            far_feat += [h, m, h, l, h, m]
            near_feat += [-2.0 * v for v in (h, h, m, h, l, m)]
        far_feat += [one] * 3 + split(norm, 3)
        near_feat += split(norm + scale * soften, 3) + [one] * 3
        for k in range(FEATURES):
            put_rows(far, slab, k, far_feat[k] if k < len(far_feat) else none, FEATURES)
            if slab == 1:
                value = near_feat[k] if k < len(near_feat) else none
                put_rows(near, 0, k, value, FEATURES)
        mass = planes[3] * weight
        terms = [split(mass * value, 3) for value in x] + [split(mass, 3)]
        for comp in range(4):
            for k in range(3):
                put_rows(summed, slab, 3 * comp + k, terms[comp][k], 16)
        for k in range(12, 16):
            put_rows(summed, slab, k, none, 16)

    def cast(e, _):
        for slab in range(3):
            rows = pl.ds(pl.multiple_of(e * FEATURES, FEATURES), FEATURES)
            far_rows[e, slab] = far[slab, rows, :].astype(bf16)
            sums = pl.ds(pl.multiple_of(e * 16, 16), 16)
            sum_rows[e, slab] = summed[slab, sums, :].astype(bf16)
        centre_rows[e] = near[0, rows, :].astype(bf16)
        return 0

    lax.fori_loop(0, CELLS + 2, cast, 0)

    def distances(c, b):
        for k in range(3):
            others = jnp.concatenate([far_rows[c + k, slab] for slab in range(3)], axis=1)
            dist[b][k * 384 : (k + 1) * 384] = lax.dot_general(
                others, centre_rows[c + 1], TN, preferred_element_type=f32
            )

    def weights(b):
        s = dist[b][...]
        inverse = lax.rsqrt(s)
        w = jnp.exp2(-s) * (inverse * inverse * inverse)
        head = w.astype(bf16)
        heavy[b][...] = head
        light[b][...] = (w - head.astype(f32)).astype(bf16)

    def sums(c, b):
        terms = jnp.concatenate(
            [sum_rows[c + k, slab] for k in range(3) for slab in range(3)], axis=1
        )
        total = lax.dot_general(terms, heavy[b][...], NN, preferred_element_type=f32)
        total += lax.dot_general(terms, light[b][...], NN, preferred_element_type=f32)
        out_rows[pl.ds(pl.multiple_of(c * 16, 16), 16), :] = total

    distances(0, 0)
    distances(1, 1)
    weights(0)

    def body(i, _):
        for b in range(2):
            c = 2 * i + b
            sums(c, b)
            distances(jnp.minimum(c + 2, CELLS - 1), b)
            weights(1 - b)
        return 0

    lax.fori_loop(0, CELLS // 2, body, 0)
    rows = [out_rows[pl.ds(k, CELLS, stride=16), :] for k in range(12)]
    total = [rows[3 * comp] + rows[3 * comp + 1] + rows[3 * comp + 2] for comp in range(4)]
    live = own[3] > 0
    turn = me_ref[0] * (LANES // n_dom)
    pieces = ins[n_dom : 2 * n_dom]
    for comp in range(3):
        accel = jnp.where(live, total[comp] - (own[comp] * root) * total[3], 0.0)
        accel = pltpu.roll(accel, turn, 1)
        speed = pltpu.roll(merged(pieces, 4 + comp, n_dom)[:CELLS], turn, 1)
        state_ref[comp, 0] = pltpu.roll(own[comp], turn, 1)
        state_ref[4 + comp, 0] = speed + kick_step * accel
        state_ref[7 + comp, 0] = accel
        accel_ref[comp] = accel
    state_ref[3, 0] = pltpu.roll(own[3], turn, 1)


def buddy_kernel(n_dom, me_ref, *refs):
    pieces, accel_ref, out_ref = refs[:n_dom], refs[n_dom], refs[n_dom + 1]
    turn = me_ref[0] * (LANES // n_dom)
    for comp in range(7):
        plane = pltpu.roll(merged(pieces, comp, n_dom)[:CELLS], turn, 1)
        if comp >= 4:
            accel = accel_ref[comp - 4]
            plane = plane + kick_step * accel
            out_ref[3 + comp, 0] = accel
        out_ref[comp, 0] = plane


def call(kernel, n_smem, n_vmem, out_shape, scratch=(), name=None, cost=None):
    smem = pl.BlockSpec(memory_space=pltpu.SMEM)
    vmem = pl.BlockSpec(memory_space=pltpu.VMEM)
    return pl.pallas_call(
        kernel,
        in_specs=[smem] * n_smem + [vmem] * n_vmem,
        out_specs=jax.tree.map(lambda _: vmem, out_shape),
        out_shape=out_shape,
        scratch_shapes=scratch,
        name=name,
        compiler_params=pltpu.CompilerParams(vmem_limit_bytes=48 << 20),
        cost_estimate=cost,
    )


def sent(value, n_slab, n_dom, by_slab, by_dom):
    pairs = [
        (s * n_dom + d, (s + by_slab) % n_slab * n_dom + (d + by_dom) % n_dom)
        for s in range(n_slab)
        for d in range(n_dom)
    ]
    return lax.ppermute(value, ("slab", "dom"), pairs)


def per_device(positions, velocities, masses, owner_cell, counts):
    n_slab, n_dom = lax.axis_size("slab"), lax.axis_size("dom")
    rows = positions.shape[1]
    lanes = LANES // n_dom
    targets = n_dom * CELLS
    groups = 8 * lanes // LANES
    half = groups // 2
    tall = CELLS + EDGES
    me = lax.axis_index("dom").astype(jnp.int32).reshape(1)
    shape = lambda *dims, dtype=f32: jax.ShapeDtypeStruct(dims, dtype)

    packed = call(
        functools.partial(pack_kernel, n_dom),
        2,
        4,
        [shape(groups, tall, LANES)] * n_dom + [shape(half, tall, LANES)] * n_dom,
        [
            pltpu.VMEM((targets, rows), bf16),
            pltpu.VMEM((1, rows), jnp.int32),
            pltpu.VMEM((8 * lanes, targets), f32),
        ],
        name="pack",
    )(me, counts, positions, velocities, masses.reshape(1, rows), owner_cell.reshape(1, rows))
    whole, shells = packed[:n_dom], packed[n_dom:]

    own = [whole[0]] + [sent(whole[-k % n_dom], n_slab, n_dom, 0, -k) for k in range(1, n_dom)]
    halo = {
        side: [sent(shells[-k % n_dom], n_slab, n_dom, side, -k) for k in range(n_dom)]
        for side in (1, -1)
    }
    early = [sent(piece, n_slab, n_dom, n_slab // 2, 0) for piece in own]
    state, accel = call(
        functools.partial(pair_kernel, n_dom),
        1,
        3 * n_dom,
        [shape(10, 1, CELLS, LANES), shape(3, CELLS, LANES)],
        [
            pltpu.VMEM((3, (CELLS + 2) * FEATURES, LANES), f32),
            pltpu.VMEM((1, (CELLS + 2) * FEATURES, LANES), f32),
            pltpu.VMEM((3, (CELLS + 2) * 16, LANES), f32),
            pltpu.VMEM((CELLS + 2, FEATURES, LANES), bf16),
            pltpu.VMEM((CELLS + 2, 3, FEATURES, LANES), bf16),
            pltpu.VMEM((CELLS + 2, 3, 16, LANES), bf16),
            pltpu.VMEM((CELLS * 16, LANES), f32),
        ]
        + [pltpu.VMEM((1152, LANES), f32)] * 2
        + [pltpu.VMEM((1152, LANES), bf16)] * 4,
        name="pairs",
    )(me, *halo[1], *own, *halo[-1])
    later = sent(accel, n_slab, n_dom, n_slab // 2, 0)
    buddy = call(
        functools.partial(buddy_kernel, n_dom),
        1,
        n_dom + 1,
        shape(10, 1, CELLS, LANES),
        name="buddy",
    )(me, *early, later)
    return state, buddy


def solution(mesh):
    placed = (
        P(None, ("slab", "dom")),
        P(None, ("slab", "dom")),
        P(("slab", "dom")),
        P(("slab", "dom"), None),
        P(("slab", "dom")),
    )
    return jax.shard_map(
        per_device,
        mesh=mesh,
        in_specs=placed,
        out_specs=(P(None, "slab", "dom", None), P(None, "slab", "dom", None)),
        check_vma=False,
    )
```

```python
import functools
import math

import jax
import jax.numpy as jnp
from jax import lax
from jax.experimental import pallas as pl
from jax.experimental.pallas import tpu as pltpu
from jax.sharding import PartitionSpec as P

CELLS = 64
LANES = 128

drift_step = 0.5
kick_step = 0.5
soften = 0.25
reach = 4.0
coupling = 0.25

scale = math.log2(math.e) / reach
fold = scale**1.5 * math.exp(soften / reach)

f32 = jnp.float32
bf16 = jnp.bfloat16
NN = (((1,), (0,)), ((), ()))
NT = (((1,), (1,)), ((), ()))
TN = (((0,), (0,)), ((), ()))
FEATURES = 32
EDGES = 8


def split(value, pieces):
    parts = []
    for _ in range(pieces):
        head = value.astype(bf16).astype(f32)
        parts.append(head)
        value = value - head
    return parts


def pack_kernel(n_dom, me_ref, count_ref, pos_ref, vel_ref, mass_ref, owner_ref, *refs):
    outs, (hot_ref, rank_ref, total_ref) = refs[:-3], refs[-3:]
    rows = pos_ref.shape[1]
    targets, lanes = n_dom * CELLS, LANES // n_dom
    chunk = 256
    before = (
        lax.broadcasted_iota(jnp.int32, (chunk, chunk + LANES), 0)
        < lax.broadcasted_iota(jnp.int32, (chunk, chunk + LANES), 1)
    ).astype(f32).astype(bf16)
    carry = jnp.zeros((targets, LANES), f32)
    number = lax.broadcasted_iota(jnp.int32, (targets, chunk), 0)
    for at in range(0, rows, chunk):
        target = owner_ref[:, at : at + chunk] - me_ref[0] * CELLS
        target = jnp.where(target < 0, target + targets, target)
        place = lax.broadcasted_iota(jnp.int32, (1, chunk), 1) + at
        target = jnp.where(place < count_ref[0], target, -1)
        same = number == target
        hot = jnp.where(same, 1.0, 0.0).astype(bf16)
        hot_ref[:, at : at + chunk] = hot
        seen = lax.dot_general(hot, before, NN, preferred_element_type=f32)
        wide = jnp.concatenate([carry] * (chunk // LANES), axis=1)
        rank = jnp.sum(jnp.where(same, seen[:, :chunk] + wide, 0.0), axis=0, keepdims=True)
        rank_ref[:, at : at + chunk] = rank.astype(jnp.int32)
        carry = carry + seen[:, chunk:]
    step = 1024
    row = lax.broadcasted_iota(jnp.int32, (lanes, step), 0)
    for at in range(0, rows, step):
        span = slice(at, at + step)
        mark = jnp.where(row == rank_ref[:, span], 1.0, 0.0)
        values = [pos_ref[i : i + 1, span] + drift_step * vel_ref[i : i + 1, span] for i in range(3)]
        values += [mass_ref[:, span]]
        values += [vel_ref[i : i + 1, span] for i in range(3)]
        pieces = [split(value, 3) for value in values]
        hot = hot_ref[:, span]
        left = [
            jnp.concatenate([(mark * piece[k]).astype(bf16) for piece in pieces], axis=0)
            for k in range(3)
        ]
        part = lax.dot_general(
            jnp.concatenate(left, axis=1),
            jnp.concatenate([hot] * 3, axis=1),
            NT,
            preferred_element_type=f32,
        )
        size = 7 * lanes
        if at == 0:
            total_ref[:size] = part
            total_ref[size:] = jnp.zeros((lanes, targets), f32)
        else:
            total_ref[:size] += part
    groups = 8 * lanes // LANES
    packed = [
        jnp.concatenate(
            [
                total_ref[g * LANES : (g + 1) * LANES, t : t + LANES].T
                for t in range(0, targets, LANES)
            ],
            axis=0,
        )
        for g in range(groups)
    ]
    for by in range(n_dom):
        low, high = by * CELLS, (by + 1) * CELLS
        edge_high, edge_low = high % targets, (low - 1) % targets
        for g in range(groups):
            edges = jnp.concatenate(
                [
                    packed[g][edge_high : edge_high + 1],
                    packed[g][edge_low : edge_low + 1],
                    jnp.zeros((EDGES - 2, LANES), f32),
                ],
                axis=0,
            )
            both = jnp.concatenate([packed[g][low:high], edges], axis=0)
            outs[by][g] = both


def merged(pieces, comp, n_dom):
    lanes = LANES // n_dom
    group, inside = comp // n_dom, comp % n_dom
    plane = None
    for k, piece in enumerate(pieces):
        value = piece[group]
        shift = ((k - inside) % n_dom) * lanes
        if shift:
            value = pltpu.roll(value, shift, 1)
        if plane is None:
            plane = value
        else:
            lane = lax.broadcasted_iota(jnp.int32, value.shape, 1)
            plane = jnp.where(lane // lanes == k, value, plane)
    return plane


def put_rows(ref, k, plane, stride, cells, edges):
    low, high = cells
    for c in range(low - edges, high + edges):
        if c >= 0 and c % 8 == 0 and c + 8 <= min(high + edges, CELLS):
            at = (c - low + edges) * stride + k
            ref[pl.ds(at, 8, stride=stride), :] = plane[c : c + 8]
        elif c < 0 or c >= CELLS or c < -(-max(low - edges, 0) // 8) * 8 or c >= min(high + edges, CELLS) // 8 * 8:
            row = CELLS + 1 if c < 0 else c
            at = (c - low + edges) * stride + k
            ref[pl.ds(at, 1), :] = plane[row : row + 1]


def build(shells_ref, cells, far, summed, near=None):
    root = math.sqrt(scale)
    x = [shells_ref[comp] * root for comp in range(3)]
    norm = x[0] * x[0] + x[1] * x[1] + x[2] * x[2]
    one, none = jnp.ones_like(norm), jnp.zeros_like(norm)
    far_feat, near_feat = [], []
    for h, m, l in [split(value, 3) for value in x]:
        far_feat += [h, m, h, l, h, m]
        near_feat += [-2.0 * v for v in (h, h, m, h, l, m)]
    far_feat += [one] * 3 + split(norm, 3)
    near_feat += split(norm + scale * soften, 3) + [one] * 3
    for k in range(FEATURES):
        put_rows(far, k, far_feat[k] if k < len(far_feat) else none, FEATURES, cells, 1)
        if near is not None:
            put_rows(near, k, near_feat[k] if k < len(near_feat) else none, FEATURES, cells, 0)
    mass = shells_ref[3] * (coupling * fold / root)
    terms = [part for value in x + [None] for part in split(mass if value is None else mass * value, 3)]
    for k in range(16):
        put_rows(summed, k, terms[k] if k < 12 else none, 16, cells, 1)


def cast_rows(pairs):
    for source, target in pairs:
        tall = target.shape[1]
        for e in range(target.shape[0]):
            target[e] = source[e * tall : (e + 1) * tall].astype(bf16)


def pair_loop(count, per, far_rows, sum_rows, centre, out, dist, heavy, light):
    blocks = [(k, n) for k in range(3) for n in range(len(far_rows))]
    tall = LANES * len(blocks)
    wide = 3

    def distances(step, b):
        for u in range(per):
            c = step * per + u
            for at in range(0, len(blocks), wide):
                others = jnp.concatenate(
                    [far_rows[n][c + k] for k, n in blocks[at : at + wide]], axis=1
                )
                low = u * tall + at * LANES
                dist[b][low : low + wide * LANES] = lax.dot_general(
                    others, centre(c), TN, preferred_element_type=f32
                )

    def weights(b):
        for at in range(0, per * tall, 64):
            s = dist[b][at : at + 64]
            inverse = lax.rsqrt(s)
            w = jnp.exp2(-s) * (inverse * inverse * inverse)
            head = w.astype(bf16)
            heavy[b][at : at + 64] = head
            light[b][at : at + 64] = (w - head.astype(f32)).astype(bf16)

    def sums(step, b):
        for u in range(per):
            c = step * per + u
            terms = jnp.concatenate([sum_rows[n][c + k] for k, n in blocks], axis=1)
            span = slice(u * tall, (u + 1) * tall)
            total = lax.dot_general(terms, heavy[b][span], NN, preferred_element_type=f32)
            total += lax.dot_general(terms, light[b][span], NN, preferred_element_type=f32)
            out[c] = total

    steps = count // per
    distances(0, 0)
    distances(1, 1)
    weights(0)

    def body(i, _):
        for b in range(2):
            step = 2 * i + b
            sums(step, b)
            distances(jnp.minimum(step + 2, steps - 1), b)
            weights(1 - b)
        return 0

    lax.fori_loop(0, steps // 2, body, 0)


def join_kernel(n_dom, me_ref, *refs):
    pieces, (shells_ref, planes_ref) = refs[:n_dom], refs[n_dom:]
    turn = me_ref[0] * (LANES // n_dom)
    for comp in range(7):
        plane = pltpu.roll(merged(pieces, comp, n_dom), turn, 1)
        if comp < 4:
            shells_ref[comp] = plane
        planes_ref[comp] = plane[:CELLS]


def own_kernel(shells_ref, near_out, out_ref, far, near, summed, far_rows, sum_rows, *work):
    cells = (0, CELLS)
    build(shells_ref, cells, far, summed, near)
    cast_rows([(far, far_rows), (near, near_out), (summed, sum_rows)])
    centre = lambda c: near_out[c]
    pair_loop(
        CELLS, 2, [far_rows], [sum_rows], centre, out_ref, work[0:2], work[2:4], work[4:6]
    )


def side_kernel(cells, up_ref, down_ref, near_ref, own_out, planes_ref, accel_ref, *refs):
    low, high = cells
    fars, sums, far_rows, sum_rows = refs[0:2], refs[2:4], refs[4:6], refs[6:8]
    out, work = refs[8], refs[9:]
    for side, shells_ref in enumerate((up_ref, down_ref)):
        build(shells_ref, cells, fars[side], sums[side])
    cast_rows([(fars[0], far_rows[0]), (fars[1], far_rows[1]), (sums[0], sum_rows[0]), (sums[1], sum_rows[1])])
    centre = lambda c: near_ref[c + low]
    pair_loop(
        high - low, 1, far_rows, sum_rows, centre, out, work[0:2], work[2:4], work[4:6]
    )
    flat = out.reshape((high - low) * 16, LANES)
    flat_own = own_out.reshape(CELLS * 16, LANES)
    rows = [
        flat[pl.ds(k, high - low, stride=16), :]
        + flat_own[pl.ds(low * 16 + k, high - low, stride=16), :]
        for k in range(12)
    ]
    total = [rows[3 * comp] + rows[3 * comp + 1] + rows[3 * comp + 2] for comp in range(4)]
    live = planes_ref[3, low:high] > 0
    for comp in range(3):
        centre_at = planes_ref[comp, low:high] * math.sqrt(scale)
        accel_ref[comp] = jnp.where(live, total[comp] - centre_at * total[3], 0.0)


def kick_kernel(planes_ref, *refs):
    accels, out_ref = refs[:-1], refs[-1]
    for comp in range(4):
        out_ref[comp, 0] = planes_ref[comp]
    low = 0
    for accel_ref in accels:
        high = low + accel_ref.shape[1]
        for comp in range(3):
            accel = accel_ref[comp]
            out_ref[4 + comp, 0, low:high] = planes_ref[4 + comp, low:high] + kick_step * accel
            out_ref[7 + comp, 0, low:high] = accel
        low = high


def call(kernel, n_smem, n_vmem, out_shape, scratch=(), name=None, cost=None, n_block=0):
    smem = pl.BlockSpec(memory_space=pltpu.SMEM)
    vmem = pl.BlockSpec(memory_space=pltpu.VMEM)
    block = pl.BlockSpec()
    return pl.pallas_call(
        kernel,
        in_specs=[smem] * n_smem + [block] * n_block + [vmem] * n_vmem,
        out_specs=jax.tree.map(lambda _: vmem, out_shape),
        out_shape=out_shape,
        scratch_shapes=scratch,
        name=name,
        compiler_params=pltpu.CompilerParams(vmem_limit_bytes=48 << 20),
        cost_estimate=cost,
    )


def sent(value, n_slab, n_dom, by_slab, by_dom):
    pairs = [
        (s * n_dom + d, (s + by_slab) % n_slab * n_dom + (d + by_dom) % n_dom)
        for s in range(n_slab)
        for d in range(n_dom)
    ]
    return lax.ppermute(value, ("slab", "dom"), pairs)


def per_device(positions, velocities, masses, owner_cell, counts):
    n_slab, n_dom = lax.axis_size("slab"), lax.axis_size("dom")
    rows = positions.shape[1]
    lanes = LANES // n_dom
    targets = n_dom * CELLS
    groups = 8 * lanes // LANES
    tall = CELLS + EDGES
    me = lax.axis_index("dom").astype(jnp.int32).reshape(1)
    shape = lambda *dims, dtype=f32: jax.ShapeDtypeStruct(dims, dtype)

    whole = call(
        functools.partial(pack_kernel, n_dom),
        2,
        0,
        [shape(groups, tall, LANES)] * n_dom,
        [
            pltpu.VMEM((targets, rows), bf16),
            pltpu.VMEM((1, rows), jnp.int32),
            pltpu.VMEM((8 * lanes, targets), f32),
        ],
        name="pack",
        n_block=4,
    )(me, counts, positions, velocities, masses.reshape(1, rows), owner_cell.reshape(1, rows))

    own = [whole[0]] + [sent(whole[-k % n_dom], n_slab, n_dom, 0, -k) for k in range(1, n_dom)]
    shells, planes = call(
        functools.partial(join_kernel, n_dom),
        1,
        n_dom,
        [shape(4, tall, LANES), shape(7, CELLS, LANES)],
        name="join",
    )(me, *own)
    below, above = (sent(shells, n_slab, n_dom, side, 0) for side in (1, -1))
    early = sent(planes, n_slab, n_dom, n_slab // 2, 0)

    def pair_work(size):
        return [pltpu.VMEM((size, LANES), f32)] * 2 + [pltpu.VMEM((size, LANES), bf16)] * 4

    def row_work(count, copies):
        edged = count + 2
        return (
            [pltpu.VMEM((edged * FEATURES, LANES), f32)] * copies,
            [pltpu.VMEM((edged * 16, LANES), f32)] * copies,
            [pltpu.VMEM((edged, FEATURES, LANES), bf16)] * copies,
            [pltpu.VMEM((edged, 16, LANES), bf16)] * copies,
        )

    far, summed, far_rows, sum_rows = row_work(CELLS, 1)
    near, sums = call(
        own_kernel,
        0,
        1,
        [shape(CELLS, FEATURES, LANES, dtype=bf16), shape(CELLS, 16, LANES)],
        far + [pltpu.VMEM((CELLS * FEATURES, LANES), f32)] + summed + far_rows + sum_rows + pair_work(768),
        name="own_slab",
        cost=pl.CostEstimate(flops=8_000_000_000, bytes_accessed=1_000_000, transcendentals=0),
    )(shells)
    accels = []
    for cells in ((0, 40), (40, CELLS)):
        count = cells[1] - cells[0]
        far, summed, far_rows, sum_rows = row_work(count, 2)
        accels.append(
            call(
                functools.partial(side_kernel, cells),
                0,
                5,
                shape(3, count, LANES),
                far + summed + far_rows + sum_rows + [pltpu.VMEM((count, 16, LANES), f32)] + pair_work(768),
                name="side_slabs",
                cost=pl.CostEstimate(flops=8_000_000_000, bytes_accessed=1_000_000, transcendentals=0),
            )(below, above, near, sums, planes)
        )
    later = [sent(accel, n_slab, n_dom, n_slab // 2, 0) for accel in accels]
    out = shape(10, 1, CELLS, LANES)
    state = call(kick_kernel, 0, 3, out, name="state")(planes, *accels)
    buddy = call(kick_kernel, 0, 3, out, name="buddy")(early, *later)
    return state, buddy


def solution(mesh):
    placed = (
        P(None, ("slab", "dom")),
        P(None, ("slab", "dom")),
        P(("slab", "dom")),
        P(("slab", "dom"), None),
        P(("slab", "dom")),
    )
    return jax.shard_map(
        per_device,
        mesh=mesh,
        in_specs=placed,
        out_specs=(P(None, "slab", "dom", None), P(None, "slab", "dom", None)),
        check_vma=False,
    )
```

```python
import functools
import math

import jax
import jax.numpy as jnp
from jax import lax
from jax.experimental import pallas as pl
from jax.experimental.pallas import tpu as pltpu
from jax.sharding import PartitionSpec as P

CELLS = 64
LANES = 128

drift_step = 0.5
kick_step = 0.5
soften = 0.25
reach = 4.0
coupling = 0.25

scale = math.log2(math.e) / reach
fold = scale**1.5 * math.exp(soften / reach)

f32 = jnp.float32
bf16 = jnp.bfloat16
NN = (((1,), (0,)), ((), ()))
NT = (((1,), (1,)), ((), ()))
TN = (((0,), (0,)), ((), ()))
FEATURES = 32
EDGES = 8


def split(value, pieces):
    parts = []
    for _ in range(pieces):
        head = value.astype(bf16).astype(f32)
        parts.append(head)
        value = value - head
    return parts


def pack_kernel(n_dom, me_ref, count_ref, pos_any, vel_any, mass_any, owner_any, *refs):
    outs, refs = refs[:n_dom], refs[n_dom:]
    pos_ref, vel_ref, mass_ref, owner_ref, rank_ref, target_ref, total_ref, sems = refs
    copies = [
        pltpu.make_async_copy(source, target, sems.at[i])
        for i, (source, target) in enumerate(
            [(owner_any, owner_ref), (pos_any, pos_ref), (vel_any, vel_ref), (mass_any, mass_ref)]
        )
    ]
    for copy in copies:
        copy.start()
    rows = pos_ref.shape[1]
    targets, lanes = n_dom * CELLS, LANES // n_dom
    part = lanes // 2
    chunk = 256
    before = (
        lax.broadcasted_iota(jnp.int32, (chunk, chunk + LANES), 0)
        < lax.broadcasted_iota(jnp.int32, (chunk, chunk + LANES), 1)
    ).astype(f32).astype(bf16)
    carry = jnp.zeros((targets, LANES), f32)
    number = lax.broadcasted_iota(jnp.int32, (targets, chunk), 0)
    copies[0].wait()
    for at in range(0, rows, chunk):
        target = owner_ref[:, at : at + chunk] - me_ref[0] * CELLS
        target = jnp.where(target < 0, target + targets, target)
        place = lax.broadcasted_iota(jnp.int32, (1, chunk), 1) + at
        target = jnp.where(place < count_ref[0], target, -1)
        target_ref[:, at : at + chunk] = target
        same = number == target
        hot = jnp.where(same, 1.0, 0.0).astype(bf16)
        seen = lax.dot_general(hot, before, NN, preferred_element_type=f32)
        wide = jnp.concatenate([carry] * (chunk // LANES), axis=1)
        rank = jnp.sum(jnp.where(same, seen[:, :chunk] + wide, 0.0), axis=0, keepdims=True)
        rank_ref[:, at : at + chunk] = rank.astype(jnp.int32)
        carry = carry + seen[:, chunk:]
    for copy in copies[1:]:
        copy.wait()
    step = 1024
    row = lax.broadcasted_iota(jnp.int32, (part, step), 0)
    column = lax.broadcasted_iota(jnp.int32, (2 * targets, step), 0)
    for at in range(0, rows, step):
        span = slice(at, at + step)
        rank, target = rank_ref[:, span], target_ref[:, span]
        upper = rank >= part
        mark = jnp.where(row == jnp.where(upper, rank - part, rank), 1.0, 0.0)
        place = jnp.where(upper & (target >= 0), target + targets, target)
        hot = jnp.where(column == place, 1.0, 0.0).astype(bf16)
        values = [pos_ref[i : i + 1, span] + drift_step * vel_ref[i : i + 1, span] for i in range(3)]
        values += [mass_ref[:, span]]
        values += [vel_ref[i : i + 1, span] for i in range(3)]
        pieces = [split(value, 2) for value in values]
        left = [
            jnp.concatenate([(mark * piece[k]).astype(bf16) for piece in pieces], axis=0)
            for k in range(2)
        ]
        found = lax.dot_general(
            jnp.concatenate(left, axis=1),
            jnp.concatenate([hot] * 2, axis=1),
            NT,
            preferred_element_type=f32,
        )
        for comp in range(7):
            for half in range(2):
                low = comp * lanes + half * part
                value = found[comp * part : (comp + 1) * part, half * targets : (half + 1) * targets]
                if at == 0:
                    total_ref[low : low + part] = value
                else:
                    total_ref[low : low + part] += value
    total_ref[7 * lanes :] = jnp.zeros((lanes, targets), f32)
    groups = 8 * lanes // LANES
    packed = [
        jnp.concatenate(
            [
                total_ref[g * LANES : (g + 1) * LANES, t : t + LANES].T
                for t in range(0, targets, LANES)
            ],
            axis=0,
        )
        for g in range(groups)
    ]
    for by in range(n_dom):
        low, high = by * CELLS, (by + 1) * CELLS
        edge_high, edge_low = high % targets, (low - 1) % targets
        for g in range(groups):
            edges = jnp.concatenate(
                [
                    packed[g][edge_high : edge_high + 1],
                    packed[g][edge_low : edge_low + 1],
                    jnp.zeros((EDGES - 2, LANES), f32),
                ],
                axis=0,
            )
            outs[by][g] = jnp.concatenate([packed[g][low:high], edges], axis=0)


def merged(pieces, comp, n_dom):
    lanes = LANES // n_dom
    group, inside = comp // n_dom, comp % n_dom
    plane = None
    for k, piece in enumerate(pieces):
        value = piece[group]
        shift = ((k - inside) % n_dom) * lanes
        if shift:
            value = pltpu.roll(value, shift, 1)
        if plane is None:
            plane = value
        else:
            lane = lax.broadcasted_iota(jnp.int32, value.shape, 1)
            plane = jnp.where(lane // lanes == k, value, plane)
    return plane


def build(shells_ref, rows_ref, far_ref, sum_ref, near_ref=None):
    root = math.sqrt(scale)
    tall = shells_ref.shape[1]
    rows_ref[...] = jnp.zeros_like(rows_ref)
    for at in range(0, tall, 8):
        for comp in range(4):
            rows_ref[pl.ds(at * 8 + comp, 8, stride=8), :] = shells_ref[comp, at : at + 8, :]
    for at in range(0, tall, 8):
        value = rows_ref[at * 8 : (at + 8) * 8]
        row = lax.broadcasted_iota(jnp.int32, value.shape, 0) % 8

        def spread(array):
            total = jnp.sum(array.reshape(8, 8, LANES), axis=1, keepdims=True)
            return jnp.broadcast_to(total, (8, 8, LANES)).reshape(64, LANES)

        mass = spread(jnp.where(row == 3, value, 0.0)) * (coupling * fold / root)
        place = jnp.where(row < 3, value * root, 0.0)
        norm = spread(place * place)
        h, m, l = split(place, 3)
        down = lambda array, by: pltpu.roll(array, by, 0)

        def ends(array, first):
            parts = split(array, 3)
            ones = (row >= 3 - first) & (row < 6 - first)
            kept = jnp.where(ones, 1.0, 0.0)
            for i in range(3):
                kept = jnp.where(row == first + i, parts[i], kept)
            return kept

        def put(ref, groups):
            both = [
                jnp.concatenate(
                    [groups[i].reshape(8, 8, LANES), groups[i + 1].reshape(8, 8, LANES)], axis=1
                )
                for i in range(0, len(groups), 2)
            ]
            count = min(8, ref.shape[0] - at)
            if count > 0:
                value = jnp.concatenate(both, axis=1).astype(bf16)
                ref[at : at + count] = value[:count]

        h3, m3, l3 = down(h, 3), down(m, 3), down(l, 3)
        put(far_ref, [h + m3, h + l3, h + m3, ends(norm, 3)])
        if near_ref is not None:
            near = [-2.0 * (h + h3), -2.0 * (m + h3), -2.0 * (l + m3)]
            put(near_ref, near + [ends(norm + scale * soften, 0)])
        terms = split(mass * jnp.where(row == 3, 1.0, place), 3)
        put(sum_ref, [terms[0] + down(terms[1], 4), terms[2]])


def pair_loop(cells, per, far_rows, sum_rows, centre, out, dist, heavy, light):
    blocks = [(k, n) for k in range(3) for n in range(len(far_rows))]
    tall = LANES * len(blocks)
    wide = 3
    first, count = cells[0], cells[1] - cells[0]

    def beside(c, k):
        at = c + first + k - 1
        return jnp.where(at < 0, CELLS + 1, at) if k == 0 else at

    def distances(step, b):
        for u in range(per):
            c = step * per + u
            for at in range(0, len(blocks), wide):
                others = jnp.concatenate(
                    [far_rows[n][beside(c, k)] for k, n in blocks[at : at + wide]], axis=1
                )
                low = u * tall + at * LANES
                dist[b][low : low + wide * LANES] = lax.dot_general(
                    others, centre[c + first], TN, preferred_element_type=f32
                )

    def weights(b):
        for at in range(0, per * tall, 64):
            s = dist[b][at : at + 64]
            inverse = lax.rsqrt(s)
            w = jnp.exp2(-s) * (inverse * inverse * inverse)
            head = w.astype(bf16)
            heavy[b][at : at + 64] = head
            light[b][at : at + 64] = (w - head.astype(f32)).astype(bf16)

    def sums(step, b):
        for u in range(per):
            c = step * per + u
            terms = jnp.concatenate([sum_rows[n][beside(c, k)] for k, n in blocks], axis=1)
            span = slice(u * tall, (u + 1) * tall)
            total = lax.dot_general(terms, heavy[b][span], NN, preferred_element_type=f32)
            total += lax.dot_general(terms, light[b][span], NN, preferred_element_type=f32)
            out[c] = total

    steps = count // per
    distances(0, 0)
    distances(1, 1)
    weights(0)

    def body(i, _):
        for b in range(2):
            step = 2 * i + b
            sums(step, b)
            distances(jnp.minimum(step + 2, steps - 1), b)
            weights(1 - b)
        return 0

    lax.fori_loop(0, steps // 2, body, 0)


def join_kernel(n_dom, me_ref, *refs):
    pieces, (shells_ref, planes_ref) = refs[:n_dom], refs[n_dom:]
    turn = me_ref[0] * (LANES // n_dom)
    for comp in range(7):
        plane = pltpu.roll(merged(pieces, comp, n_dom), turn, 1)
        if comp < 4:
            shells_ref[comp] = plane
        planes_ref[comp] = plane[:CELLS]


def own_kernel(shells_ref, near_out, out_ref, rows, far_rows, sum_rows, *work):
    build(shells_ref, rows, far_rows, sum_rows, near_out)
    pair_loop(
        (0, CELLS), 2, [far_rows], [sum_rows], near_out, out_ref, work[0:2], work[2:4], work[4:6]
    )


def side_kernel(cells, up_ref, down_ref, near_ref, own_out, planes_ref, accel_ref, *refs):
    low, high = cells
    count = high - low
    rows, far_rows, sum_rows, out, work = refs[0], refs[1:3], refs[3:5], refs[5], refs[6:]
    for side, shells_ref in enumerate((up_ref, down_ref)):
        build(shells_ref, rows, far_rows[side], sum_rows[side])
    pair_loop(cells, 1, far_rows, sum_rows, near_ref, out, work[0:2], work[2:4], work[4:6])
    both = out[...] + own_out[low:high]
    both = (both[:, :8] + both[:, 8:]).reshape(count * 8, LANES)
    rows[: count * 8] = both + pltpu.roll(both, count * 8 - 4, 0)
    total = [rows[pl.ds(comp, count, stride=8), :] for comp in range(4)]
    live = planes_ref[3, low:high] > 0
    for comp in range(3):
        centre_at = planes_ref[comp, low:high] * math.sqrt(scale)
        accel_ref[comp] = jnp.where(live, total[comp] - centre_at * total[3], 0.0)


def kick_kernel(planes_ref, *refs):
    accels, out_ref = refs[:-1], refs[-1]
    for comp in range(4):
        out_ref[comp, 0] = planes_ref[comp]
    low = 0
    for accel_ref in accels:
        high = low + accel_ref.shape[1]
        for comp in range(3):
            accel = accel_ref[comp]
            out_ref[4 + comp, 0, low:high] = planes_ref[4 + comp, low:high] + kick_step * accel
            out_ref[7 + comp, 0, low:high] = accel
        low = high


def call(kernel, n_smem, n_vmem, out_shape, scratch=(), name=None, cost=None, n_any=0):
    smem = pl.BlockSpec(memory_space=pltpu.SMEM)
    vmem = pl.BlockSpec(memory_space=pltpu.VMEM)
    here = pl.BlockSpec(memory_space=pl.ANY)
    return pl.pallas_call(
        kernel,
        in_specs=[smem] * n_smem + [here] * n_any + [vmem] * n_vmem,
        out_specs=jax.tree.map(lambda _: vmem, out_shape),
        out_shape=out_shape,
        scratch_shapes=scratch,
        name=name,
        compiler_params=pltpu.CompilerParams(vmem_limit_bytes=48 << 20),
        cost_estimate=cost,
    )


def sent(value, n_slab, n_dom, by_slab, by_dom):
    pairs = [
        (s * n_dom + d, (s + by_slab) % n_slab * n_dom + (d + by_dom) % n_dom)
        for s in range(n_slab)
        for d in range(n_dom)
    ]
    return lax.ppermute(value, ("slab", "dom"), pairs)


def per_device(positions, velocities, masses, owner_cell, counts):
    n_slab, n_dom = lax.axis_size("slab"), lax.axis_size("dom")
    rows = positions.shape[1]
    lanes = LANES // n_dom
    targets = n_dom * CELLS
    groups = 8 * lanes // LANES
    tall = CELLS + EDGES
    me = lax.axis_index("dom").astype(jnp.int32).reshape(1)
    shape = lambda *dims, dtype=f32: jax.ShapeDtypeStruct(dims, dtype)

    whole = call(
        functools.partial(pack_kernel, n_dom),
        2,
        0,
        [shape(groups, tall, LANES)] * n_dom,
        [
            pltpu.VMEM((3, rows), f32),
            pltpu.VMEM((3, rows), f32),
            pltpu.VMEM((1, rows), f32),
            pltpu.VMEM((1, rows), jnp.int32),
            pltpu.VMEM((1, rows), jnp.int32),
            pltpu.VMEM((1, rows), jnp.int32),
            pltpu.VMEM((8 * lanes, targets), f32),
            pltpu.SemaphoreType.DMA((4,)),
        ],
        name="pack",
        n_any=4,
    )(me, counts, positions, velocities, masses.reshape(1, rows), owner_cell.reshape(1, rows))

    own = [whole[0]] + [sent(whole[-k % n_dom], n_slab, n_dom, 0, -k) for k in range(1, n_dom)]
    shells, planes = call(
        functools.partial(join_kernel, n_dom),
        1,
        n_dom,
        [shape(4, tall, LANES), shape(7, CELLS, LANES)],
        name="join",
    )(me, *own)
    below, above = (sent(shells, n_slab, n_dom, side, 0) for side in (1, -1))
    early = sent(planes, n_slab, n_dom, n_slab // 2, 0)

    def pair_work(size):
        return [pltpu.VMEM((size, LANES), f32)] * 2 + [pltpu.VMEM((size, LANES), bf16)] * 4

    def row_work(copies):
        return (
            [pltpu.VMEM((tall * 8, LANES), f32)]
            + [pltpu.VMEM((tall, FEATURES, LANES), bf16)] * copies
            + [pltpu.VMEM((tall, 16, LANES), bf16)] * copies
        )

    near, sums = call(
        own_kernel,
        0,
        1,
        [shape(CELLS, FEATURES, LANES, dtype=bf16), shape(CELLS, 16, LANES)],
        row_work(1) + pair_work(768),
        name="own_slab",
        cost=pl.CostEstimate(flops=8_000_000_000, bytes_accessed=1_000_000, transcendentals=0),
    )(shells)
    accels = []
    for cells in ((0, 40), (40, CELLS)):
        count = cells[1] - cells[0]
        accels.append(
            call(
                functools.partial(side_kernel, cells),
                0,
                5,
                shape(3, count, LANES),
                row_work(2) + [pltpu.VMEM((count, 16, LANES), f32)] + pair_work(768),
                name="side_slabs",
                cost=pl.CostEstimate(flops=8_000_000_000, bytes_accessed=1_000_000, transcendentals=0),
            )(below, above, near, sums, planes)
        )
    later = [sent(accel, n_slab, n_dom, n_slab // 2, 0) for accel in accels]
    out = shape(10, 1, CELLS, LANES)
    state = call(kick_kernel, 0, 3, out, name="state")(planes, *accels)
    buddy = call(kick_kernel, 0, 3, out, name="buddy")(early, *later)
    return state, buddy


def solution(mesh):
    placed = (
        P(None, ("slab", "dom")),
        P(None, ("slab", "dom")),
        P(("slab", "dom")),
        P(("slab", "dom"), None),
        P(("slab", "dom")),
    )
    return jax.shard_map(
        per_device,
        mesh=mesh,
        in_specs=placed,
        out_specs=(P(None, "slab", "dom", None), P(None, "slab", "dom", None)),
        check_vma=False,
    )
```

```python
import functools
import math

import jax
import jax.numpy as jnp
from jax import lax
from jax.experimental import pallas as pl
from jax.experimental.pallas import tpu as pltpu
from jax.sharding import PartitionSpec as P

CELLS = 64
LANES = 128

drift_step = 0.5
kick_step = 0.5
soften = 0.25
reach = 4.0
coupling = 0.25

scale = math.log2(math.e) / reach
fold = scale**1.5 * math.exp(soften / reach)

f32 = jnp.float32
bf16 = jnp.bfloat16
NN = (((1,), (0,)), ((), ()))
NT = (((1,), (1,)), ((), ()))
TN = (((0,), (0,)), ((), ()))
FEATURES = 32
EDGES = 8


def split(value, pieces):
    parts = []
    for _ in range(pieces):
        head = value.astype(bf16).astype(f32)
        parts.append(head)
        value = value - head
    return parts


def pack_kernel(n_dom, me_ref, count_ref, pos_any, vel_any, mass_any, owner_any, *refs):
    outs, refs = refs[: 2 * n_dom], refs[2 * n_dom :]
    pos_ref, vel_ref, mass_ref, owner_ref, rank_ref, target_ref, total_ref, sems = refs
    copies = [
        pltpu.make_async_copy(source, target, sems.at[i])
        for i, (source, target) in enumerate(
            [(owner_any, owner_ref), (pos_any, pos_ref), (vel_any, vel_ref), (mass_any, mass_ref)]
        )
    ]
    for copy in copies:
        copy.start()
    rows = pos_ref.shape[1]
    targets, lanes = n_dom * CELLS, LANES // n_dom
    part = lanes // 2
    chunk = 256
    before = (
        lax.broadcasted_iota(jnp.int32, (chunk, chunk + LANES), 0)
        < lax.broadcasted_iota(jnp.int32, (chunk, chunk + LANES), 1)
    ).astype(f32).astype(bf16)
    carry = jnp.zeros((targets, LANES), f32)
    number = lax.broadcasted_iota(jnp.int32, (targets, chunk), 0)
    copies[0].wait()
    for at in range(0, rows, chunk):
        target = owner_ref[:, at : at + chunk] - me_ref[0] * CELLS
        target = jnp.where(target < 0, target + targets, target)
        place = lax.broadcasted_iota(jnp.int32, (1, chunk), 1) + at
        target = jnp.where(place < count_ref[0], target, -1)
        target_ref[:, at : at + chunk] = target
        same = number == target
        hot = jnp.where(same, 1.0, 0.0).astype(bf16)
        seen = lax.dot_general(hot, before, NN, preferred_element_type=f32)
        wide = jnp.concatenate([carry] * (chunk // LANES), axis=1)
        rank = jnp.sum(jnp.where(same, seen[:, :chunk] + wide, 0.0), axis=0, keepdims=True)
        rank_ref[:, at : at + chunk] = rank.astype(jnp.int32)
        carry = carry + seen[:, chunk:]
    for copy in copies[1:]:
        copy.wait()
    step = 1024
    row = lax.broadcasted_iota(jnp.int32, (part, step), 0)
    column = lax.broadcasted_iota(jnp.int32, (2 * targets, step), 0)
    for at in range(0, rows, step):
        span = slice(at, at + step)
        rank, target = rank_ref[:, span], target_ref[:, span]
        upper = rank >= part
        mark = jnp.where(row == jnp.where(upper, rank - part, rank), 1.0, 0.0)
        place = jnp.where(upper & (target >= 0), target + targets, target)
        hot = jnp.where(column == place, 1.0, 0.0).astype(bf16)
        values = [pos_ref[i : i + 1, span] + drift_step * vel_ref[i : i + 1, span] for i in range(3)]
        values += [mass_ref[:, span]]
        values += [vel_ref[i : i + 1, span] for i in range(3)]
        pieces = [split(value, 2) for value in values]
        left = [
            jnp.concatenate([(mark * piece[k]).astype(bf16) for piece in pieces], axis=0)
            for k in range(2)
        ]
        found = lax.dot_general(
            jnp.concatenate(left, axis=1),
            jnp.concatenate([hot] * 2, axis=1),
            NT,
            preferred_element_type=f32,
        )
        for comp in range(7):
            for half in range(2):
                low = comp * lanes + half * part
                value = found[comp * part : (comp + 1) * part, half * targets : (half + 1) * targets]
                if at == 0:
                    total_ref[low : low + part] = value
                else:
                    total_ref[low : low + part] += value
    total_ref[7 * lanes :] = jnp.zeros((lanes, targets), f32)
    groups = 8 * lanes // LANES
    packed = [
        jnp.concatenate(
            [
                total_ref[g * LANES : (g + 1) * LANES, t : t + LANES].T
                for t in range(0, targets, LANES)
            ],
            axis=0,
        )
        for g in range(groups)
    ]
    for by in range(n_dom):
        low, high = by * CELLS, (by + 1) * CELLS
        edge_high, edge_low = high % targets, (low - 1) % targets
        for g in range(groups // 2):
            edges = jnp.concatenate(
                [
                    packed[g][edge_high : edge_high + 1],
                    packed[g][edge_low : edge_low + 1],
                    jnp.zeros((EDGES - 2, LANES), f32),
                ],
                axis=0,
            )
            outs[by][g] = jnp.concatenate([packed[g][low:high], edges], axis=0)
            outs[n_dom + by][g] = packed[groups // 2 + g][low:high]


def merged(pieces, comp, n_dom):
    lanes = LANES // n_dom
    group, inside = comp // n_dom, comp % n_dom
    plane = None
    for k, piece in enumerate(pieces):
        value = piece[group]
        shift = ((k - inside) % n_dom) * lanes
        if shift:
            value = pltpu.roll(value, shift, 1)
        if plane is None:
            plane = value
        else:
            lane = lax.broadcasted_iota(jnp.int32, value.shape, 1)
            plane = jnp.where(lane // lanes == k, value, plane)
    return plane


def build(shells_ref, rows_ref, far_ref, sum_ref, near_ref=None):
    root = math.sqrt(scale)
    tall = shells_ref.shape[1]
    rows_ref[...] = jnp.zeros_like(rows_ref)
    for at in range(0, tall, 8):
        for comp in range(4):
            rows_ref[pl.ds(at * 8 + comp, 8, stride=8), :] = shells_ref[comp, at : at + 8, :]
    for at in range(0, tall, 8):
        value = rows_ref[at * 8 : (at + 8) * 8]
        row = lax.broadcasted_iota(jnp.int32, value.shape, 0) % 8

        def spread(array):
            total = jnp.sum(array.reshape(8, 8, LANES), axis=1, keepdims=True)
            return jnp.broadcast_to(total, (8, 8, LANES)).reshape(64, LANES)

        mass = spread(jnp.where(row == 3, value, 0.0)) * (coupling * fold / root)
        place = jnp.where(row < 3, value * root, 0.0)
        norm = spread(place * place)
        h, m, l = split(place, 3)
        down = lambda array, by: pltpu.roll(array, by, 0)

        def ends(array, first):
            parts = split(array, 3)
            ones = (row >= 3 - first) & (row < 6 - first)
            kept = jnp.where(ones, 1.0, 0.0)
            for i in range(3):
                kept = jnp.where(row == first + i, parts[i], kept)
            return kept

        def put(ref, groups):
            both = [
                jnp.concatenate(
                    [groups[i].reshape(8, 8, LANES), groups[i + 1].reshape(8, 8, LANES)], axis=1
                )
                for i in range(0, len(groups), 2)
            ]
            count = min(8, ref.shape[0] - at)
            if count > 0:
                value = jnp.concatenate(both, axis=1).astype(bf16)
                ref[at : at + count] = value[:count]

        h3, m3, l3 = down(h, 3), down(m, 3), down(l, 3)
        put(far_ref, [h + m3, h + l3, h + m3, ends(norm, 3)])
        if near_ref is not None:
            near = [-2.0 * (h + h3), -2.0 * (m + h3), -2.0 * (l + m3)]
            put(near_ref, near + [ends(norm + scale * soften, 0)])
        terms = split(mass * jnp.where(row == 3, 1.0, place), 3)
        put(sum_ref, [terms[0] + down(terms[1], 4), terms[2]])


def pair_loop(cells, per, far_rows, sum_rows, centre, out, dist, heavy, light):
    blocks = [(k, n) for k in range(3) for n in range(len(far_rows))]
    tall = LANES * len(blocks)
    wide = 3
    first, count = cells[0], cells[1] - cells[0]

    def beside(c, k):
        at = c + first + k - 1
        return jnp.where(at < 0, CELLS + 1, at) if k == 0 else at

    def distances(step, b):
        for u in range(per):
            c = step * per + u
            for at in range(0, len(blocks), wide):
                others = jnp.concatenate(
                    [far_rows[n][beside(c, k)] for k, n in blocks[at : at + wide]], axis=1
                )
                low = u * tall + at * LANES
                dist[b][low : low + wide * LANES] = lax.dot_general(
                    others, centre[c + first], TN, preferred_element_type=f32
                )

    def weights(b):
        for at in range(0, per * tall, 64):
            s = dist[b][at : at + 64]
            inverse = lax.rsqrt(s)
            w = jnp.exp2(-s) * (inverse * inverse * inverse)
            head = w.astype(bf16)
            heavy[b][at : at + 64] = head
            light[b][at : at + 64] = (w - head.astype(f32)).astype(bf16)

    def sums(step, b):
        for u in range(per):
            c = step * per + u
            terms = jnp.concatenate([sum_rows[n][beside(c, k)] for k, n in blocks], axis=1)
            span = slice(u * tall, (u + 1) * tall)
            total = lax.dot_general(terms, heavy[b][span], NN, preferred_element_type=f32)
            total += lax.dot_general(terms, light[b][span], NN, preferred_element_type=f32)
            out[c] = total

    steps = count // per
    distances(0, 0)
    distances(1, 1)
    weights(0)

    def body(i, _):
        for b in range(2):
            step = 2 * i + b
            sums(step, b)
            distances(jnp.minimum(step + 2, steps - 1), b)
            weights(1 - b)
        return 0

    lax.fori_loop(0, steps // 2, body, 0)


def join_kernel(n_dom, me_ref, *refs):
    pieces, shells_ref = refs[:n_dom], refs[n_dom]
    turn = me_ref[0] * (LANES // n_dom)
    for comp in range(4):
        shells_ref[comp] = pltpu.roll(merged(pieces, comp, n_dom), turn, 1)


def speeds_kernel(n_dom, me_ref, shells_ref, *refs):
    pieces, planes_ref = refs[:n_dom], refs[n_dom]
    turn = me_ref[0] * (LANES // n_dom)
    planes_ref[:4] = shells_ref[:, :CELLS]
    for comp in range(3):
        planes_ref[4 + comp] = pltpu.roll(merged(pieces, comp, n_dom), turn, 1)


def own_kernel(shells_ref, near_out, out_ref, rows, far_rows, sum_rows, *work):
    build(shells_ref, rows, far_rows, sum_rows, near_out)
    pair_loop(
        (0, CELLS), 2, [far_rows], [sum_rows], near_out, out_ref, work[0:2], work[2:4], work[4:6]
    )


def side_kernel(cells, up_ref, down_ref, near_ref, own_out, shells_ref, accel_ref, *refs):
    low, high = cells
    count = high - low
    rows, far_rows, sum_rows, out, work = refs[0], refs[1:3], refs[3:5], refs[5], refs[6:]
    for side, there_ref in enumerate((up_ref, down_ref)):
        build(there_ref, rows, far_rows[side], sum_rows[side])
    pair_loop(cells, 1, far_rows, sum_rows, near_ref, out, work[0:2], work[2:4], work[4:6])
    both = out[...] + own_out[low:high]
    both = (both[:, :8] + both[:, 8:]).reshape(count * 8, LANES)
    rows[: count * 8] = both + pltpu.roll(both, count * 8 - 4, 0)
    total = [rows[pl.ds(comp, count, stride=8), :] for comp in range(4)]
    live = shells_ref[3, low:high] > 0
    for comp in range(3):
        centre_at = shells_ref[comp, low:high] * math.sqrt(scale)
        accel_ref[comp] = jnp.where(live, total[comp] - centre_at * total[3], 0.0)


def kick_kernel(planes_ref, *refs):
    accels, out_ref = refs[:-1], refs[-1]
    for comp in range(4):
        out_ref[comp, 0] = planes_ref[comp]
    low = 0
    for accel_ref in accels:
        high = low + accel_ref.shape[1]
        for comp in range(3):
            accel = accel_ref[comp]
            out_ref[4 + comp, 0, low:high] = planes_ref[4 + comp, low:high] + kick_step * accel
            out_ref[7 + comp, 0, low:high] = accel
        low = high


def last_kick_kernel(low, _, planes_ref, accel_ref, out_ref, kicked, sem):
    high = low + accel_ref.shape[1]
    for comp in range(3):
        accel = accel_ref[comp]
        kicked[comp, 0] = planes_ref[4 + comp, low:high] + kick_step * accel
        kicked[3 + comp, 0] = accel
    copy = pltpu.make_async_copy(kicked, out_ref.at[4:10, :, low:high], sem)
    copy.start()
    copy.wait()


def call(
    kernel, n_smem, n_vmem, out_shape, scratch=(), name=None, cost=None, n_any=0, n_same=0, vmem_mib=48
):
    smem = pl.BlockSpec(memory_space=pltpu.SMEM)
    vmem = pl.BlockSpec(memory_space=pltpu.VMEM)
    here = pl.BlockSpec(memory_space=pltpu.HBM)
    return pl.pallas_call(
        kernel,
        in_specs=[smem] * n_smem + [here] * n_any + [vmem] * n_vmem,
        out_specs=jax.tree.map(lambda _: here if n_same else vmem, out_shape),
        out_shape=out_shape,
        scratch_shapes=scratch,
        name=name,
        compiler_params=pltpu.CompilerParams(vmem_limit_bytes=vmem_mib << 20),
        cost_estimate=cost,
        input_output_aliases={i: i for i in range(n_same)},
    )


def sent(value, n_slab, n_dom, by_slab, by_dom):
    pairs = [
        (s * n_dom + d, (s + by_slab) % n_slab * n_dom + (d + by_dom) % n_dom)
        for s in range(n_slab)
        for d in range(n_dom)
    ]
    return lax.ppermute(value, ("slab", "dom"), pairs)


def per_device(positions, velocities, masses, owner_cell, counts):
    n_slab, n_dom = lax.axis_size("slab"), lax.axis_size("dom")
    rows = positions.shape[1]
    lanes = LANES // n_dom
    targets = n_dom * CELLS
    half = 4 * lanes // LANES
    tall = CELLS + EDGES
    me = lax.axis_index("dom").astype(jnp.int32).reshape(1)
    shape = lambda *dims, dtype=f32: jax.ShapeDtypeStruct(dims, dtype)

    whole = call(
        functools.partial(pack_kernel, n_dom),
        2,
        0,
        [shape(half, tall, LANES)] * n_dom + [shape(half, CELLS, LANES)] * n_dom,
        [
            pltpu.VMEM((3, rows), f32),
            pltpu.VMEM((3, rows), f32),
            pltpu.VMEM((1, rows), f32),
            pltpu.VMEM((1, rows), jnp.int32),
            pltpu.VMEM((1, rows), jnp.int32),
            pltpu.VMEM((1, rows), jnp.int32),
            pltpu.VMEM((8 * lanes, targets), f32),
            pltpu.SemaphoreType.DMA((4,)),
        ],
        name="pack",
        n_any=4,
        vmem_mib=63,
    )(me, counts, positions, velocities, masses.reshape(1, rows), owner_cell.reshape(1, rows))

    def swapped(parts):
        return [parts[0]] + [
            sent(parts[-k % n_dom], n_slab, n_dom, 0, -k) for k in range(1, n_dom)
        ]

    places, speeds = swapped(whole[:n_dom]), swapped(whole[n_dom:])
    shells = call(
        functools.partial(join_kernel, n_dom), 1, n_dom, shape(4, tall, LANES), name="join"
    )(me, *places)
    planes = call(
        functools.partial(speeds_kernel, n_dom),
        1,
        1 + n_dom,
        shape(7, CELLS, LANES),
        name="speeds",
    )(me, shells, *speeds)
    below, above = (sent(shells, n_slab, n_dom, side, 0) for side in (1, -1))
    early = sent(planes, n_slab, n_dom, n_slab // 2, 0)

    def pair_work(size):
        return [pltpu.VMEM((size, LANES), f32)] * 2 + [pltpu.VMEM((size, LANES), bf16)] * 4

    def row_work(copies):
        return (
            [pltpu.VMEM((tall * 8, LANES), f32)]
            + [pltpu.VMEM((tall, FEATURES, LANES), bf16)] * copies
            + [pltpu.VMEM((tall, 16, LANES), bf16)] * copies
        )

    near, sums = call(
        own_kernel,
        0,
        1,
        [shape(CELLS, FEATURES, LANES, dtype=bf16), shape(CELLS, 16, LANES)],
        row_work(1) + pair_work(768),
        name="own_slab",
        cost=pl.CostEstimate(flops=8_000_000_000, bytes_accessed=1_000_000, transcendentals=0),
    )(shells)
    accels = []
    cut = CELLS * 3 // 4
    for cells in ((0, cut), (cut, CELLS)):
        count = cells[1] - cells[0]
        accels.append(
            call(
                functools.partial(side_kernel, cells),
                0,
                5,
                shape(3, count, LANES),
                row_work(2) + [pltpu.VMEM((count, 16, LANES), f32)] + pair_work(768),
                name="side_slabs",
                cost=pl.CostEstimate(flops=8_000_000_000, bytes_accessed=1_000_000, transcendentals=0),
            )(below, above, near, sums, shells)
        )
    later = [sent(accel, n_slab, n_dom, n_slab // 2, 0) for accel in accels]
    out = shape(10, 1, CELLS, LANES)
    state = call(kick_kernel, 0, 3, out, name="state")(planes, *accels)
    part = call(kick_kernel, 0, 2, out, name="buddy")(early, later[0])
    buddy = call(
        functools.partial(last_kick_kernel, cut),
        0,
        2,
        out,
        [pltpu.VMEM((6, 1, CELLS - cut, LANES), f32), pltpu.SemaphoreType.DMA],
        name="buddy_end",
        n_any=1,
        n_same=1,
    )(part, early, later[1])
    return state, buddy


def solution(mesh):
    placed = (
        P(None, ("slab", "dom")),
        P(None, ("slab", "dom")),
        P(("slab", "dom")),
        P(("slab", "dom"), None),
        P(("slab", "dom")),
    )
    return jax.shard_map(
        per_device,
        mesh=mesh,
        in_specs=placed,
        out_specs=(P(None, "slab", "dom", None), P(None, "slab", "dom", None)),
        check_vma=False,
    )
```

```python
import functools
import math

import jax
import jax.numpy as jnp
from jax import lax
from jax.experimental import pallas as pl
from jax.experimental.pallas import tpu as pltpu
from jax.sharding import PartitionSpec as P

CELLS = 64
LANES = 128

drift_step = 0.5
kick_step = 0.5
soften = 0.25
reach = 4.0
coupling = 0.25

scale = math.log2(math.e) / reach
fold = scale**1.5 * math.exp(soften / reach)

f32 = jnp.float32
bf16 = jnp.bfloat16
NN = (((1,), (0,)), ((), ()))
NT = (((1,), (1,)), ((), ()))
TN = (((0,), (0,)), ((), ()))
FEATURES = 32
EDGES = 8


def split(value, pieces):
    parts = []
    for _ in range(pieces):
        head = value.astype(bf16).astype(f32)
        parts.append(head)
        value = value - head
    return parts


def pack_kernel(n_dom, me_ref, count_ref, pos_any, vel_any, mass_any, owner_any, *refs):
    outs, refs = refs[: 2 * n_dom], refs[2 * n_dom :]
    pos_ref, vel_ref, mass_ref, owner_ref, rank_ref, target_ref, total_ref, sems = refs
    copies = [
        pltpu.make_async_copy(source, target, sems.at[i])
        for i, (source, target) in enumerate(
            [(owner_any, owner_ref), (pos_any, pos_ref), (vel_any, vel_ref), (mass_any, mass_ref)]
        )
    ]
    for copy in copies:
        copy.start()
    rows = pos_ref.shape[1]
    targets, lanes = n_dom * CELLS, LANES // n_dom
    part = lanes // 2
    chunk = 256
    before = (
        lax.broadcasted_iota(jnp.int32, (chunk, chunk + LANES), 0)
        < lax.broadcasted_iota(jnp.int32, (chunk, chunk + LANES), 1)
    ).astype(f32).astype(bf16)
    carry = jnp.zeros((targets, LANES), f32)
    number = lax.broadcasted_iota(jnp.int32, (targets, chunk), 0)
    copies[0].wait()
    for at in range(0, rows, chunk):
        target = owner_ref[:, at : at + chunk] - me_ref[0] * CELLS
        target = jnp.where(target < 0, target + targets, target)
        place = lax.broadcasted_iota(jnp.int32, (1, chunk), 1) + at
        target = jnp.where(place < count_ref[0], target, -1)
        target_ref[:, at : at + chunk] = target
        same = number == target
        hot = jnp.where(same, 1.0, 0.0).astype(bf16)
        seen = lax.dot_general(hot, before, NN, preferred_element_type=f32)
        wide = jnp.concatenate([carry] * (chunk // LANES), axis=1)
        rank = jnp.sum(jnp.where(same, seen[:, :chunk] + wide, 0.0), axis=0, keepdims=True)
        rank_ref[:, at : at + chunk] = rank.astype(jnp.int32)
        carry = carry + seen[:, chunk:]
    for copy in copies[1:]:
        copy.wait()
    step = 1024
    row = lax.broadcasted_iota(jnp.int32, (part, step), 0)
    column = lax.broadcasted_iota(jnp.int32, (2 * targets, step), 0)
    for at in range(0, rows, step):
        span = slice(at, at + step)
        rank, target = rank_ref[:, span], target_ref[:, span]
        upper = rank >= part
        mark = jnp.where(row == jnp.where(upper, rank - part, rank), 1.0, 0.0)
        place = jnp.where(upper & (target >= 0), target + targets, target)
        hot = jnp.where(column == place, 1.0, 0.0).astype(bf16)
        values = [pos_ref[i : i + 1, span] + drift_step * vel_ref[i : i + 1, span] for i in range(3)]
        values += [mass_ref[:, span]]
        values += [vel_ref[i : i + 1, span] for i in range(3)]
        pieces = [split(value, 2) for value in values]
        left = [
            jnp.concatenate([(mark * piece[k]).astype(bf16) for piece in pieces], axis=0)
            for k in range(2)
        ]
        found = lax.dot_general(
            jnp.concatenate(left, axis=1),
            jnp.concatenate([hot] * 2, axis=1),
            NT,
            preferred_element_type=f32,
        )
        for comp in range(7):
            for half in range(2):
                low = comp * lanes + half * part
                value = found[comp * part : (comp + 1) * part, half * targets : (half + 1) * targets]
                if at == 0:
                    total_ref[low : low + part] = value
                else:
                    total_ref[low : low + part] += value
    total_ref[7 * lanes :] = jnp.zeros((lanes, targets), f32)
    groups = 8 * lanes // LANES
    packed = [
        jnp.concatenate(
            [
                total_ref[g * LANES : (g + 1) * LANES, t : t + LANES].T
                for t in range(0, targets, LANES)
            ],
            axis=0,
        )
        for g in range(groups)
    ]
    for by in range(n_dom):
        low, high = by * CELLS, (by + 1) * CELLS
        edge_high, edge_low = high % targets, (low - 1) % targets
        for g in range(groups // 2):
            edges = jnp.concatenate(
                [
                    packed[g][edge_high : edge_high + 1],
                    packed[g][edge_low : edge_low + 1],
                    jnp.zeros((EDGES - 2, LANES), f32),
                ],
                axis=0,
            )
            outs[by][g] = jnp.concatenate([packed[g][low:high], edges], axis=0)
            outs[n_dom + by][g] = packed[groups // 2 + g][low:high]


def merged(pieces, comp, n_dom):
    lanes = LANES // n_dom
    group, inside = comp // n_dom, comp % n_dom
    plane = None
    for k, piece in enumerate(pieces):
        value = piece[group]
        shift = ((k - inside) % n_dom) * lanes
        if shift:
            value = pltpu.roll(value, shift, 1)
        if plane is None:
            plane = value
        else:
            lane = lax.broadcasted_iota(jnp.int32, value.shape, 1)
            plane = jnp.where(lane // lanes == k, value, plane)
    return plane


def build(shells_ref, cells, rows_ref, far_ref, sum_ref, near_ref=None):
    root = math.sqrt(scale)
    low, high = cells
    needed = [c % (CELLS + 2) for c in range(low - 1, high + 1)]
    groups_at = sorted({c // 8 * 8 for c in needed})
    rows_ref[...] = jnp.zeros_like(rows_ref)
    for at in groups_at:
        for comp in range(4):
            rows_ref[pl.ds(at * 8 + comp, 8, stride=8), :] = shells_ref[comp, at : at + 8, :]
    for at in groups_at:
        value = rows_ref[at * 8 : (at + 8) * 8]
        row = lax.broadcasted_iota(jnp.int32, value.shape, 0) % 8

        def spread(array):
            total = jnp.sum(array.reshape(8, 8, LANES), axis=1, keepdims=True)
            return jnp.broadcast_to(total, (8, 8, LANES)).reshape(64, LANES)

        mass = spread(jnp.where(row == 3, value, 0.0)) * (coupling * fold / root)
        place = jnp.where(row < 3, value * root, 0.0)
        norm = spread(place * place)
        h, m, l = split(place, 3)
        down = lambda array, by: pltpu.roll(array, by, 0)

        def ends(array, first):
            parts = split(array, 3)
            ones = (row >= 3 - first) & (row < 6 - first)
            kept = jnp.where(ones, 1.0, 0.0)
            for i in range(3):
                kept = jnp.where(row == first + i, parts[i], kept)
            return kept

        def put(ref, groups):
            both = [
                jnp.concatenate(
                    [groups[i].reshape(8, 8, LANES), groups[i + 1].reshape(8, 8, LANES)], axis=1
                )
                for i in range(0, len(groups), 2)
            ]
            count = min(8, ref.shape[0] - at)
            if count > 0:
                value = jnp.concatenate(both, axis=1).astype(bf16)
                ref[at : at + count] = value[:count]

        h3, m3, l3 = down(h, 3), down(m, 3), down(l, 3)
        put(far_ref, [h + m3, h + l3, h + m3, ends(norm, 3)])
        if near_ref is not None:
            near = [-2.0 * (h + h3), -2.0 * (m + h3), -2.0 * (l + m3)]
            put(near_ref, near + [ends(norm + scale * soften, 0)])
        terms = split(mass * jnp.where(row == 3, 1.0, place), 3)
        put(sum_ref, [terms[0] + down(terms[1], 4), terms[2]])


def pair_loop(cells, per, far_rows, sum_rows, centre, out, dist, heavy):
    blocks = [(k, n) for k in range(3) for n in range(len(far_rows))]
    tall = LANES * len(blocks)
    wide = 3
    first, count = cells[0], cells[1] - cells[0]

    def beside(c, k):
        at = c + first + k - 1
        return jnp.where(at < 0, CELLS + 1, at) if k == 0 else at

    def distances(step, b):
        for u in range(per):
            c = step * per + u
            for at in range(0, len(blocks), wide):
                others = jnp.concatenate(
                    [far_rows[n][beside(c, k)] for k, n in blocks[at : at + wide]], axis=1
                )
                low = u * tall + at * LANES
                dist[b][low : low + wide * LANES] = lax.dot_general(
                    others, centre[c + first], TN, preferred_element_type=f32
                )

    def weights(b):
        for at in range(0, per * tall, 64):
            s = dist[b][at : at + 64]
            inverse = lax.rsqrt(s)
            heavy[b][at : at + 64] = jnp.exp2(-s) * (inverse * inverse * inverse)

    def sums(step, b):
        for u in range(per):
            c = step * per + u
            total = None
            for at in range(0, len(blocks), wide):
                terms = jnp.concatenate(
                    [sum_rows[n][beside(c, k)] for k, n in blocks[at : at + wide]], axis=1
                )
                low = u * tall + at * LANES
                w = heavy[b][low : low + wide * LANES]
                head = w.astype(bf16)
                tail = (w - head.astype(f32)).astype(bf16)
                part = lax.dot_general(
                    terms, jnp.concatenate([head, tail], axis=1), NN, preferred_element_type=f32
                )
                part = part[:, :LANES] + part[:, LANES:]
                total = part if total is None else total + part
            out[c] = total

    steps = count // per
    distances(0, 0)
    distances(1, 1)
    weights(0)

    def body(i, _):
        for b in range(2):
            step = 2 * i + b
            sums(step, b)
            weights(1 - b)
            distances(jnp.minimum(step + 2, steps - 1), b)
        return 0

    lax.fori_loop(0, steps // 2, body, 0)


def copy_kernel(source_ref, target_ref):
    target_ref[...] = source_ref[...]


def join_kernel(n_dom, me_ref, *refs):
    pieces, shells_ref = refs[:n_dom], refs[n_dom]
    turn = me_ref[0] * (LANES // n_dom)
    for comp in range(4):
        shells_ref[comp] = pltpu.roll(merged(pieces, comp, n_dom), turn, 1)


def speeds_kernel(n_dom, me_ref, shells_ref, *refs):
    pieces, planes_ref = refs[:n_dom], refs[n_dom]
    turn = me_ref[0] * (LANES // n_dom)
    planes_ref[:4] = shells_ref[:, :CELLS]
    for comp in range(3):
        planes_ref[4 + comp] = pltpu.roll(merged(pieces, comp, n_dom), turn, 1)


def own_kernel(shells_ref, near_out, out_ref, rows, far_rows, sum_rows, *work):
    build(shells_ref, (0, CELLS), rows, far_rows, sum_rows, near_out)
    pair_loop(
        (0, CELLS), 2, [far_rows], [sum_rows], near_out, out_ref, work[0:2], work[2:4]
    )


def side_kernel(cells, up_ref, down_ref, near_ref, own_out, shells_ref, accel_ref, *refs):
    low, high = cells
    count = high - low
    rows, far_rows, sum_rows, out, work = refs[0], refs[1:3], refs[3:5], refs[5], refs[6:]
    for side, there_ref in enumerate((up_ref, down_ref)):
        build(there_ref, cells, rows, far_rows[side], sum_rows[side])
    pair_loop(cells, 1, far_rows, sum_rows, near_ref, out, work[0:2], work[2:4])
    both = out[...] + own_out[low:high]
    both = (both[:, :8] + both[:, 8:]).reshape(count * 8, LANES)
    rows[: count * 8] = both + pltpu.roll(both, count * 8 - 4, 0)
    total = [rows[pl.ds(comp, count, stride=8), :] for comp in range(4)]
    live = shells_ref[3, low:high] > 0
    for comp in range(3):
        centre_at = shells_ref[comp, low:high] * math.sqrt(scale)
        accel_ref[comp] = jnp.where(live, total[comp] - centre_at * total[3], 0.0)


def kick_kernel(planes_ref, *refs):
    accels, out_ref = refs[:-1], refs[-1]
    for comp in range(4):
        out_ref[comp, 0] = planes_ref[comp]
    low = 0
    for accel_ref in accels:
        high = low + accel_ref.shape[1]
        for comp in range(3):
            accel = accel_ref[comp]
            out_ref[4 + comp, 0, low:high] = planes_ref[4 + comp, low:high] + kick_step * accel
            out_ref[7 + comp, 0, low:high] = accel
        low = high


def last_kick_kernel(low, _, planes_ref, accel_ref, out_ref, kicked, sem):
    high = low + accel_ref.shape[1]
    for comp in range(3):
        accel = accel_ref[comp]
        kicked[comp, 0] = planes_ref[4 + comp, low:high] + kick_step * accel
        kicked[3 + comp, 0] = accel
    copy = pltpu.make_async_copy(kicked, out_ref.at[4:10, :, low:high], sem)
    copy.start()
    copy.wait()


def call(
    kernel, n_smem, n_vmem, out_shape, scratch=(), name=None, cost=None, n_any=0, n_same=0, vmem_mib=48
):
    smem = pl.BlockSpec(memory_space=pltpu.SMEM)
    vmem = pl.BlockSpec(memory_space=pltpu.VMEM)
    here = pl.BlockSpec(memory_space=pltpu.HBM)
    return pl.pallas_call(
        kernel,
        in_specs=[smem] * n_smem + [here] * n_any + [vmem] * n_vmem,
        out_specs=jax.tree.map(lambda _: here if n_same else vmem, out_shape),
        out_shape=out_shape,
        scratch_shapes=scratch,
        name=name,
        compiler_params=pltpu.CompilerParams(vmem_limit_bytes=vmem_mib << 20),
        cost_estimate=cost,
        input_output_aliases={i: i for i in range(n_same)},
    )


def sent(value, n_slab, n_dom, by_slab, by_dom):
    pairs = [
        (s * n_dom + d, (s + by_slab) % n_slab * n_dom + (d + by_dom) % n_dom)
        for s in range(n_slab)
        for d in range(n_dom)
    ]
    return lax.ppermute(value, ("slab", "dom"), pairs)


def per_device(positions, velocities, masses, owner_cell, counts):
    n_slab, n_dom = lax.axis_size("slab"), lax.axis_size("dom")
    rows = positions.shape[1]
    lanes = LANES // n_dom
    targets = n_dom * CELLS
    half = 4 * lanes // LANES
    tall = CELLS + EDGES
    me = lax.axis_index("dom").astype(jnp.int32).reshape(1)
    shape = lambda *dims, dtype=f32: jax.ShapeDtypeStruct(dims, dtype)

    whole = call(
        functools.partial(pack_kernel, n_dom),
        2,
        0,
        [shape(half, tall, LANES)] * n_dom + [shape(half, CELLS, LANES)] * n_dom,
        [
            pltpu.VMEM((3, rows), f32),
            pltpu.VMEM((3, rows), f32),
            pltpu.VMEM((1, rows), f32),
            pltpu.VMEM((1, rows), jnp.int32),
            pltpu.VMEM((1, rows), jnp.int32),
            pltpu.VMEM((1, rows), jnp.int32),
            pltpu.VMEM((8 * lanes, targets), f32),
            pltpu.SemaphoreType.DMA((4,)),
        ],
        name="pack",
        n_any=4,
        vmem_mib=63,
    )(me, counts, positions, velocities, masses.reshape(1, rows), owner_cell.reshape(1, rows))

    def swapped(parts):
        return [parts[0]] + [
            sent(parts[-k % n_dom], n_slab, n_dom, 0, -k) for k in range(1, n_dom)
        ]

    places, speeds = swapped(whole[:n_dom]), swapped(whole[n_dom:])
    places[0] = call(copy_kernel, 0, 1, shape(half, tall, LANES), name="own_piece")(places[0])
    shells = call(
        functools.partial(join_kernel, n_dom), 1, n_dom, shape(4, tall, LANES), name="join"
    )(me, *places)
    planes = call(
        functools.partial(speeds_kernel, n_dom),
        1,
        1 + n_dom,
        shape(7, CELLS, LANES),
        name="speeds",
    )(me, shells, *speeds)
    below, above = (sent(shells, n_slab, n_dom, side, 0) for side in (1, -1))
    early = sent(planes, n_slab, n_dom, n_slab // 2, 0)

    def pair_work(size):
        return [pltpu.VMEM((size, LANES), f32)] * 4

    def row_work(copies):
        return (
            [pltpu.VMEM((tall * 8, LANES), f32)]
            + [pltpu.VMEM((tall, FEATURES, LANES), bf16)] * copies
            + [pltpu.VMEM((tall, 16, LANES), bf16)] * copies
        )

    near, sums = call(
        own_kernel,
        0,
        1,
        [shape(CELLS, FEATURES, LANES, dtype=bf16), shape(CELLS, 16, LANES)],
        row_work(1) + pair_work(768),
        name="own_slab",
        cost=pl.CostEstimate(flops=8_000_000_000, bytes_accessed=1_000_000, transcendentals=0),
    )(shells)
    accels = []
    cut = CELLS * 3 // 4
    for cells in ((0, cut), (cut, CELLS)):
        count = cells[1] - cells[0]
        accels.append(
            call(
                functools.partial(side_kernel, cells),
                0,
                5,
                shape(3, count, LANES),
                row_work(2) + [pltpu.VMEM((count, 16, LANES), f32)] + pair_work(768),
                name="side_slabs",
                cost=pl.CostEstimate(flops=8_000_000_000, bytes_accessed=1_000_000, transcendentals=0),
            )(below, above, near, sums, shells)
        )
    later = [sent(accel, n_slab, n_dom, n_slab // 2, 0) for accel in accels]
    out = shape(10, 1, CELLS, LANES)
    state = call(kick_kernel, 0, 3, out, name="state")(planes, *accels)
    part = call(kick_kernel, 0, 2, out, name="buddy")(early, later[0])
    buddy = call(
        functools.partial(last_kick_kernel, cut),
        0,
        2,
        out,
        [pltpu.VMEM((6, 1, CELLS - cut, LANES), f32), pltpu.SemaphoreType.DMA],
        name="buddy_end",
        n_any=1,
        n_same=1,
    )(part, early, later[1])
    return state, buddy


def solution(mesh):
    placed = (
        P(None, ("slab", "dom")),
        P(None, ("slab", "dom")),
        P(("slab", "dom")),
        P(("slab", "dom"), None),
        P(("slab", "dom")),
    )
    return jax.shard_map(
        per_device,
        mesh=mesh,
        in_specs=placed,
        out_specs=(P(None, "slab", "dom", None), P(None, "slab", "dom", None)),
        check_vma=False,
    )
```

```python
import functools
import math

import jax
import jax.numpy as jnp
from jax import lax
from jax.experimental import pallas as pl
from jax.experimental.pallas import tpu as pltpu
from jax.sharding import PartitionSpec as P

CELLS = 64
LANES = 128

drift_step = 0.5
kick_step = 0.5
soften = 0.25
reach = 4.0
coupling = 0.25

scale = math.log2(math.e) / reach
fold = scale**1.5 * math.exp(soften / reach)

f32 = jnp.float32
bf16 = jnp.bfloat16
NN = (((1,), (0,)), ((), ()))
NT = (((1,), (1,)), ((), ()))
TN = (((0,), (0,)), ((), ()))
FEATURES = 32
EDGES = 8


def split(value, pieces):
    parts = []
    for _ in range(pieces):
        head = value.astype(bf16).astype(f32)
        parts.append(head)
        value = value - head
    return parts


def pack_kernel(n_dom, me_ref, count_ref, pos_any, vel_any, mass_any, owner_any, *refs):
    outs, refs = refs[: 2 * n_dom], refs[2 * n_dom :]
    pos_ref, vel_ref, mass_ref, owner_ref, rank_ref, target_ref, total_ref, sems = refs
    copies = [
        pltpu.make_async_copy(source, target, sems.at[i])
        for i, (source, target) in enumerate(
            [(owner_any, owner_ref), (pos_any, pos_ref), (vel_any, vel_ref), (mass_any, mass_ref)]
        )
    ]
    for copy in copies:
        copy.start()
    rows = pos_ref.shape[1]
    targets, lanes = n_dom * CELLS, LANES // n_dom
    part = lanes // 2
    chunk = 256
    before = (
        lax.broadcasted_iota(jnp.int32, (chunk, chunk + LANES), 0)
        < lax.broadcasted_iota(jnp.int32, (chunk, chunk + LANES), 1)
    ).astype(f32).astype(bf16)
    carry = jnp.zeros((targets, LANES), f32)
    number = lax.broadcasted_iota(jnp.int32, (targets, chunk), 0)
    copies[0].wait()
    for at in range(0, rows, chunk):
        target = owner_ref[:, at : at + chunk] - me_ref[0] * CELLS
        target = jnp.where(target < 0, target + targets, target)
        place = lax.broadcasted_iota(jnp.int32, (1, chunk), 1) + at
        target = jnp.where(place < count_ref[0], target, -1)
        target_ref[:, at : at + chunk] = target
        same = number == target
        hot = jnp.where(same, 1.0, 0.0).astype(bf16)
        seen = lax.dot_general(hot, before, NN, preferred_element_type=f32)
        wide = jnp.concatenate([carry] * (chunk // LANES), axis=1)
        rank = jnp.sum(jnp.where(same, seen[:, :chunk] + wide, 0.0), axis=0, keepdims=True)
        rank_ref[:, at : at + chunk] = rank.astype(jnp.int32)
        carry = carry + seen[:, chunk:]
    for copy in copies[1:]:
        copy.wait()
    step = 1024
    row = lax.broadcasted_iota(jnp.int32, (part, step), 0)
    column = lax.broadcasted_iota(jnp.int32, (2 * targets, step), 0)
    for at in range(0, rows, step):
        span = slice(at, at + step)
        rank, target = rank_ref[:, span], target_ref[:, span]
        upper = rank >= part
        mark = jnp.where(row == jnp.where(upper, rank - part, rank), 1.0, 0.0)
        place = jnp.where(upper & (target >= 0), target + targets, target)
        hot = jnp.where(column == place, 1.0, 0.0).astype(bf16)
        values = [pos_ref[i : i + 1, span] + drift_step * vel_ref[i : i + 1, span] for i in range(3)]
        values += [mass_ref[:, span]]
        values += [vel_ref[i : i + 1, span] for i in range(3)]
        pieces = [split(value, 2) for value in values]
        left = [
            jnp.concatenate([(mark * piece[k]).astype(bf16) for piece in pieces], axis=0)
            for k in range(2)
        ]
        found = lax.dot_general(
            jnp.concatenate(left, axis=1),
            jnp.concatenate([hot] * 2, axis=1),
            NT,
            preferred_element_type=f32,
        )
        for comp in range(7):
            for half in range(2):
                low = comp * lanes + half * part
                value = found[comp * part : (comp + 1) * part, half * targets : (half + 1) * targets]
                if at == 0:
                    total_ref[low : low + part] = value
                else:
                    total_ref[low : low + part] += value
    total_ref[7 * lanes :] = jnp.zeros((lanes, targets), f32)
    groups = 8 * lanes // LANES
    packed = [
        jnp.concatenate(
            [
                total_ref[g * LANES : (g + 1) * LANES, t : t + LANES].T
                for t in range(0, targets, LANES)
            ],
            axis=0,
        )
        for g in range(groups)
    ]
    for by in range(n_dom):
        low, high = by * CELLS, (by + 1) * CELLS
        edge_high, edge_low = high % targets, (low - 1) % targets
        for g in range(groups // 2):
            edges = jnp.concatenate(
                [
                    packed[g][edge_high : edge_high + 1],
                    packed[g][edge_low : edge_low + 1],
                    jnp.zeros((EDGES - 2, LANES), f32),
                ],
                axis=0,
            )
            outs[by][g] = jnp.concatenate([packed[g][low:high], edges], axis=0)
            outs[n_dom + by][g] = packed[groups // 2 + g][low:high]


def merged(pieces, comp, n_dom):
    lanes = LANES // n_dom
    group, inside = comp // n_dom, comp % n_dom
    plane = None
    for k, piece in enumerate(pieces):
        value = piece[group]
        shift = ((k - inside) % n_dom) * lanes
        if shift:
            value = pltpu.roll(value, shift, 1)
        if plane is None:
            plane = value
        else:
            lane = lax.broadcasted_iota(jnp.int32, value.shape, 1)
            plane = jnp.where(lane // lanes == k, value, plane)
    return plane


def build(shells_ref, cells, rows_ref, far_ref, sum_ref, near_ref=None):
    root = math.sqrt(scale)
    low, high = cells
    needed = [c % (CELLS + 2) for c in range(low - 1, high + 1)]
    groups_at = sorted({c // 8 * 8 for c in needed})
    rows_ref[...] = jnp.zeros_like(rows_ref)
    for at in groups_at:
        for comp in range(4):
            rows_ref[pl.ds(at * 8 + comp, 8, stride=8), :] = shells_ref[comp, at : at + 8, :]
    for at in groups_at:
        value = rows_ref[at * 8 : (at + 8) * 8]
        row = lax.broadcasted_iota(jnp.int32, value.shape, 0) % 8

        def spread(array):
            total = jnp.sum(array.reshape(8, 8, LANES), axis=1, keepdims=True)
            return jnp.broadcast_to(total, (8, 8, LANES)).reshape(64, LANES)

        mass = spread(jnp.where(row == 3, value, 0.0)) * (coupling * fold / root)
        place = jnp.where(row < 3, value * root, 0.0)
        norm = spread(place * place)
        h, m, l = split(place, 3)
        down = lambda array, by: pltpu.roll(array, by, 0)

        def ends(array, first):
            parts = split(array, 3)
            ones = (row >= 3 - first) & (row < 6 - first)
            kept = jnp.where(ones, 1.0, 0.0)
            for i in range(3):
                kept = jnp.where(row == first + i, parts[i], kept)
            return kept

        def put(ref, groups):
            both = [
                jnp.concatenate(
                    [groups[i].reshape(8, 8, LANES), groups[i + 1].reshape(8, 8, LANES)], axis=1
                )
                for i in range(0, len(groups), 2)
            ]
            count = min(8, ref.shape[0] - at)
            if count > 0:
                value = jnp.concatenate(both, axis=1).astype(bf16)
                ref[at : at + count] = value[:count]

        h3, m3, l3 = down(h, 3), down(m, 3), down(l, 3)
        put(far_ref, [h + m3, h + l3, h + m3, ends(norm, 3)])
        if near_ref is not None:
            near = [-2.0 * (h + h3), -2.0 * (m + h3), -2.0 * (l + m3)]
            put(near_ref, near + [ends(norm + scale * soften, 0)])
        terms = split(mass * jnp.where(row == 3, 1.0, place), 3)
        put(sum_ref, [terms[0] + down(terms[1], 4), terms[2]])


def pair_loop(cells, per, apart, far_rows, sum_rows, centre, out, dist, heavy):
    blocks = [(k, n) for k in range(3) for n in range(len(far_rows))]
    tall = LANES * len(blocks)
    wide = 3
    first, count = cells[0], cells[1] - cells[0]

    def beside(c, k):
        at = c + first + k - 1
        return jnp.where(at < 0, CELLS + 1, at) if k == 0 else at

    def distances(step, b):
        for u in range(per):
            c = step * per + u
            for at in range(0, len(blocks), apart):
                others = jnp.concatenate(
                    [far_rows[n][beside(c, k)] for k, n in blocks[at : at + apart]], axis=1
                )
                low = u * tall + at * LANES
                dist[b][low : low + apart * LANES] = lax.dot_general(
                    others, centre[c + first], TN, preferred_element_type=f32
                )

    def weights(b):
        for at in range(0, per * tall, 64):
            s = dist[b][at : at + 64]
            inverse = lax.rsqrt(s)
            heavy[b][at : at + 64] = jnp.exp2(-s) * (inverse * inverse * inverse)

    def sums(step, b):
        for u in range(per):
            c = step * per + u
            total = None
            for at in range(0, len(blocks), wide):
                terms = jnp.concatenate(
                    [sum_rows[n][beside(c, k)] for k, n in blocks[at : at + wide]], axis=1
                )
                low = u * tall + at * LANES
                w = heavy[b][low : low + wide * LANES]
                head = w.astype(bf16)
                tail = (w - head.astype(f32)).astype(bf16)
                part = lax.dot_general(
                    terms, jnp.concatenate([head, tail], axis=1), NN, preferred_element_type=f32
                )
                part = part[:, :LANES] + part[:, LANES:]
                total = part if total is None else total + part
            out[c] = total

    steps = count // per
    distances(0, 0)
    distances(1, 1)
    weights(0)

    def body(i, _):
        for b in range(2):
            step = 2 * i + b
            sums(step, b)
            weights(1 - b)
            distances(jnp.minimum(step + 2, steps - 1), b)
        return 0

    lax.fori_loop(0, steps // 2, body, 0, unroll=8)


def copy_kernel(source_ref, target_ref):
    target_ref[...] = source_ref[...]


def join_kernel(n_dom, me_ref, *refs):
    pieces, shells_ref = refs[:n_dom], refs[n_dom]
    turn = me_ref[0] * (LANES // n_dom)
    for comp in range(4):
        shells_ref[comp] = pltpu.roll(merged(pieces, comp, n_dom), turn, 1)


def speeds_kernel(n_dom, me_ref, shells_ref, *refs):
    pieces, planes_ref = refs[:n_dom], refs[n_dom]
    turn = me_ref[0] * (LANES // n_dom)
    planes_ref[:4] = shells_ref[:, :CELLS]
    for comp in range(3):
        planes_ref[4 + comp] = pltpu.roll(merged(pieces, comp, n_dom), turn, 1)


def own_kernel(shells_ref, near_out, out_ref, rows, far_rows, sum_rows, *work):
    build(shells_ref, (0, CELLS), rows, far_rows, sum_rows, near_out)
    pair_loop(
        (0, CELLS), 2, 1, [far_rows], [sum_rows], near_out, out_ref, work[0:2], work[2:4]
    )


def side_kernel(cells, up_ref, down_ref, near_ref, own_out, shells_ref, accel_ref, *refs):
    low, high = cells
    count = high - low
    rows, far_rows, sum_rows, out, work = refs[0], refs[1:3], refs[3:5], refs[5], refs[6:]
    for side, there_ref in enumerate((up_ref, down_ref)):
        build(there_ref, cells, rows, far_rows[side], sum_rows[side])
    pair_loop(cells, 1, 2, far_rows, sum_rows, near_ref, out, work[0:2], work[2:4])
    both = out[...] + own_out[low:high]
    both = (both[:, :8] + both[:, 8:]).reshape(count * 8, LANES)
    rows[: count * 8] = both + pltpu.roll(both, count * 8 - 4, 0)
    total = [rows[pl.ds(comp, count, stride=8), :] for comp in range(4)]
    live = shells_ref[3, low:high] > 0
    for comp in range(3):
        centre_at = shells_ref[comp, low:high] * math.sqrt(scale)
        accel_ref[comp] = jnp.where(live, total[comp] - centre_at * total[3], 0.0)


def kick_kernel(planes_ref, *refs):
    accels, out_ref = refs[:-1], refs[-1]
    for comp in range(4):
        out_ref[comp, 0] = planes_ref[comp]
    low = 0
    for accel_ref in accels:
        high = low + accel_ref.shape[1]
        for comp in range(3):
            accel = accel_ref[comp]
            out_ref[4 + comp, 0, low:high] = planes_ref[4 + comp, low:high] + kick_step * accel
            out_ref[7 + comp, 0, low:high] = accel
        low = high


def last_kick_kernel(low, _, planes_ref, accel_ref, out_ref, kicked, sem):
    high = low + accel_ref.shape[1]
    for comp in range(3):
        accel = accel_ref[comp]
        kicked[comp, 0] = planes_ref[4 + comp, low:high] + kick_step * accel
        kicked[3 + comp, 0] = accel
    copy = pltpu.make_async_copy(kicked, out_ref.at[4:10, :, low:high], sem)
    copy.start()
    copy.wait()


def call(
    kernel, n_smem, n_vmem, out_shape, scratch=(), name=None, cost=None, n_any=0, n_same=0, vmem_mib=48
):
    smem = pl.BlockSpec(memory_space=pltpu.SMEM)
    vmem = pl.BlockSpec(memory_space=pltpu.VMEM)
    here = pl.BlockSpec(memory_space=pltpu.HBM)
    return pl.pallas_call(
        kernel,
        in_specs=[smem] * n_smem + [here] * n_any + [vmem] * n_vmem,
        out_specs=jax.tree.map(lambda _: here if n_same else vmem, out_shape),
        out_shape=out_shape,
        scratch_shapes=scratch,
        name=name,
        compiler_params=pltpu.CompilerParams(vmem_limit_bytes=vmem_mib << 20),
        cost_estimate=cost,
        input_output_aliases={i: i for i in range(n_same)},
    )


def sent(value, n_slab, n_dom, by_slab, by_dom):
    pairs = [
        (s * n_dom + d, (s + by_slab) % n_slab * n_dom + (d + by_dom) % n_dom)
        for s in range(n_slab)
        for d in range(n_dom)
    ]
    return lax.ppermute(value, ("slab", "dom"), pairs)


def per_device(positions, velocities, masses, owner_cell, counts):
    n_slab, n_dom = lax.axis_size("slab"), lax.axis_size("dom")
    rows = positions.shape[1]
    lanes = LANES // n_dom
    targets = n_dom * CELLS
    half = 4 * lanes // LANES
    tall = CELLS + EDGES
    me = lax.axis_index("dom").astype(jnp.int32).reshape(1)
    shape = lambda *dims, dtype=f32: jax.ShapeDtypeStruct(dims, dtype)

    whole = call(
        functools.partial(pack_kernel, n_dom),
        2,
        0,
        [shape(half, tall, LANES)] * n_dom + [shape(half, CELLS, LANES)] * n_dom,
        [
            pltpu.VMEM((3, rows), f32),
            pltpu.VMEM((3, rows), f32),
            pltpu.VMEM((1, rows), f32),
            pltpu.VMEM((1, rows), jnp.int32),
            pltpu.VMEM((1, rows), jnp.int32),
            pltpu.VMEM((1, rows), jnp.int32),
            pltpu.VMEM((8 * lanes, targets), f32),
            pltpu.SemaphoreType.DMA((4,)),
        ],
        name="pack",
        n_any=4,
        vmem_mib=63,
    )(me, counts, positions, velocities, masses.reshape(1, rows), owner_cell.reshape(1, rows))

    def swapped(parts):
        return [parts[0]] + [
            sent(parts[-k % n_dom], n_slab, n_dom, 0, -k) for k in range(1, n_dom)
        ]

    places, speeds = swapped(whole[:n_dom]), swapped(whole[n_dom:])
    places[0] = call(copy_kernel, 0, 1, shape(half, tall, LANES), name="own_piece")(places[0])
    shells = call(
        functools.partial(join_kernel, n_dom), 1, n_dom, shape(4, tall, LANES), name="join"
    )(me, *places)
    planes = call(
        functools.partial(speeds_kernel, n_dom),
        1,
        1 + n_dom,
        shape(7, CELLS, LANES),
        name="speeds",
    )(me, shells, *speeds)
    below, above = (sent(shells, n_slab, n_dom, side, 0) for side in (1, -1))
    early = sent(planes, n_slab, n_dom, n_slab // 2, 0)

    def pair_work(size):
        return [pltpu.VMEM((size, LANES), f32)] * 4

    def row_work(copies):
        return (
            [pltpu.VMEM((tall * 8, LANES), f32)]
            + [pltpu.VMEM((tall, FEATURES, LANES), bf16)] * copies
            + [pltpu.VMEM((tall, 16, LANES), bf16)] * copies
        )

    near, sums = call(
        own_kernel,
        0,
        1,
        [shape(CELLS, FEATURES, LANES, dtype=bf16), shape(CELLS, 16, LANES)],
        row_work(1) + pair_work(768),
        name="own_slab",
        cost=pl.CostEstimate(flops=8_000_000_000, bytes_accessed=1_000_000, transcendentals=0),
    )(shells)
    accels = []
    cut = CELLS * 3 // 4
    for cells in ((0, cut), (cut, CELLS)):
        count = cells[1] - cells[0]
        accels.append(
            call(
                functools.partial(side_kernel, cells),
                0,
                5,
                shape(3, count, LANES),
                row_work(2) + [pltpu.VMEM((count, 16, LANES), f32)] + pair_work(768),
                name="side_slabs",
                cost=pl.CostEstimate(flops=8_000_000_000, bytes_accessed=1_000_000, transcendentals=0),
            )(below, above, near, sums, shells)
        )
    later = [sent(accel, n_slab, n_dom, n_slab // 2, 0) for accel in accels]
    out = shape(10, 1, CELLS, LANES)
    state = call(kick_kernel, 0, 3, out, name="state")(planes, *accels)
    part = call(kick_kernel, 0, 2, out, name="buddy")(early, later[0])
    buddy = call(
        functools.partial(last_kick_kernel, cut),
        0,
        2,
        out,
        [pltpu.VMEM((6, 1, CELLS - cut, LANES), f32), pltpu.SemaphoreType.DMA],
        name="buddy_end",
        n_any=1,
        n_same=1,
    )(part, early, later[1])
    return state, buddy


def solution(mesh):
    placed = (
        P(None, ("slab", "dom")),
        P(None, ("slab", "dom")),
        P(("slab", "dom")),
        P(("slab", "dom"), None),
        P(("slab", "dom")),
    )
    return jax.shard_map(
        per_device,
        mesh=mesh,
        in_specs=placed,
        out_specs=(P(None, "slab", "dom", None), P(None, "slab", "dom", None)),
        check_vma=False,
    )
```

```python
import functools
import math

import jax
import jax.numpy as jnp
from jax import lax
from jax.experimental import pallas as pl
from jax.experimental.pallas import tpu as pltpu
from jax.sharding import PartitionSpec as P

CELLS = 64
LANES = 128

drift_step = 0.5
kick_step = 0.5
soften = 0.25
reach = 4.0
coupling = 0.25

scale = math.log2(math.e) / reach
fold = scale**1.5 * math.exp(soften / reach)

f32 = jnp.float32
bf16 = jnp.bfloat16
NN = (((1,), (0,)), ((), ()))
NT = (((1,), (1,)), ((), ()))
TN = (((0,), (0,)), ((), ()))
FEATURES = 32
EDGES = 8


def split(value, pieces):
    parts = []
    for _ in range(pieces):
        head = value.astype(bf16).astype(f32)
        parts.append(head)
        value = value - head
    return parts


def pack_kernel(n_dom, me_ref, count_ref, pos_any, vel_any, mass_any, owner_any, *refs):
    outs, refs = refs[: 2 * n_dom], refs[2 * n_dom :]
    pos_ref, vel_ref, mass_ref, owner_ref, rank_ref, target_ref, total_ref, sems = refs
    copies = [
        pltpu.make_async_copy(source, target, sems.at[i])
        for i, (source, target) in enumerate(
            [(owner_any, owner_ref), (pos_any, pos_ref), (vel_any, vel_ref), (mass_any, mass_ref)]
        )
    ]
    for copy in copies:
        copy.start()
    rows = pos_ref.shape[1]
    targets, lanes = n_dom * CELLS, LANES // n_dom
    part = lanes // 2
    chunk = 256
    before = (
        lax.broadcasted_iota(jnp.int32, (chunk, chunk + LANES), 0)
        < lax.broadcasted_iota(jnp.int32, (chunk, chunk + LANES), 1)
    ).astype(f32).astype(bf16)
    carry = jnp.zeros((targets, LANES), f32)
    number = lax.broadcasted_iota(jnp.int32, (targets, chunk), 0)
    copies[0].wait()
    for at in range(0, rows, chunk):
        target = owner_ref[:, at : at + chunk] - me_ref[0] * CELLS
        target = jnp.where(target < 0, target + targets, target)
        place = lax.broadcasted_iota(jnp.int32, (1, chunk), 1) + at
        target = jnp.where(place < count_ref[0], target, -1)
        target_ref[:, at : at + chunk] = target
        same = number == target
        hot = jnp.where(same, 1.0, 0.0).astype(bf16)
        seen = lax.dot_general(hot, before, NN, preferred_element_type=f32)
        wide = jnp.concatenate([carry] * (chunk // LANES), axis=1)
        rank = jnp.sum(jnp.where(same, seen[:, :chunk] + wide, 0.0), axis=0, keepdims=True)
        rank_ref[:, at : at + chunk] = rank.astype(jnp.int32)
        carry = carry + seen[:, chunk:]
    for copy in copies[1:]:
        copy.wait()
    step = 1024
    row = lax.broadcasted_iota(jnp.int32, (part, step), 0)
    column = lax.broadcasted_iota(jnp.int32, (2 * targets, step), 0)
    for at in range(0, rows, step):
        span = slice(at, at + step)
        rank, target = rank_ref[:, span], target_ref[:, span]
        upper = rank >= part
        mark = row == jnp.where(upper, rank - part, rank)
        place = jnp.where(upper & (target >= 0), target + targets, target)
        hot = jnp.where(column == place, 1.0, 0.0).astype(bf16)
        values = [pos_ref[i : i + 1, span] + drift_step * vel_ref[i : i + 1, span] for i in range(3)]
        values += [mass_ref[:, span]]
        values += [vel_ref[i : i + 1, span] for i in range(3)]
        pieces = [split(value, 2) for value in values]
        left = [
            jnp.concatenate([jnp.where(mark, piece[k], 0.0).astype(bf16) for piece in pieces], axis=0)
            for k in range(2)
        ]
        found = lax.dot_general(
            jnp.concatenate(left, axis=1),
            jnp.concatenate([hot] * 2, axis=1),
            NT,
            preferred_element_type=f32,
        )
        for comp in range(7):
            for half in range(2):
                low = comp * lanes + half * part
                value = found[comp * part : (comp + 1) * part, half * targets : (half + 1) * targets]
                if at == 0:
                    total_ref[low : low + part] = value
                else:
                    total_ref[low : low + part] += value
    total_ref[7 * lanes :] = jnp.zeros((lanes, targets), f32)
    groups = 8 * lanes // LANES
    packed = [
        jnp.concatenate(
            [
                total_ref[g * LANES : (g + 1) * LANES, t : t + LANES].T
                for t in range(0, targets, LANES)
            ],
            axis=0,
        )
        for g in range(groups)
    ]
    for by in range(n_dom):
        low, high = by * CELLS, (by + 1) * CELLS
        edge_high, edge_low = high % targets, (low - 1) % targets
        for g in range(groups // 2):
            edges = jnp.concatenate(
                [
                    packed[g][edge_high : edge_high + 1],
                    packed[g][edge_low : edge_low + 1],
                    jnp.zeros((EDGES - 2, LANES), f32),
                ],
                axis=0,
            )
            outs[by][g] = jnp.concatenate([packed[g][low:high], edges], axis=0)
            outs[n_dom + by][g] = packed[groups // 2 + g][low:high]


def merged(pieces, comp, n_dom):
    lanes = LANES // n_dom
    group, inside = comp // n_dom, comp % n_dom
    plane = None
    for k, piece in enumerate(pieces):
        value = piece[group]
        shift = ((k - inside) % n_dom) * lanes
        if shift:
            value = pltpu.roll(value, shift, 1)
        if plane is None:
            plane = value
        else:
            lane = lax.broadcasted_iota(jnp.int32, value.shape, 1)
            plane = jnp.where(lane // lanes == k, value, plane)
    return plane


def build(shells_ref, cells, rows_ref, far_ref, sum_ref, near_ref=None):
    root = math.sqrt(scale)
    low, high = cells
    needed = [c % (CELLS + 2) for c in range(low - 1, high + 1)]
    groups_at = sorted({c // 8 * 8 for c in needed})
    rows_ref[...] = jnp.zeros_like(rows_ref)
    for at in groups_at:
        for comp in range(4):
            rows_ref[pl.ds(at * 8 + comp, 8, stride=8), :] = shells_ref[comp, at : at + 8, :]
    for at in groups_at:
        value = rows_ref[at * 8 : (at + 8) * 8]
        row = lax.broadcasted_iota(jnp.int32, value.shape, 0) % 8

        def spread(array):
            total = jnp.sum(array.reshape(8, 8, LANES), axis=1, keepdims=True)
            return jnp.broadcast_to(total, (8, 8, LANES)).reshape(64, LANES)

        mass = spread(jnp.where(row == 3, value, 0.0)) * (coupling * fold / root)
        place = jnp.where(row < 3, value * root, 0.0)
        norm = spread(place * place)
        h, m, l = split(place, 3)
        down = lambda array, by: pltpu.roll(array, by, 0)

        def ends(array, first):
            parts = split(array, 3)
            ones = (row >= 3 - first) & (row < 6 - first)
            kept = jnp.where(ones, 1.0, 0.0)
            for i in range(3):
                kept = jnp.where(row == first + i, parts[i], kept)
            return kept

        def put(ref, groups):
            both = [
                jnp.concatenate(
                    [groups[i].reshape(8, 8, LANES), groups[i + 1].reshape(8, 8, LANES)], axis=1
                )
                for i in range(0, len(groups), 2)
            ]
            count = min(8, ref.shape[0] - at)
            if count > 0:
                value = jnp.concatenate(both, axis=1).astype(bf16)
                ref[at : at + count] = value[:count]

        h3, m3, l3 = down(h, 3), down(m, 3), down(l, 3)
        put(far_ref, [h + m3, h + l3, h + m3, ends(norm, 3)])
        if near_ref is not None:
            near = [-2.0 * (h + h3), -2.0 * (m + h3), -2.0 * (l + m3)]
            put(near_ref, near + [ends(norm + scale * soften, 0)])
        terms = split(mass * jnp.where(row == 3, 1.0, place), 3)
        put(sum_ref, [terms[0] + down(terms[1], 4), terms[2]])


def pair_loop(cells, per, apart, far_rows, sum_rows, centre, out, dist, heavy):
    blocks = [(k, n) for k in range(3) for n in range(len(far_rows))]
    tall = LANES * len(blocks)
    wide = 3
    first, count = cells[0], cells[1] - cells[0]

    def beside(c, k):
        at = c + first + k - 1
        return jnp.where(at < 0, CELLS + 1, at) if k == 0 else at

    def distances(step, b):
        for u in range(per):
            c = step * per + u
            for at in range(0, len(blocks), apart):
                others = jnp.concatenate(
                    [far_rows[n][beside(c, k)] for k, n in blocks[at : at + apart]], axis=1
                )
                low = u * tall + at * LANES
                dist[b][low : low + apart * LANES] = lax.dot_general(
                    others, centre[c + first], TN, preferred_element_type=f32
                )

    def weights(b):
        for at in range(0, per * tall, 64):
            s = dist[b][at : at + 64]
            inverse = lax.rsqrt(s)
            heavy[b][at : at + 64] = jnp.exp2(-s) * (inverse * inverse * inverse)

    def sums(step, b):
        for u in range(per):
            c = step * per + u
            total = None
            for at in range(0, len(blocks), wide):
                terms = jnp.concatenate(
                    [sum_rows[n][beside(c, k)] for k, n in blocks[at : at + wide]], axis=1
                )
                low = u * tall + at * LANES
                w = heavy[b][low : low + wide * LANES]
                head = w.astype(bf16)
                tail = (w - head.astype(f32)).astype(bf16)
                part = lax.dot_general(
                    terms, jnp.concatenate([head, tail], axis=1), NN, preferred_element_type=f32
                )
                part = part[:, :LANES] + part[:, LANES:]
                total = part if total is None else total + part
            out[c] = total

    steps = count // per
    distances(0, 0)
    distances(1, 1)
    weights(0)

    def body(i, _):
        for b in range(2):
            step = 2 * i + b
            sums(step, b)
            weights(1 - b)
            distances(jnp.minimum(step + 2, steps - 1), b)
        return 0

    lax.fori_loop(0, steps // 2, body, 0, unroll=8)


def copy_kernel(source_ref, target_ref):
    target_ref[...] = source_ref[...]


def join_kernel(n_dom, me_ref, *refs):
    pieces, shells_ref = refs[:n_dom], refs[n_dom]
    turn = me_ref[0] * (LANES // n_dom)
    for comp in range(4):
        shells_ref[comp] = pltpu.roll(merged(pieces, comp, n_dom), turn, 1)


def speeds_kernel(n_dom, me_ref, shells_ref, *refs):
    pieces, planes_ref = refs[:n_dom], refs[n_dom]
    turn = me_ref[0] * (LANES // n_dom)
    planes_ref[:4] = shells_ref[:, :CELLS]
    for comp in range(3):
        planes_ref[4 + comp] = pltpu.roll(merged(pieces, comp, n_dom), turn, 1)


def own_kernel(shells_ref, near_out, out_ref, rows, far_rows, sum_rows, *work):
    build(shells_ref, (0, CELLS), rows, far_rows, sum_rows, near_out)
    pair_loop(
        (0, CELLS), 2, 1, [far_rows], [sum_rows], near_out, out_ref, work[0:2], work[2:4]
    )


def side_kernel(cells, up_ref, down_ref, near_ref, own_out, shells_ref, accel_ref, *refs):
    low, high = cells
    count = high - low
    rows, far_rows, sum_rows, out, work = refs[0], refs[1:3], refs[3:5], refs[5], refs[6:]
    for side, there_ref in enumerate((up_ref, down_ref)):
        build(there_ref, cells, rows, far_rows[side], sum_rows[side])
    pair_loop(cells, 1, 2, far_rows, sum_rows, near_ref, out, work[0:2], work[2:4])
    both = out[...] + own_out[low:high]
    both = (both[:, :8] + both[:, 8:]).reshape(count * 8, LANES)
    rows[: count * 8] = both + pltpu.roll(both, count * 8 - 4, 0)
    total = [rows[pl.ds(comp, count, stride=8), :] for comp in range(4)]
    live = shells_ref[3, low:high] > 0
    for comp in range(3):
        centre_at = shells_ref[comp, low:high] * math.sqrt(scale)
        accel_ref[comp] = jnp.where(live, total[comp] - centre_at * total[3], 0.0)


def kick_kernel(planes_ref, *refs):
    accels, out_ref = refs[:-1], refs[-1]
    for comp in range(4):
        out_ref[comp, 0] = planes_ref[comp]
    low = 0
    for accel_ref in accels:
        high = low + accel_ref.shape[1]
        for comp in range(3):
            accel = accel_ref[comp]
            out_ref[4 + comp, 0, low:high] = planes_ref[4 + comp, low:high] + kick_step * accel
            out_ref[7 + comp, 0, low:high] = accel
        low = high


def last_kick_kernel(low, _, planes_ref, accel_ref, out_ref, kicked, sem):
    high = low + accel_ref.shape[1]
    for comp in range(3):
        accel = accel_ref[comp]
        kicked[comp, 0] = planes_ref[4 + comp, low:high] + kick_step * accel
        kicked[3 + comp, 0] = accel
    copy = pltpu.make_async_copy(kicked, out_ref.at[4:10, :, low:high], sem)
    copy.start()
    copy.wait()


def call(
    kernel, n_smem, n_vmem, out_shape, scratch=(), name=None, cost=None, n_any=0, n_same=0, vmem_mib=48
):
    smem = pl.BlockSpec(memory_space=pltpu.SMEM)
    vmem = pl.BlockSpec(memory_space=pltpu.VMEM)
    here = pl.BlockSpec(memory_space=pltpu.HBM)
    return pl.pallas_call(
        kernel,
        in_specs=[smem] * n_smem + [here] * n_any + [vmem] * n_vmem,
        out_specs=jax.tree.map(lambda _: here if n_same else vmem, out_shape),
        out_shape=out_shape,
        scratch_shapes=scratch,
        name=name,
        compiler_params=pltpu.CompilerParams(vmem_limit_bytes=vmem_mib << 20),
        cost_estimate=cost,
        input_output_aliases={i: i for i in range(n_same)},
    )


def sent(value, n_slab, n_dom, by_slab, by_dom):
    pairs = [
        (s * n_dom + d, (s + by_slab) % n_slab * n_dom + (d + by_dom) % n_dom)
        for s in range(n_slab)
        for d in range(n_dom)
    ]
    return lax.ppermute(value, ("slab", "dom"), pairs)


def per_device(positions, velocities, masses, owner_cell, counts):
    n_slab, n_dom = lax.axis_size("slab"), lax.axis_size("dom")
    rows = positions.shape[1]
    lanes = LANES // n_dom
    targets = n_dom * CELLS
    half = 4 * lanes // LANES
    tall = CELLS + EDGES
    me = lax.axis_index("dom").astype(jnp.int32).reshape(1)
    shape = lambda *dims, dtype=f32: jax.ShapeDtypeStruct(dims, dtype)

    whole = call(
        functools.partial(pack_kernel, n_dom),
        2,
        0,
        [shape(half, tall, LANES)] * n_dom + [shape(half, CELLS, LANES)] * n_dom,
        [
            pltpu.VMEM((3, rows), f32),
            pltpu.VMEM((3, rows), f32),
            pltpu.VMEM((1, rows), f32),
            pltpu.VMEM((1, rows), jnp.int32),
            pltpu.VMEM((1, rows), jnp.int32),
            pltpu.VMEM((1, rows), jnp.int32),
            pltpu.VMEM((8 * lanes, targets), f32),
            pltpu.SemaphoreType.DMA((4,)),
        ],
        name="pack",
        n_any=4,
        vmem_mib=63,
    )(me, counts, positions, velocities, masses.reshape(1, rows), owner_cell.reshape(1, rows))

    def swapped(parts):
        return [parts[0]] + [
            sent(parts[-k % n_dom], n_slab, n_dom, 0, -k) for k in range(1, n_dom)
        ]

    places = swapped(whole[:n_dom])
    places[0] = call(copy_kernel, 0, 1, shape(half, tall, LANES), name="own_piece")(places[0])
    shells = call(
        functools.partial(join_kernel, n_dom), 1, n_dom, shape(4, tall, LANES), name="join"
    )(me, *places)
    shells, held = lax.optimization_barrier((shells, whole[n_dom:]))
    speeds = swapped(held)
    planes = call(
        functools.partial(speeds_kernel, n_dom),
        1,
        1 + n_dom,
        shape(7, CELLS, LANES),
        name="speeds",
    )(me, shells, *speeds)
    below, above = (sent(shells, n_slab, n_dom, side, 0) for side in (1, -1))
    early = sent(planes, n_slab, n_dom, n_slab // 2, 0)

    def pair_work(size):
        return [pltpu.VMEM((size, LANES), f32)] * 4

    def row_work(copies):
        return (
            [pltpu.VMEM((tall * 8, LANES), f32)]
            + [pltpu.VMEM((tall, FEATURES, LANES), bf16)] * copies
            + [pltpu.VMEM((tall, 16, LANES), bf16)] * copies
        )

    near, sums = call(
        own_kernel,
        0,
        1,
        [shape(CELLS, FEATURES, LANES, dtype=bf16), shape(CELLS, 16, LANES)],
        row_work(1) + pair_work(768),
        name="own_slab",
        cost=pl.CostEstimate(flops=8_000_000_000, bytes_accessed=1_000_000, transcendentals=0),
    )(shells)
    accels = []
    cut = CELLS * 3 // 4
    for cells in ((0, cut), (cut, CELLS)):
        count = cells[1] - cells[0]
        accels.append(
            call(
                functools.partial(side_kernel, cells),
                0,
                5,
                shape(3, count, LANES),
                row_work(2) + [pltpu.VMEM((count, 16, LANES), f32)] + pair_work(768),
                name="side_slabs",
                cost=pl.CostEstimate(flops=8_000_000_000, bytes_accessed=1_000_000, transcendentals=0),
            )(below, above, near, sums, shells)
        )
    later = [sent(accel, n_slab, n_dom, n_slab // 2, 0) for accel in accels]
    out = shape(10, 1, CELLS, LANES)
    state = call(kick_kernel, 0, 3, out, name="state")(planes, *accels)
    part = call(kick_kernel, 0, 2, out, name="buddy")(early, later[0])
    buddy = call(
        functools.partial(last_kick_kernel, cut),
        0,
        2,
        out,
        [pltpu.VMEM((6, 1, CELLS - cut, LANES), f32), pltpu.SemaphoreType.DMA],
        name="buddy_end",
        n_any=1,
        n_same=1,
    )(part, early, later[1])
    return state, buddy


def solution(mesh):
    placed = (
        P(None, ("slab", "dom")),
        P(None, ("slab", "dom")),
        P(("slab", "dom")),
        P(("slab", "dom"), None),
        P(("slab", "dom")),
    )
    return jax.shard_map(
        per_device,
        mesh=mesh,
        in_specs=placed,
        out_specs=(P(None, "slab", "dom", None), P(None, "slab", "dom", None)),
        check_vma=False,
    )
```

```python
import functools
import math

import jax
import jax.numpy as jnp
from jax import lax
from jax.experimental import pallas as pl
from jax.experimental.pallas import tpu as pltpu
from jax.sharding import PartitionSpec as P

CELLS = 64
LANES = 128

drift_step = 0.5
kick_step = 0.5
soften = 0.25
reach = 4.0
coupling = 0.25

scale = math.log2(math.e) / reach
fold = scale**1.5 * math.exp(soften / reach)

f32 = jnp.float32
bf16 = jnp.bfloat16
NN = (((1,), (0,)), ((), ()))
NT = (((1,), (1,)), ((), ()))
TN = (((0,), (0,)), ((), ()))
FEATURES = 32
EDGES = 8


def split(value, pieces):
    parts = []
    for _ in range(pieces):
        head = value.astype(bf16).astype(f32)
        parts.append(head)
        value = value - head
    return parts


def pack_kernel(n_dom, me_ref, count_ref, pos_any, vel_any, mass_any, owner_any, *refs):
    outs, refs = refs[: 2 * n_dom], refs[2 * n_dom :]
    pos_ref, vel_ref, mass_ref, owner_ref, rank_ref, target_ref, total_ref, sems = refs
    copies = [
        pltpu.make_async_copy(source, target, sems.at[i])
        for i, (source, target) in enumerate(
            [(owner_any, owner_ref), (pos_any, pos_ref), (vel_any, vel_ref), (mass_any, mass_ref)]
        )
    ]
    for copy in copies:
        copy.start()
    rows = pos_ref.shape[1]
    targets, lanes = n_dom * CELLS, LANES // n_dom
    part = lanes // 2
    chunk = 256
    before = (
        lax.broadcasted_iota(jnp.int32, (chunk, chunk + LANES), 0)
        < lax.broadcasted_iota(jnp.int32, (chunk, chunk + LANES), 1)
    ).astype(f32).astype(bf16)
    carry = jnp.zeros((targets, LANES), f32)
    number = lax.broadcasted_iota(jnp.int32, (targets, chunk), 0)
    copies[0].wait()
    for at in range(0, rows, chunk):
        target = owner_ref[:, at : at + chunk] - me_ref[0] * CELLS
        target = jnp.where(target < 0, target + targets, target)
        place = lax.broadcasted_iota(jnp.int32, (1, chunk), 1) + at
        target = jnp.where(place < count_ref[0], target, -1)
        target_ref[:, at : at + chunk] = target
        same = number == target
        hot = jnp.where(same, 1.0, 0.0).astype(bf16)
        seen = lax.dot_general(hot, before, NN, preferred_element_type=f32)
        wide = jnp.concatenate([carry] * (chunk // LANES), axis=1)
        rank = jnp.sum(jnp.where(same, seen[:, :chunk] + wide, 0.0), axis=0, keepdims=True)
        rank_ref[:, at : at + chunk] = rank.astype(jnp.int32)
        carry = carry + seen[:, chunk:]
    for copy in copies[1:]:
        copy.wait()
    step = 1024
    row = lax.broadcasted_iota(jnp.int32, (part, step), 0)
    column = lax.broadcasted_iota(jnp.int32, (2 * targets, step), 0)
    for at in range(0, rows, step):
        span = slice(at, at + step)
        rank, target = rank_ref[:, span], target_ref[:, span]
        upper = rank >= part
        mark = row == jnp.where(upper, rank - part, rank)
        place = jnp.where(upper & (target >= 0), target + targets, target)
        hot = jnp.where(column == place, 1.0, 0.0).astype(bf16)
        values = [pos_ref[i : i + 1, span] + drift_step * vel_ref[i : i + 1, span] for i in range(3)]
        values += [mass_ref[:, span]]
        values += [vel_ref[i : i + 1, span] for i in range(3)]
        pieces = [split(value, 2) for value in values]
        left = [
            jnp.concatenate([jnp.where(mark, piece[k], 0.0).astype(bf16) for piece in pieces], axis=0)
            for k in range(2)
        ]
        found = lax.dot_general(
            jnp.concatenate(left, axis=1),
            jnp.concatenate([hot] * 2, axis=1),
            NT,
            preferred_element_type=f32,
        )
        for comp in range(7):
            for half in range(2):
                low = comp * lanes + half * part
                value = found[comp * part : (comp + 1) * part, half * targets : (half + 1) * targets]
                if at == 0:
                    total_ref[low : low + part] = value
                else:
                    total_ref[low : low + part] += value
    total_ref[7 * lanes :] = jnp.zeros((lanes, targets), f32)
    groups = 8 * lanes // LANES
    packed = [
        jnp.concatenate(
            [
                total_ref[g * LANES : (g + 1) * LANES, t : t + LANES].T
                for t in range(0, targets, LANES)
            ],
            axis=0,
        )
        for g in range(groups)
    ]
    for by in range(n_dom):
        low, high = by * CELLS, (by + 1) * CELLS
        edge_high, edge_low = high % targets, (low - 1) % targets
        for g in range(groups // 2):
            edges = jnp.concatenate(
                [
                    packed[g][edge_high : edge_high + 1],
                    packed[g][edge_low : edge_low + 1],
                    jnp.zeros((EDGES - 2, LANES), f32),
                ],
                axis=0,
            )
            outs[by][g] = jnp.concatenate([packed[g][low:high], edges], axis=0)
            outs[n_dom + by][g] = packed[groups // 2 + g][low:high]


def merged(pieces, comp, n_dom):
    lanes = LANES // n_dom
    group, inside = comp // n_dom, comp % n_dom
    plane = None
    for k, piece in enumerate(pieces):
        value = piece[group]
        shift = ((k - inside) % n_dom) * lanes
        if shift:
            value = pltpu.roll(value, shift, 1)
        if plane is None:
            plane = value
        else:
            lane = lax.broadcasted_iota(jnp.int32, value.shape, 1)
            plane = jnp.where(lane // lanes == k, value, plane)
    return plane


def build(shells_ref, cells, rows_ref, far_ref, sum_ref, near_ref=None):
    root = math.sqrt(scale)
    low, high = cells
    needed = [c % (CELLS + 2) for c in range(low - 1, high + 1)]
    groups_at = sorted({c // 8 * 8 for c in needed})
    rows_ref[...] = jnp.zeros_like(rows_ref)
    for at in groups_at:
        for comp in range(4):
            rows_ref[pl.ds(at * 8 + comp, 8, stride=8), :] = shells_ref[comp, at : at + 8, :]
    for at in groups_at:
        value = rows_ref[at * 8 : (at + 8) * 8]
        row = lax.broadcasted_iota(jnp.int32, value.shape, 0) % 8

        def spread(array):
            total = jnp.sum(array.reshape(8, 8, LANES), axis=1, keepdims=True)
            return jnp.broadcast_to(total, (8, 8, LANES)).reshape(64, LANES)

        mass = spread(jnp.where(row == 3, value, 0.0)) * (coupling * fold / root)
        place = jnp.where(row < 3, value * root, 0.0)
        norm = spread(place * place)
        h, m, l = split(place, 3)
        down = lambda array, by: pltpu.roll(array, by, 0)

        def ends(array, first):
            parts = split(array, 3)
            ones = (row >= 3 - first) & (row < 6 - first)
            kept = jnp.where(ones, 1.0, 0.0)
            for i in range(3):
                kept = jnp.where(row == first + i, parts[i], kept)
            return kept

        def put(ref, groups):
            both = [
                jnp.concatenate(
                    [groups[i].reshape(8, 8, LANES), groups[i + 1].reshape(8, 8, LANES)], axis=1
                )
                for i in range(0, len(groups), 2)
            ]
            count = min(8, ref.shape[0] - at)
            if count > 0:
                value = jnp.concatenate(both, axis=1).astype(bf16)
                ref[at : at + count] = value[:count]

        h3, m3, l3 = down(h, 3), down(m, 3), down(l, 3)
        put(far_ref, [h + m3, h + l3, h + m3, ends(norm, 3)])
        if near_ref is not None:
            near = [-2.0 * (h + h3), -2.0 * (m + h3), -2.0 * (l + m3)]
            put(near_ref, near + [ends(norm + scale * soften, 0)])
        terms = split(mass * jnp.where(row == 3, 1.0, place), 3)
        put(sum_ref, [terms[0] + down(terms[1], 4), terms[2]])


def pair_loop(cells, per, apart, far_rows, sum_rows, centre, out, dist, heavy):
    blocks = [(k, n) for k in range(3) for n in range(len(far_rows))]
    tall = LANES * len(blocks)
    wide = 3
    first, count = cells[0], cells[1] - cells[0]

    def beside(c, k):
        at = c + first + k - 1
        return jnp.where(at < 0, CELLS + 1, at) if k == 0 else at

    def distances(step, b):
        for u in range(per):
            c = step * per + u
            for at in range(0, len(blocks), apart):
                others = jnp.concatenate(
                    [far_rows[n][beside(c, k)] for k, n in blocks[at : at + apart]], axis=1
                )
                low = u * tall + at * LANES
                dist[b][low : low + apart * LANES] = lax.dot_general(
                    others, centre[c + first], TN, preferred_element_type=f32
                )

    def weights(b):
        for at in range(0, per * tall, 64):
            s = dist[b][at : at + 64]
            inverse = lax.rsqrt(s)
            heavy[b][at : at + 64] = jnp.exp2(-s) * (inverse * inverse * inverse)

    def sums(step, b):
        for u in range(per):
            c = step * per + u
            total = None
            for at in range(0, len(blocks), wide):
                terms = jnp.concatenate(
                    [sum_rows[n][beside(c, k)] for k, n in blocks[at : at + wide]], axis=1
                )
                low = u * tall + at * LANES
                w = heavy[b][low : low + wide * LANES]
                head = w.astype(bf16)
                tail = (w - head.astype(f32)).astype(bf16)
                part = lax.dot_general(
                    terms, jnp.concatenate([head, tail], axis=1), NN, preferred_element_type=f32
                )
                part = part[:, :LANES] + part[:, LANES:]
                total = part if total is None else total + part
            out[c] = total

    steps = count // per
    distances(0, 0)
    distances(1, 1)
    weights(0)

    def body(i, _):
        for b in range(2):
            step = 2 * i + b
            sums(step, b)
            weights(1 - b)
            distances(jnp.minimum(step + 2, steps - 1), b)
        return 0

    lax.fori_loop(0, steps // 2, body, 0, unroll=8)


def copy_kernel(source_ref, target_ref):
    target_ref[...] = source_ref[...]


def join_kernel(n_dom, me_ref, *refs):
    pieces, shells_ref = refs[:n_dom], refs[n_dom]
    turn = me_ref[0] * (LANES // n_dom)
    for comp in range(4):
        shells_ref[comp] = pltpu.roll(merged(pieces, comp, n_dom), turn, 1)


def speeds_kernel(n_dom, me_ref, shells_ref, *refs):
    pieces, planes_ref = refs[:n_dom], refs[n_dom]
    turn = me_ref[0] * (LANES // n_dom)
    planes_ref[:4] = shells_ref[:, :CELLS]
    for comp in range(3):
        planes_ref[4 + comp] = pltpu.roll(merged(pieces, comp, n_dom), turn, 1)


def own_kernel(shells_ref, near_out, out_ref, rows, far_rows, sum_rows, *work):
    build(shells_ref, (0, CELLS), rows, far_rows, sum_rows, near_out)
    pair_loop(
        (0, CELLS), 2, 1, [far_rows], [sum_rows], near_out, out_ref, work[0:2], work[2:4]
    )


def side_kernel(cells, up_ref, down_ref, near_ref, own_out, shells_ref, accel_ref, *refs):
    low, high = cells
    count = high - low
    rows, far_rows, sum_rows, out, work = refs[0], refs[1:3], refs[3:5], refs[5], refs[6:]
    for side, there_ref in enumerate((up_ref, down_ref)):
        build(there_ref, cells, rows, far_rows[side], sum_rows[side])
    pair_loop(cells, 1, 2, far_rows, sum_rows, near_ref, out, work[0:2], work[2:4])
    both = out[...] + own_out[low:high]
    both = (both[:, :8] + both[:, 8:]).reshape(count * 8, LANES)
    rows[: count * 8] = both + pltpu.roll(both, count * 8 - 4, 0)
    total = [rows[pl.ds(comp, count, stride=8), :] for comp in range(4)]
    live = shells_ref[3, low:high] > 0
    for comp in range(3):
        centre_at = shells_ref[comp, low:high] * math.sqrt(scale)
        accel_ref[comp] = jnp.where(live, total[comp] - centre_at * total[3], 0.0)


def kick_kernel(planes_ref, *refs):
    accels, out_ref = refs[:-1], refs[-1]
    for comp in range(4):
        out_ref[comp, 0] = planes_ref[comp]
    low = 0
    for accel_ref in accels:
        high = low + accel_ref.shape[1]
        for comp in range(3):
            accel = accel_ref[comp]
            out_ref[4 + comp, 0, low:high] = planes_ref[4 + comp, low:high] + kick_step * accel
            out_ref[7 + comp, 0, low:high] = accel
        low = high


def place_kernel(planes_ref, out_ref):
    for comp in range(4):
        out_ref[comp, 0] = planes_ref[comp]
    out_ref[4:] = jnp.zeros((6, 1) + planes_ref.shape[1:], f32)


def last_kick_kernel(low, _, planes_ref, accel_ref, out_ref, kicked, sem):
    high = low + accel_ref.shape[1]
    for comp in range(3):
        accel = accel_ref[comp]
        kicked[comp, 0] = planes_ref[4 + comp, low:high] + kick_step * accel
        kicked[3 + comp, 0] = accel
    copy = pltpu.make_async_copy(kicked, out_ref.at[4:10, :, low:high], sem)
    copy.start()
    copy.wait()


def call(
    kernel, n_smem, n_vmem, out_shape, scratch=(), name=None, cost=None, n_any=0, n_same=0, vmem_mib=48
):
    smem = pl.BlockSpec(memory_space=pltpu.SMEM)
    vmem = pl.BlockSpec(memory_space=pltpu.VMEM)
    here = pl.BlockSpec(memory_space=pltpu.HBM)
    return pl.pallas_call(
        kernel,
        in_specs=[smem] * n_smem + [here] * n_any + [vmem] * n_vmem,
        out_specs=jax.tree.map(lambda _: here if n_same else vmem, out_shape),
        out_shape=out_shape,
        scratch_shapes=scratch,
        name=name,
        compiler_params=pltpu.CompilerParams(vmem_limit_bytes=vmem_mib << 20),
        cost_estimate=cost,
        input_output_aliases={i: i for i in range(n_same)},
    )


def sent(value, n_slab, n_dom, by_slab, by_dom):
    pairs = [
        (s * n_dom + d, (s + by_slab) % n_slab * n_dom + (d + by_dom) % n_dom)
        for s in range(n_slab)
        for d in range(n_dom)
    ]
    return lax.ppermute(value, ("slab", "dom"), pairs)


def per_device(positions, velocities, masses, owner_cell, counts):
    n_slab, n_dom = lax.axis_size("slab"), lax.axis_size("dom")
    rows = positions.shape[1]
    lanes = LANES // n_dom
    targets = n_dom * CELLS
    half = 4 * lanes // LANES
    tall = CELLS + EDGES
    me = lax.axis_index("dom").astype(jnp.int32).reshape(1)
    shape = lambda *dims, dtype=f32: jax.ShapeDtypeStruct(dims, dtype)

    whole = call(
        functools.partial(pack_kernel, n_dom),
        2,
        0,
        [shape(half, tall, LANES)] * n_dom + [shape(half, CELLS, LANES)] * n_dom,
        [
            pltpu.VMEM((3, rows), f32),
            pltpu.VMEM((3, rows), f32),
            pltpu.VMEM((1, rows), f32),
            pltpu.VMEM((1, rows), jnp.int32),
            pltpu.VMEM((1, rows), jnp.int32),
            pltpu.VMEM((1, rows), jnp.int32),
            pltpu.VMEM((8 * lanes, targets), f32),
            pltpu.SemaphoreType.DMA((4,)),
        ],
        name="pack",
        n_any=4,
        vmem_mib=63,
    )(me, counts, positions, velocities, masses.reshape(1, rows), owner_cell.reshape(1, rows))

    def swapped(parts):
        return [parts[0]] + [
            sent(parts[-k % n_dom], n_slab, n_dom, 0, -k) for k in range(1, n_dom)
        ]

    places, speeds = swapped(whole[:n_dom]), swapped(whole[n_dom:])
    places[0] = call(copy_kernel, 0, 1, shape(half, tall, LANES), name="own_piece")(places[0])
    shells = call(
        functools.partial(join_kernel, n_dom), 1, n_dom, shape(4, tall, LANES), name="join"
    )(me, *places)
    planes = call(
        functools.partial(speeds_kernel, n_dom),
        1,
        1 + n_dom,
        shape(7, CELLS, LANES),
        name="speeds",
    )(me, shells, *speeds)
    below, above = (sent(shells, n_slab, n_dom, side, 0) for side in (1, -1))
    early = sent(planes, n_slab, n_dom, n_slab // 2, 0)

    def pair_work(size):
        return [pltpu.VMEM((size, LANES), f32)] * 4

    def row_work(copies):
        return (
            [pltpu.VMEM((tall * 8, LANES), f32)]
            + [pltpu.VMEM((tall, FEATURES, LANES), bf16)] * copies
            + [pltpu.VMEM((tall, 16, LANES), bf16)] * copies
        )

    near, sums = call(
        own_kernel,
        0,
        1,
        [shape(CELLS, FEATURES, LANES, dtype=bf16), shape(CELLS, 16, LANES)],
        row_work(1) + pair_work(768),
        name="own_slab",
        cost=pl.CostEstimate(flops=8_000_000_000, bytes_accessed=1_000_000, transcendentals=0),
    )(shells)
    accel = call(
        functools.partial(side_kernel, (0, CELLS)),
        0,
        5,
        shape(3, CELLS, LANES),
        row_work(2) + [pltpu.VMEM((CELLS, 16, LANES), f32)] + pair_work(768),
        name="side_slabs",
        cost=pl.CostEstimate(flops=8_000_000_000, bytes_accessed=1_000_000, transcendentals=0),
    )(below, above, near, sums, shells)
    later = sent(accel, n_slab, n_dom, n_slab // 2, 0)
    out = shape(10, 1, CELLS, LANES)
    state = call(kick_kernel, 0, 2, out, name="state")(planes, accel)
    part = call(place_kernel, 0, 1, out, name="buddy")(early)
    buddy = call(
        functools.partial(last_kick_kernel, 0),
        0,
        2,
        out,
        [pltpu.VMEM((6, 1, CELLS, LANES), f32), pltpu.SemaphoreType.DMA],
        name="buddy_end",
        n_any=1,
        n_same=1,
    )(part, early, later)
    return state, buddy


def solution(mesh):
    placed = (
        P(None, ("slab", "dom")),
        P(None, ("slab", "dom")),
        P(("slab", "dom")),
        P(("slab", "dom"), None),
        P(("slab", "dom")),
    )
    return jax.shard_map(
        per_device,
        mesh=mesh,
        in_specs=placed,
        out_specs=(P(None, "slab", "dom", None), P(None, "slab", "dom", None)),
        check_vma=False,
    )
```

```python
import functools
import math

import jax
import jax.numpy as jnp
from jax import lax
from jax.experimental import pallas as pl
from jax.experimental.pallas import tpu as pltpu
from jax.sharding import PartitionSpec as P

CELLS = 64
LANES = 128

drift_step = 0.5
kick_step = 0.5
soften = 0.25
reach = 4.0
coupling = 0.25

scale = math.log2(math.e) / reach
fold = scale**1.5 * math.exp(soften / reach)

f32 = jnp.float32
bf16 = jnp.bfloat16
NN = (((1,), (0,)), ((), ()))
NT = (((1,), (1,)), ((), ()))
TN = (((0,), (0,)), ((), ()))
FEATURES = 32
EDGES = 8


def split(value, pieces):
    parts = []
    for _ in range(pieces):
        head = value.astype(bf16).astype(f32)
        parts.append(head)
        value = value - head
    return parts


def pack_kernel(n_dom, me_ref, count_ref, pos_any, vel_any, mass_any, owner_any, *refs):
    outs, refs = refs[: 2 * n_dom], refs[2 * n_dom :]
    pos_ref, vel_ref, mass_ref, owner_ref, rank_ref, target_ref, total_ref, sems = refs
    copies = [
        pltpu.make_async_copy(source, target, sems.at[i])
        for i, (source, target) in enumerate(
            [(owner_any, owner_ref), (pos_any, pos_ref), (vel_any, vel_ref), (mass_any, mass_ref)]
        )
    ]
    for copy in copies:
        copy.start()
    rows = pos_ref.shape[1]
    targets, lanes = n_dom * CELLS, LANES // n_dom
    part = lanes // 2
    chunk = 256
    before = (
        lax.broadcasted_iota(jnp.int32, (chunk, chunk + LANES), 0)
        < lax.broadcasted_iota(jnp.int32, (chunk, chunk + LANES), 1)
    ).astype(f32).astype(bf16)
    carry = jnp.zeros((targets, LANES), f32)
    number = lax.broadcasted_iota(jnp.int32, (targets, chunk), 0)
    copies[0].wait()
    for at in range(0, rows, chunk):
        target = owner_ref[:, at : at + chunk] - me_ref[0] * CELLS
        target = jnp.where(target < 0, target + targets, target)
        place = lax.broadcasted_iota(jnp.int32, (1, chunk), 1) + at
        target = jnp.where(place < count_ref[0], target, -1)
        target_ref[:, at : at + chunk] = target
        same = number == target
        hot = jnp.where(same, 1.0, 0.0).astype(bf16)
        seen = lax.dot_general(hot, before, NN, preferred_element_type=f32)
        wide = jnp.concatenate([carry] * (chunk // LANES), axis=1)
        rank = jnp.sum(jnp.where(same, seen[:, :chunk] + wide, 0.0), axis=0, keepdims=True)
        rank_ref[:, at : at + chunk] = rank.astype(jnp.int32)
        carry = carry + seen[:, chunk:]
    for copy in copies[1:]:
        copy.wait()
    step = 1024
    row = lax.broadcasted_iota(jnp.int32, (part, step), 0)
    column = lax.broadcasted_iota(jnp.int32, (2 * targets, step), 0)
    for at in range(0, rows, step):
        span = slice(at, at + step)
        rank, target = rank_ref[:, span], target_ref[:, span]
        upper = rank >= part
        mark = row == jnp.where(upper, rank - part, rank)
        place = jnp.where(upper & (target >= 0), target + targets, target)
        hot = jnp.where(column == place, 1.0, 0.0).astype(bf16)
        values = [pos_ref[i : i + 1, span] + drift_step * vel_ref[i : i + 1, span] for i in range(3)]
        values += [mass_ref[:, span]]
        values += [vel_ref[i : i + 1, span] for i in range(3)]
        pieces = [split(value, 2) for value in values]
        left = [
            jnp.concatenate([jnp.where(mark, piece[k], 0.0).astype(bf16) for piece in pieces], axis=0)
            for k in range(2)
        ]
        found = lax.dot_general(
            jnp.concatenate(left, axis=1),
            jnp.concatenate([hot] * 2, axis=1),
            NT,
            preferred_element_type=f32,
        )
        for comp in range(7):
            for half in range(2):
                low = comp * lanes + half * part
                value = found[comp * part : (comp + 1) * part, half * targets : (half + 1) * targets]
                if at == 0:
                    total_ref[low : low + part] = value
                else:
                    total_ref[low : low + part] += value
    total_ref[7 * lanes :] = jnp.zeros((lanes, targets), f32)
    groups = 8 * lanes // LANES
    packed = [
        jnp.concatenate(
            [
                total_ref[g * LANES : (g + 1) * LANES, t : t + LANES].T
                for t in range(0, targets, LANES)
            ],
            axis=0,
        )
        for g in range(groups)
    ]
    for by in range(n_dom):
        low, high = by * CELLS, (by + 1) * CELLS
        edge_high, edge_low = high % targets, (low - 1) % targets
        for g in range(groups // 2):
            edges = jnp.concatenate(
                [
                    packed[g][edge_high : edge_high + 1],
                    packed[g][edge_low : edge_low + 1],
                    jnp.zeros((EDGES - 2, LANES), f32),
                ],
                axis=0,
            )
            outs[by][g] = jnp.concatenate([packed[g][low:high], edges], axis=0)
            outs[n_dom + by][g] = packed[groups // 2 + g][low:high]


def merged(pieces, comp, n_dom):
    lanes = LANES // n_dom
    group, inside = comp // n_dom, comp % n_dom
    plane = None
    for k, piece in enumerate(pieces):
        value = piece[group]
        shift = ((k - inside) % n_dom) * lanes
        if shift:
            value = pltpu.roll(value, shift, 1)
        if plane is None:
            plane = value
        else:
            lane = lax.broadcasted_iota(jnp.int32, value.shape, 1)
            plane = jnp.where(lane // lanes == k, value, plane)
    return plane


def build(shells_ref, cells, rows_ref, far_ref, sum_ref, near_ref=None):
    root = math.sqrt(scale)
    low, high = cells
    needed = [c % (CELLS + 2) for c in range(low - 1, high + 1)]
    groups_at = sorted({c // 8 * 8 for c in needed})
    rows_ref[...] = jnp.zeros_like(rows_ref)
    for at in groups_at:
        for comp in range(4):
            rows_ref[pl.ds(at * 8 + comp, 8, stride=8), :] = shells_ref[comp, at : at + 8, :]
    for at in groups_at:
        value = rows_ref[at * 8 : (at + 8) * 8]
        row = lax.broadcasted_iota(jnp.int32, value.shape, 0) % 8

        def spread(array):
            total = jnp.sum(array.reshape(8, 8, LANES), axis=1, keepdims=True)
            return jnp.broadcast_to(total, (8, 8, LANES)).reshape(64, LANES)

        mass = spread(jnp.where(row == 3, value, 0.0)) * (coupling * fold / root)
        place = jnp.where(row < 3, value * root, 0.0)
        norm = spread(place * place)
        h, m, l = split(place, 3)
        down = lambda array, by: pltpu.roll(array, by, 0)

        def ends(array, first):
            parts = split(array, 3)
            ones = (row >= 3 - first) & (row < 6 - first)
            kept = jnp.where(ones, 1.0, 0.0)
            for i in range(3):
                kept = jnp.where(row == first + i, parts[i], kept)
            return kept

        def put(ref, groups):
            both = [
                jnp.concatenate(
                    [groups[i].reshape(8, 8, LANES), groups[i + 1].reshape(8, 8, LANES)], axis=1
                )
                for i in range(0, len(groups), 2)
            ]
            count = min(8, ref.shape[0] - at)
            if count > 0:
                value = jnp.concatenate(both, axis=1).astype(bf16)
                ref[at : at + count] = value[:count]

        h3, m3, l3 = down(h, 3), down(m, 3), down(l, 3)
        put(far_ref, [h + m3, h + l3, h + m3, ends(norm, 3)])
        if near_ref is not None:
            near = [-2.0 * (h + h3), -2.0 * (m + h3), -2.0 * (l + m3)]
            put(near_ref, near + [ends(norm + scale * soften, 0)])
        terms = split(mass * jnp.where(row == 3, 1.0, place), 3)
        put(sum_ref, [terms[0] + down(terms[1], 4), terms[2]])


def pair_loop(cells, per, apart, wide, far_rows, sum_rows, centre, out, dist, heavy):
    blocks = [(k, n) for k in range(3) for n in range(len(far_rows))]
    tall = LANES * len(blocks)
    first, count = cells[0], cells[1] - cells[0]

    def beside(c, k):
        at = c + first + k - 1
        return jnp.where(at < 0, CELLS + 1, at) if k == 0 else at

    def distances(step, b):
        for u in range(per):
            c = step * per + u
            for at in range(0, len(blocks), apart):
                others = jnp.concatenate(
                    [far_rows[n][beside(c, k)] for k, n in blocks[at : at + apart]], axis=1
                )
                low = u * tall + at * LANES
                dist[b][low : low + apart * LANES] = lax.dot_general(
                    others, centre[c + first], TN, preferred_element_type=f32
                )

    def weights(b):
        for at in range(0, per * tall, 64):
            s = dist[b][at : at + 64]
            inverse = lax.rsqrt(s)
            heavy[b][at : at + 64] = jnp.exp2(-s) * (inverse * inverse * inverse)

    def sums(step, b):
        for u in range(per):
            c = step * per + u
            total = None
            for at in range(0, len(blocks), wide):
                terms = jnp.concatenate(
                    [sum_rows[n][beside(c, k)] for k, n in blocks[at : at + wide]], axis=1
                )
                low = u * tall + at * LANES
                w = heavy[b][low : low + wide * LANES]
                head = w.astype(bf16)
                tail = (w - head.astype(f32)).astype(bf16)
                part = lax.dot_general(
                    terms, jnp.concatenate([head, tail], axis=1), NN, preferred_element_type=f32
                )
                part = part[:, :LANES] + part[:, LANES:]
                total = part if total is None else total + part
            out[c] = total

    steps = count // per
    distances(0, 0)
    distances(1, 1)
    weights(0)

    def body(i, _):
        for b in range(2):
            step = 2 * i + b
            sums(step, b)
            weights(1 - b)
            distances(jnp.minimum(step + 2, steps - 1), b)
        return 0

    lax.fori_loop(0, steps // 2, body, 0, unroll=8)


def copy_kernel(source_ref, target_ref):
    target_ref[...] = source_ref[...]


def join_kernel(n_dom, me_ref, *refs):
    pieces, shells_ref = refs[:n_dom], refs[n_dom]
    turn = me_ref[0] * (LANES // n_dom)
    for comp in range(4):
        shells_ref[comp] = pltpu.roll(merged(pieces, comp, n_dom), turn, 1)


def speeds_kernel(n_dom, me_ref, shells_ref, *refs):
    pieces, planes_ref = refs[:n_dom], refs[n_dom]
    turn = me_ref[0] * (LANES // n_dom)
    planes_ref[:4] = shells_ref[:, :CELLS]
    for comp in range(3):
        planes_ref[4 + comp] = pltpu.roll(merged(pieces, comp, n_dom), turn, 1)


def own_kernel(shells_ref, near_out, out_ref, rows, far_rows, sum_rows, *work):
    build(shells_ref, (0, CELLS), rows, far_rows, sum_rows, near_out)
    pair_loop(
        (0, CELLS), 2, 1, 3, [far_rows], [sum_rows], near_out, out_ref, work[0:2], work[2:4]
    )


def side_kernel(cells, up_ref, down_ref, near_ref, own_out, shells_ref, accel_ref, *refs):
    low, high = cells
    count = high - low
    rows, far_rows, sum_rows, out, work = refs[0], refs[1:3], refs[3:5], refs[5], refs[6:]
    for side, there_ref in enumerate((up_ref, down_ref)):
        build(there_ref, cells, rows, far_rows[side], sum_rows[side])
    pair_loop(cells, 1, 6, 6, far_rows, sum_rows, near_ref, out, work[0:2], work[2:4])
    both = out[...] + own_out[low:high]
    both = (both[:, :8] + both[:, 8:]).reshape(count * 8, LANES)
    rows[: count * 8] = both + pltpu.roll(both, count * 8 - 4, 0)
    total = [rows[pl.ds(comp, count, stride=8), :] for comp in range(4)]
    live = shells_ref[3, low:high] > 0
    for comp in range(3):
        centre_at = shells_ref[comp, low:high] * math.sqrt(scale)
        accel_ref[comp] = jnp.where(live, total[comp] - centre_at * total[3], 0.0)


def kick_kernel(planes_ref, *refs):
    accels, out_ref = refs[:-1], refs[-1]
    for comp in range(4):
        out_ref[comp, 0] = planes_ref[comp]
    low = 0
    for accel_ref in accels:
        high = low + accel_ref.shape[1]
        for comp in range(3):
            accel = accel_ref[comp]
            out_ref[4 + comp, 0, low:high] = planes_ref[4 + comp, low:high] + kick_step * accel
            out_ref[7 + comp, 0, low:high] = accel
        low = high


def place_kernel(planes_ref, out_ref):
    for comp in range(4):
        out_ref[comp, 0] = planes_ref[comp]
    out_ref[4:] = jnp.zeros((6, 1) + planes_ref.shape[1:], f32)


def last_kick_kernel(low, _, planes_ref, accel_ref, out_ref, kicked, sem):
    high = low + accel_ref.shape[1]
    for comp in range(3):
        accel = accel_ref[comp]
        kicked[comp, 0] = planes_ref[4 + comp, low:high] + kick_step * accel
        kicked[3 + comp, 0] = accel
    copy = pltpu.make_async_copy(kicked, out_ref.at[4:10, :, low:high], sem)
    copy.start()
    copy.wait()


def call(
    kernel, n_smem, n_vmem, out_shape, scratch=(), name=None, cost=None, n_any=0, n_same=0, vmem_mib=48
):
    smem = pl.BlockSpec(memory_space=pltpu.SMEM)
    vmem = pl.BlockSpec(memory_space=pltpu.VMEM)
    here = pl.BlockSpec(memory_space=pltpu.HBM)
    return pl.pallas_call(
        kernel,
        in_specs=[smem] * n_smem + [here] * n_any + [vmem] * n_vmem,
        out_specs=jax.tree.map(lambda _: here if n_same else vmem, out_shape),
        out_shape=out_shape,
        scratch_shapes=scratch,
        name=name,
        compiler_params=pltpu.CompilerParams(vmem_limit_bytes=vmem_mib << 20),
        cost_estimate=cost,
        input_output_aliases={i: i for i in range(n_same)},
    )


def sent(value, n_slab, n_dom, by_slab, by_dom):
    pairs = [
        (s * n_dom + d, (s + by_slab) % n_slab * n_dom + (d + by_dom) % n_dom)
        for s in range(n_slab)
        for d in range(n_dom)
    ]
    return lax.ppermute(value, ("slab", "dom"), pairs)


def per_device(positions, velocities, masses, owner_cell, counts):
    n_slab, n_dom = lax.axis_size("slab"), lax.axis_size("dom")
    rows = positions.shape[1]
    lanes = LANES // n_dom
    targets = n_dom * CELLS
    half = 4 * lanes // LANES
    tall = CELLS + EDGES
    me = lax.axis_index("dom").astype(jnp.int32).reshape(1)
    shape = lambda *dims, dtype=f32: jax.ShapeDtypeStruct(dims, dtype)

    whole = call(
        functools.partial(pack_kernel, n_dom),
        2,
        0,
        [shape(half, tall, LANES)] * n_dom + [shape(half, CELLS, LANES)] * n_dom,
        [
            pltpu.VMEM((3, rows), f32),
            pltpu.VMEM((3, rows), f32),
            pltpu.VMEM((1, rows), f32),
            pltpu.VMEM((1, rows), jnp.int32),
            pltpu.VMEM((1, rows), jnp.int32),
            pltpu.VMEM((1, rows), jnp.int32),
            pltpu.VMEM((8 * lanes, targets), f32),
            pltpu.SemaphoreType.DMA((4,)),
        ],
        name="pack",
        n_any=4,
        vmem_mib=63,
    )(me, counts, positions, velocities, masses.reshape(1, rows), owner_cell.reshape(1, rows))

    def swapped(parts):
        return [parts[0]] + [
            sent(parts[-k % n_dom], n_slab, n_dom, 0, -k) for k in range(1, n_dom)
        ]

    places, speeds = swapped(whole[:n_dom]), swapped(whole[n_dom:])
    places[0] = call(copy_kernel, 0, 1, shape(half, tall, LANES), name="own_piece")(places[0])
    shells = call(
        functools.partial(join_kernel, n_dom), 1, n_dom, shape(4, tall, LANES), name="join"
    )(me, *places)
    planes = call(
        functools.partial(speeds_kernel, n_dom),
        1,
        1 + n_dom,
        shape(7, CELLS, LANES),
        name="speeds",
    )(me, shells, *speeds)
    below, above = (sent(shells, n_slab, n_dom, side, 0) for side in (1, -1))
    early = sent(planes, n_slab, n_dom, n_slab // 2, 0)

    ready, _ = lax.optimization_barrier((shells, planes))

    def pair_work(size):
        return [pltpu.VMEM((size, LANES), f32)] * 4

    def row_work(copies):
        return (
            [pltpu.VMEM((tall * 8, LANES), f32)]
            + [pltpu.VMEM((tall, FEATURES, LANES), bf16)] * copies
            + [pltpu.VMEM((tall, 16, LANES), bf16)] * copies
        )

    near, sums = call(
        own_kernel,
        0,
        1,
        [shape(CELLS, FEATURES, LANES, dtype=bf16), shape(CELLS, 16, LANES)],
        row_work(1) + pair_work(768),
        name="own_slab",
        cost=pl.CostEstimate(flops=8_000_000_000, bytes_accessed=1_000_000, transcendentals=0),
    )(ready)
    accel = call(
        functools.partial(side_kernel, (0, CELLS)),
        0,
        5,
        shape(3, CELLS, LANES),
        row_work(2) + [pltpu.VMEM((CELLS, 16, LANES), f32)] + pair_work(768),
        name="side_slabs",
        cost=pl.CostEstimate(flops=8_000_000_000, bytes_accessed=1_000_000, transcendentals=0),
    )(below, above, near, sums, shells)
    later = sent(accel, n_slab, n_dom, n_slab // 2, 0)
    out = shape(10, 1, CELLS, LANES)
    state = call(kick_kernel, 0, 2, out, name="state")(planes, accel)
    part = call(place_kernel, 0, 1, out, name="buddy")(early)
    buddy = call(
        functools.partial(last_kick_kernel, 0),
        0,
        2,
        out,
        [pltpu.VMEM((6, 1, CELLS, LANES), f32), pltpu.SemaphoreType.DMA],
        name="buddy_end",
        n_any=1,
        n_same=1,
    )(part, early, later)
    return state, buddy


def solution(mesh):
    placed = (
        P(None, ("slab", "dom")),
        P(None, ("slab", "dom")),
        P(("slab", "dom")),
        P(("slab", "dom"), None),
        P(("slab", "dom")),
    )
    return jax.shard_map(
        per_device,
        mesh=mesh,
        in_specs=placed,
        out_specs=(P(None, "slab", "dom", None), P(None, "slab", "dom", None)),
        check_vma=False,
    )
```

```python
import functools
import math

import jax
import jax.numpy as jnp
from jax import lax
from jax.experimental import pallas as pl
from jax.experimental.pallas import tpu as pltpu
from jax.sharding import PartitionSpec as P

CELLS = 64
LANES = 128

drift_step = 0.5
kick_step = 0.5
soften = 0.25
reach = 4.0
coupling = 0.25

scale = math.log2(math.e) / reach
fold = scale**1.5 * math.exp(soften / reach)

f32 = jnp.float32
bf16 = jnp.bfloat16
NN = (((1,), (0,)), ((), ()))
NT = (((1,), (1,)), ((), ()))
TN = (((0,), (0,)), ((), ()))
FEATURES = 32
EDGES = 8


def split(value, pieces):
    parts = []
    for _ in range(pieces):
        head = value.astype(bf16).astype(f32)
        parts.append(head)
        value = value - head
    return parts


def pack_kernel(n_dom, me_ref, count_ref, pos_any, vel_any, mass_any, owner_any, *refs):
    outs, refs = refs[: 2 * n_dom], refs[2 * n_dom :]
    pos_ref, vel_ref, mass_ref, owner_ref, rank_ref, target_ref, total_ref, sems = refs
    copies = [
        pltpu.make_async_copy(source, target, sems.at[i])
        for i, (source, target) in enumerate(
            [(owner_any, owner_ref), (pos_any, pos_ref), (vel_any, vel_ref), (mass_any, mass_ref)]
        )
    ]
    for copy in copies:
        copy.start()
    rows = pos_ref.shape[1]
    targets, lanes = n_dom * CELLS, LANES // n_dom
    part = lanes // 2
    chunk = 256
    before = (
        lax.broadcasted_iota(jnp.int32, (chunk, chunk + LANES), 0)
        < lax.broadcasted_iota(jnp.int32, (chunk, chunk + LANES), 1)
    ).astype(f32).astype(bf16)
    carry = jnp.zeros((targets, LANES), f32)
    number = lax.broadcasted_iota(jnp.int32, (targets, chunk), 0)
    copies[0].wait()
    for at in range(0, rows, chunk):
        target = owner_ref[:, at : at + chunk] - me_ref[0] * CELLS
        target = jnp.where(target < 0, target + targets, target)
        place = lax.broadcasted_iota(jnp.int32, (1, chunk), 1) + at
        target = jnp.where(place < count_ref[0], target, -1)
        target_ref[:, at : at + chunk] = target
        same = number == target
        hot = jnp.where(same, 1.0, 0.0).astype(bf16)
        seen = lax.dot_general(hot, before, NN, preferred_element_type=f32)
        wide = jnp.concatenate([carry] * (chunk // LANES), axis=1)
        rank = jnp.sum(jnp.where(same, seen[:, :chunk] + wide, 0.0), axis=0, keepdims=True)
        rank_ref[:, at : at + chunk] = rank.astype(jnp.int32)
        carry = carry + seen[:, chunk:]
    for copy in copies[1:]:
        copy.wait()
    step = 1024
    row = lax.broadcasted_iota(jnp.int32, (part, step), 0)
    column = lax.broadcasted_iota(jnp.int32, (2 * targets, step), 0)
    for at in range(0, rows, step):
        span = slice(at, at + step)
        rank, target = rank_ref[:, span], target_ref[:, span]
        upper = rank >= part
        mark = row == jnp.where(upper, rank - part, rank)
        place = jnp.where(upper & (target >= 0), target + targets, target)
        hot = jnp.where(column == place, 1.0, 0.0).astype(bf16)
        values = [pos_ref[i : i + 1, span] + drift_step * vel_ref[i : i + 1, span] for i in range(3)]
        values += [mass_ref[:, span]]
        values += [vel_ref[i : i + 1, span] for i in range(3)]
        pieces = [split(value, 2) for value in values]
        left = [
            jnp.concatenate([jnp.where(mark, piece[k], 0.0).astype(bf16) for piece in pieces], axis=0)
            for k in range(2)
        ]
        found = lax.dot_general(
            jnp.concatenate(left, axis=1),
            jnp.concatenate([hot] * 2, axis=1),
            NT,
            preferred_element_type=f32,
        )
        for comp in range(7):
            for half in range(2):
                low = comp * lanes + half * part
                value = found[comp * part : (comp + 1) * part, half * targets : (half + 1) * targets]
                if at == 0:
                    total_ref[low : low + part] = value
                else:
                    total_ref[low : low + part] += value
    total_ref[7 * lanes :] = jnp.zeros((lanes, targets), f32)
    groups = 8 * lanes // LANES
    packed = [
        jnp.concatenate(
            [
                total_ref[g * LANES : (g + 1) * LANES, t : t + LANES].T
                for t in range(0, targets, LANES)
            ],
            axis=0,
        )
        for g in range(groups)
    ]
    for by in range(n_dom):
        low, high = by * CELLS, (by + 1) * CELLS
        edge_high, edge_low = high % targets, (low - 1) % targets
        for g in range(groups // 2):
            edges = jnp.concatenate(
                [
                    packed[g][edge_high : edge_high + 1],
                    packed[g][edge_low : edge_low + 1],
                    jnp.zeros((EDGES - 2, LANES), f32),
                ],
                axis=0,
            )
            outs[by][g] = jnp.concatenate([packed[g][low:high], edges], axis=0)
            outs[n_dom + by][g] = packed[groups // 2 + g][low:high]


def merged(pieces, comp, n_dom):
    lanes = LANES // n_dom
    group, inside = comp // n_dom, comp % n_dom
    plane = None
    for k, piece in enumerate(pieces):
        value = piece[group]
        shift = ((k - inside) % n_dom) * lanes
        if shift:
            value = pltpu.roll(value, shift, 1)
        if plane is None:
            plane = value
        else:
            lane = lax.broadcasted_iota(jnp.int32, value.shape, 1)
            plane = jnp.where(lane // lanes == k, value, plane)
    return plane


def build(shells_ref, cells, rows_ref, far_ref, sum_ref, near_ref=None):
    root = math.sqrt(scale)
    low, high = cells
    needed = [c % (CELLS + 2) for c in range(low - 1, high + 1)]
    groups_at = sorted({c // 8 * 8 for c in needed})
    rows_ref[...] = jnp.zeros_like(rows_ref)
    for at in groups_at:
        for comp in range(4):
            rows_ref[pl.ds(at * 8 + comp, 8, stride=8), :] = shells_ref[comp, at : at + 8, :]
    for at in groups_at:
        value = rows_ref[at * 8 : (at + 8) * 8]
        row = lax.broadcasted_iota(jnp.int32, value.shape, 0) % 8

        def spread(array):
            total = jnp.sum(array.reshape(8, 8, LANES), axis=1, keepdims=True)
            return jnp.broadcast_to(total, (8, 8, LANES)).reshape(64, LANES)

        mass = spread(jnp.where(row == 3, value, 0.0)) * (coupling * fold / root)
        place = jnp.where(row < 3, value * root, 0.0)
        norm = spread(place * place)
        h, m, l = split(place, 3)
        down = lambda array, by: pltpu.roll(array, by, 0)

        def ends(array, first):
            parts = split(array, 3)
            ones = (row >= 3 - first) & (row < 6 - first)
            kept = jnp.where(ones, 1.0, 0.0)
            for i in range(3):
                kept = jnp.where(row == first + i, parts[i], kept)
            return kept

        def put(ref, groups):
            both = [
                jnp.concatenate(
                    [groups[i].reshape(8, 8, LANES), groups[i + 1].reshape(8, 8, LANES)], axis=1
                )
                for i in range(0, len(groups), 2)
            ]
            count = min(8, ref.shape[0] - at)
            if count > 0:
                value = jnp.concatenate(both, axis=1).astype(bf16)
                ref[at : at + count] = value[:count]

        h3, m3, l3 = down(h, 3), down(m, 3), down(l, 3)
        put(far_ref, [h + m3, h + l3, h + m3, ends(norm, 3)])
        if near_ref is not None:
            near = [-2.0 * (h + h3), -2.0 * (m + h3), -2.0 * (l + m3)]
            put(near_ref, near + [ends(norm + scale * soften, 0)])
        terms = split(mass * jnp.where(row == 3, 1.0, place), 3)
        put(sum_ref, [terms[0] + down(terms[1], 4), terms[2]])


def pair_loop(cells, per, apart, wide, far_rows, sum_rows, centre, out, dist, heavy):
    blocks = [(k, n) for k in range(3) for n in range(len(far_rows))]
    tall = LANES * len(blocks)
    first, count = cells[0], cells[1] - cells[0]

    def beside(c, k):
        at = c + first + k - 1
        return jnp.where(at < 0, CELLS + 1, at) if k == 0 else at

    def distances(step, b):
        for u in range(per):
            c = step * per + u
            for at in range(0, len(blocks), apart):
                others = jnp.concatenate(
                    [far_rows[n][beside(c, k)] for k, n in blocks[at : at + apart]], axis=1
                )
                low = u * tall + at * LANES
                dist[b][low : low + apart * LANES] = lax.dot_general(
                    others, centre[c + first], TN, preferred_element_type=f32
                )

    def weights(b):
        for at in range(0, per * tall, 64):
            s = dist[b][at : at + 64]
            inverse = lax.rsqrt(s)
            heavy[b][at : at + 64] = jnp.exp2(-s) * (inverse * inverse * inverse)

    def sums(step, b):
        for u in range(per):
            c = step * per + u
            total = None
            for at in range(0, len(blocks), wide):
                terms = jnp.concatenate(
                    [sum_rows[n][beside(c, k)] for k, n in blocks[at : at + wide]], axis=1
                )
                low = u * tall + at * LANES
                w = heavy[b][low : low + wide * LANES]
                head = w.astype(bf16)
                tail = (w - head.astype(f32)).astype(bf16)
                part = lax.dot_general(
                    terms, jnp.concatenate([head, tail], axis=1), NN, preferred_element_type=f32
                )
                part = part[:, :LANES] + part[:, LANES:]
                total = part if total is None else total + part
            out[c] = total

    steps = count // per
    distances(0, 0)
    distances(1, 1)
    weights(0)

    def body(i, _):
        for b in range(2):
            step = 2 * i + b
            sums(step, b)
            weights(1 - b)
            distances(jnp.minimum(step + 2, steps - 1), b)
        return 0

    lax.fori_loop(0, steps // 2, body, 0, unroll=8)


def copy_kernel(source_ref, target_ref):
    target_ref[...] = source_ref[...]


def join_kernel(n_dom, me_ref, *refs):
    pieces, shells_ref = refs[:n_dom], refs[n_dom]
    turn = me_ref[0] * (LANES // n_dom)
    for comp in range(4):
        shells_ref[comp] = pltpu.roll(merged(pieces, comp, n_dom), turn, 1)


def speeds_kernel(n_dom, me_ref, shells_ref, *refs):
    pieces, planes_ref = refs[:n_dom], refs[n_dom]
    turn = me_ref[0] * (LANES // n_dom)
    planes_ref[:4] = shells_ref[:, :CELLS]
    for comp in range(3):
        planes_ref[4 + comp] = pltpu.roll(merged(pieces, comp, n_dom), turn, 1)


def own_rows_kernel(shells_ref, near_ref, far_ref, sum_ref, rows):
    build(shells_ref, (0, CELLS), rows, far_ref, sum_ref, near_ref)


def own_kernel(near_ref, far_ref, sum_ref, out_ref, *work):
    pair_loop(
        (0, CELLS), 2, 1, 3, [far_ref], [sum_ref], near_ref, out_ref, work[0:2], work[2:4]
    )


def side_kernel(cells, up_ref, down_ref, near_ref, own_out, shells_ref, accel_ref, *refs):
    low, high = cells
    count = high - low
    rows, far_rows, sum_rows, out, work = refs[0], refs[1:3], refs[3:5], refs[5], refs[6:]
    for side, there_ref in enumerate((up_ref, down_ref)):
        build(there_ref, cells, rows, far_rows[side], sum_rows[side])
    pair_loop(cells, 1, 6, 6, far_rows, sum_rows, near_ref, out, work[0:2], work[2:4])
    both = out[...] + own_out[low:high]
    both = (both[:, :8] + both[:, 8:]).reshape(count * 8, LANES)
    rows[: count * 8] = both + pltpu.roll(both, count * 8 - 4, 0)
    total = [rows[pl.ds(comp, count, stride=8), :] for comp in range(4)]
    live = shells_ref[3, low:high] > 0
    for comp in range(3):
        centre_at = shells_ref[comp, low:high] * math.sqrt(scale)
        accel_ref[comp] = jnp.where(live, total[comp] - centre_at * total[3], 0.0)


def kick_kernel(planes_ref, *refs):
    accels, out_ref = refs[:-1], refs[-1]
    for comp in range(4):
        out_ref[comp, 0] = planes_ref[comp]
    low = 0
    for accel_ref in accels:
        high = low + accel_ref.shape[1]
        for comp in range(3):
            accel = accel_ref[comp]
            out_ref[4 + comp, 0, low:high] = planes_ref[4 + comp, low:high] + kick_step * accel
            out_ref[7 + comp, 0, low:high] = accel
        low = high


def place_kernel(planes_ref, out_ref):
    for comp in range(4):
        out_ref[comp, 0] = planes_ref[comp]
    out_ref[4:] = jnp.zeros((6, 1) + planes_ref.shape[1:], f32)


def last_kick_kernel(low, _, planes_ref, accel_ref, out_ref, kicked, sem):
    high = low + accel_ref.shape[1]
    for comp in range(3):
        accel = accel_ref[comp]
        kicked[comp, 0] = planes_ref[4 + comp, low:high] + kick_step * accel
        kicked[3 + comp, 0] = accel
    copy = pltpu.make_async_copy(kicked, out_ref.at[4:10, :, low:high], sem)
    copy.start()
    copy.wait()


def call(
    kernel, n_smem, n_vmem, out_shape, scratch=(), name=None, cost=None, n_any=0, n_same=0, vmem_mib=48
):
    smem = pl.BlockSpec(memory_space=pltpu.SMEM)
    vmem = pl.BlockSpec(memory_space=pltpu.VMEM)
    here = pl.BlockSpec(memory_space=pltpu.HBM)
    return pl.pallas_call(
        kernel,
        in_specs=[smem] * n_smem + [here] * n_any + [vmem] * n_vmem,
        out_specs=jax.tree.map(lambda _: here if n_same else vmem, out_shape),
        out_shape=out_shape,
        scratch_shapes=scratch,
        name=name,
        compiler_params=pltpu.CompilerParams(vmem_limit_bytes=vmem_mib << 20),
        cost_estimate=cost,
        input_output_aliases={i: i for i in range(n_same)},
    )


def sent(value, n_slab, n_dom, by_slab, by_dom):
    pairs = [
        (s * n_dom + d, (s + by_slab) % n_slab * n_dom + (d + by_dom) % n_dom)
        for s in range(n_slab)
        for d in range(n_dom)
    ]
    return lax.ppermute(value, ("slab", "dom"), pairs)


def per_device(positions, velocities, masses, owner_cell, counts):
    n_slab, n_dom = lax.axis_size("slab"), lax.axis_size("dom")
    rows = positions.shape[1]
    lanes = LANES // n_dom
    targets = n_dom * CELLS
    half = 4 * lanes // LANES
    tall = CELLS + EDGES
    me = lax.axis_index("dom").astype(jnp.int32).reshape(1)
    shape = lambda *dims, dtype=f32: jax.ShapeDtypeStruct(dims, dtype)

    whole = call(
        functools.partial(pack_kernel, n_dom),
        2,
        0,
        [shape(half, tall, LANES)] * n_dom + [shape(half, CELLS, LANES)] * n_dom,
        [
            pltpu.VMEM((3, rows), f32),
            pltpu.VMEM((3, rows), f32),
            pltpu.VMEM((1, rows), f32),
            pltpu.VMEM((1, rows), jnp.int32),
            pltpu.VMEM((1, rows), jnp.int32),
            pltpu.VMEM((1, rows), jnp.int32),
            pltpu.VMEM((8 * lanes, targets), f32),
            pltpu.SemaphoreType.DMA((4,)),
        ],
        name="pack",
        n_any=4,
        vmem_mib=63,
    )(me, counts, positions, velocities, masses.reshape(1, rows), owner_cell.reshape(1, rows))

    def swapped(parts):
        return [parts[0]] + [
            sent(parts[-k % n_dom], n_slab, n_dom, 0, -k) for k in range(1, n_dom)
        ]

    places, speeds = swapped(whole[:n_dom]), swapped(whole[n_dom:])
    places[0] = call(copy_kernel, 0, 1, shape(half, tall, LANES), name="own_piece")(places[0])
    shells = call(
        functools.partial(join_kernel, n_dom), 1, n_dom, shape(4, tall, LANES), name="join"
    )(me, *places)
    below, above = (sent(shells, n_slab, n_dom, side, 0) for side in (1, -1))
    near, far_rows, sum_rows = call(
        own_rows_kernel,
        0,
        1,
        [
            shape(CELLS, FEATURES, LANES, dtype=bf16),
            shape(tall, FEATURES, LANES, dtype=bf16),
            shape(tall, 16, LANES, dtype=bf16),
        ],
        [pltpu.VMEM((tall * 8, LANES), f32)],
        name="own_rows",
        cost=pl.CostEstimate(flops=1_000_000_000, bytes_accessed=1_000_000, transcendentals=0),
    )(shells)
    kept, near = lax.optimization_barrier((shells, near))
    planes = call(
        functools.partial(speeds_kernel, n_dom),
        1,
        1 + n_dom,
        shape(7, CELLS, LANES),
        name="speeds",
    )(me, kept, *speeds)
    early = sent(planes, n_slab, n_dom, n_slab // 2, 0)

    far_rows, _ = lax.optimization_barrier((far_rows, planes))

    def pair_work(size):
        return [pltpu.VMEM((size, LANES), f32)] * 4

    def row_work(copies):
        return (
            [pltpu.VMEM((tall * 8, LANES), f32)]
            + [pltpu.VMEM((tall, FEATURES, LANES), bf16)] * copies
            + [pltpu.VMEM((tall, 16, LANES), bf16)] * copies
        )

    sums = call(
        own_kernel,
        0,
        3,
        shape(CELLS, 16, LANES),
        pair_work(768),
        name="own_slab",
        cost=pl.CostEstimate(flops=8_000_000_000, bytes_accessed=1_000_000, transcendentals=0),
    )(near, far_rows, sum_rows)
    accel = call(
        functools.partial(side_kernel, (0, CELLS)),
        0,
        5,
        shape(3, CELLS, LANES),
        row_work(2) + [pltpu.VMEM((CELLS, 16, LANES), f32)] + pair_work(768),
        name="side_slabs",
        cost=pl.CostEstimate(flops=8_000_000_000, bytes_accessed=1_000_000, transcendentals=0),
    )(below, above, near, sums, shells)
    later = sent(accel, n_slab, n_dom, n_slab // 2, 0)
    out = shape(10, 1, CELLS, LANES)
    state = call(kick_kernel, 0, 2, out, name="state")(planes, accel)
    part = call(place_kernel, 0, 1, out, name="buddy")(early)
    buddy = call(
        functools.partial(last_kick_kernel, 0),
        0,
        2,
        out,
        [pltpu.VMEM((6, 1, CELLS, LANES), f32), pltpu.SemaphoreType.DMA],
        name="buddy_end",
        n_any=1,
        n_same=1,
    )(part, early, later)
    return state, buddy


def solution(mesh):
    placed = (
        P(None, ("slab", "dom")),
        P(None, ("slab", "dom")),
        P(("slab", "dom")),
        P(("slab", "dom"), None),
        P(("slab", "dom")),
    )
    return jax.shard_map(
        per_device,
        mesh=mesh,
        in_specs=placed,
        out_specs=(P(None, "slab", "dom", None), P(None, "slab", "dom", None)),
        check_vma=False,
    )
```

```python
import functools
import math

import jax
import jax.numpy as jnp
from jax import lax
from jax.experimental import pallas as pl
from jax.experimental.pallas import tpu as pltpu
from jax.sharding import PartitionSpec as P

CELLS = 64
LANES = 128

drift_step = 0.5
kick_step = 0.5
soften = 0.25
reach = 4.0
coupling = 0.25

scale = math.log2(math.e) / reach
fold = scale**1.5 * math.exp(soften / reach)

f32 = jnp.float32
bf16 = jnp.bfloat16
NN = (((1,), (0,)), ((), ()))
NT = (((1,), (1,)), ((), ()))
TN = (((0,), (0,)), ((), ()))
FEATURES = 32
EDGES = 8


def split(value, pieces):
    parts = []
    for _ in range(pieces):
        head = value.astype(bf16).astype(f32)
        parts.append(head)
        value = value - head
    return parts


def pack_kernel(n_dom, me_ref, count_ref, pos_any, vel_any, mass_any, owner_any, *refs):
    outs, refs = refs[: 2 * n_dom], refs[2 * n_dom :]
    pos_ref, vel_ref, mass_ref, owner_ref, rank_ref, target_ref, total_ref, sems = refs
    copies = [
        pltpu.make_async_copy(source, target, sems.at[i])
        for i, (source, target) in enumerate(
            [(owner_any, owner_ref), (pos_any, pos_ref), (vel_any, vel_ref), (mass_any, mass_ref)]
        )
    ]
    for copy in copies:
        copy.start()
    rows = pos_ref.shape[1]
    targets, lanes = n_dom * CELLS, LANES // n_dom
    part = lanes // 2
    chunk = 256
    before = (
        lax.broadcasted_iota(jnp.int32, (chunk, chunk + LANES), 0)
        < lax.broadcasted_iota(jnp.int32, (chunk, chunk + LANES), 1)
    ).astype(f32).astype(bf16)
    carry = jnp.zeros((targets, LANES), f32)
    number = lax.broadcasted_iota(jnp.int32, (targets, chunk), 0)
    copies[0].wait()
    for at in range(0, rows, chunk):
        target = owner_ref[:, at : at + chunk] - me_ref[0] * CELLS
        target = jnp.where(target < 0, target + targets, target)
        place = lax.broadcasted_iota(jnp.int32, (1, chunk), 1) + at
        target = jnp.where(place < count_ref[0], target, -1)
        target_ref[:, at : at + chunk] = target
        same = number == target
        hot = jnp.where(same, 1.0, 0.0).astype(bf16)
        seen = lax.dot_general(hot, before, NN, preferred_element_type=f32)
        wide = jnp.concatenate([carry] * (chunk // LANES), axis=1)
        rank = jnp.sum(jnp.where(same, seen[:, :chunk] + wide, 0.0), axis=0, keepdims=True)
        rank_ref[:, at : at + chunk] = rank.astype(jnp.int32)
        carry = carry + seen[:, chunk:]
    for copy in copies[1:]:
        copy.wait()
    step = 1024
    row = lax.broadcasted_iota(jnp.int32, (part, step), 0)
    column = lax.broadcasted_iota(jnp.int32, (2 * targets, step), 0)
    for at in range(0, rows, step):
        span = slice(at, at + step)
        rank, target = rank_ref[:, span], target_ref[:, span]
        upper = rank >= part
        mark = row == jnp.where(upper, rank - part, rank)
        place = jnp.where(upper & (target >= 0), target + targets, target)
        hot = jnp.where(column == place, 1.0, 0.0).astype(bf16)
        values = [pos_ref[i : i + 1, span] + drift_step * vel_ref[i : i + 1, span] for i in range(3)]
        values += [mass_ref[:, span]]
        values += [vel_ref[i : i + 1, span] for i in range(3)]
        pieces = [split(value, 2) for value in values]
        left = [
            jnp.concatenate([jnp.where(mark, piece[k], 0.0).astype(bf16) for piece in pieces], axis=0)
            for k in range(2)
        ]
        found = lax.dot_general(
            jnp.concatenate(left, axis=1),
            jnp.concatenate([hot] * 2, axis=1),
            NT,
            preferred_element_type=f32,
        )
        for comp in range(7):
            for half in range(2):
                low = comp * lanes + half * part
                value = found[comp * part : (comp + 1) * part, half * targets : (half + 1) * targets]
                if at == 0:
                    total_ref[low : low + part] = value
                else:
                    total_ref[low : low + part] += value
    total_ref[7 * lanes :] = jnp.zeros((lanes, targets), f32)
    groups = 8 * lanes // LANES
    packed = [
        jnp.concatenate(
            [
                total_ref[g * LANES : (g + 1) * LANES, t : t + LANES].T
                for t in range(0, targets, LANES)
            ],
            axis=0,
        )
        for g in range(groups)
    ]
    for by in range(n_dom):
        low, high = by * CELLS, (by + 1) * CELLS
        edge_high, edge_low = high % targets, (low - 1) % targets
        for g in range(groups // 2):
            edges = jnp.concatenate(
                [
                    packed[g][edge_high : edge_high + 1],
                    packed[g][edge_low : edge_low + 1],
                    jnp.zeros((EDGES - 2, LANES), f32),
                ],
                axis=0,
            )
            outs[by][g] = jnp.concatenate([packed[g][low:high], edges], axis=0)
            outs[n_dom + by][g] = packed[groups // 2 + g][low:high]


def merged(pieces, comp, n_dom):
    lanes = LANES // n_dom
    group, inside = comp // n_dom, comp % n_dom
    plane = None
    for k, piece in enumerate(pieces):
        value = piece[group]
        shift = ((k - inside) % n_dom) * lanes
        if shift:
            value = pltpu.roll(value, shift, 1)
        if plane is None:
            plane = value
        else:
            lane = lax.broadcasted_iota(jnp.int32, value.shape, 1)
            plane = jnp.where(lane // lanes == k, value, plane)
    return plane


def build(shells_ref, cells, rows_ref, far_ref, sum_ref, near_ref=None):
    root = math.sqrt(scale)
    low, high = cells
    needed = [c % (CELLS + 2) for c in range(low - 1, high + 1)]
    groups_at = sorted({c // 8 * 8 for c in needed})
    rows_ref[...] = jnp.zeros_like(rows_ref)
    for at in groups_at:
        for comp in range(4):
            rows_ref[pl.ds(at * 8 + comp, 8, stride=8), :] = shells_ref[comp, at : at + 8, :]
    for at in groups_at:
        value = rows_ref[at * 8 : (at + 8) * 8]
        row = lax.broadcasted_iota(jnp.int32, value.shape, 0) % 8

        def spread(array):
            total = jnp.sum(array.reshape(8, 8, LANES), axis=1, keepdims=True)
            return jnp.broadcast_to(total, (8, 8, LANES)).reshape(64, LANES)

        mass = spread(jnp.where(row == 3, value, 0.0)) * (coupling * fold / root)
        place = jnp.where(row < 3, value * root, 0.0)
        norm = spread(place * place)
        h, m, l = split(place, 3)
        down = lambda array, by: pltpu.roll(array, by, 0)

        def ends(array, first):
            parts = split(array, 3)
            ones = (row >= 3 - first) & (row < 6 - first)
            kept = jnp.where(ones, 1.0, 0.0)
            for i in range(3):
                kept = jnp.where(row == first + i, parts[i], kept)
            return kept

        def put(ref, groups):
            both = [
                jnp.concatenate(
                    [groups[i].reshape(8, 8, LANES), groups[i + 1].reshape(8, 8, LANES)], axis=1
                )
                for i in range(0, len(groups), 2)
            ]
            count = min(8, ref.shape[0] - at)
            if count > 0:
                value = jnp.concatenate(both, axis=1).astype(bf16)
                ref[at : at + count] = value[:count]

        h3, m3, l3 = down(h, 3), down(m, 3), down(l, 3)
        put(far_ref, [h + m3, h + l3, h + m3, ends(norm, 3)])
        if near_ref is not None:
            near = [-2.0 * (h + h3), -2.0 * (m + h3), -2.0 * (l + m3)]
            put(near_ref, near + [ends(norm + scale * soften, 0)])
        terms = split(mass * jnp.where(row == 3, 1.0, place), 3)
        put(sum_ref, [terms[0] + down(terms[1], 4), terms[2]])


def pair_loop(cells, per, apart, wide, far_rows, sum_rows, centre, out, dist, heavy):
    blocks = [(k, n) for k in range(3) for n in range(len(far_rows))]
    tall = LANES * len(blocks)
    first, count = cells[0], cells[1] - cells[0]

    def beside(c, k):
        at = c + first + k - 1
        return jnp.where(at < 0, CELLS + 1, at) if k == 0 else at

    def distances(step, b):
        for u in range(per):
            c = step * per + u
            for at in range(0, len(blocks), apart):
                others = jnp.concatenate(
                    [far_rows[n][beside(c, k)] for k, n in blocks[at : at + apart]], axis=1
                )
                low = u * tall + at * LANES
                dist[b][low : low + apart * LANES] = lax.dot_general(
                    others, centre[c + first], TN, preferred_element_type=f32
                )

    def weights(b):
        for at in range(0, per * tall, 64):
            s = dist[b][at : at + 64]
            inverse = lax.rsqrt(s)
            heavy[b][at : at + 64] = jnp.exp2(-s) * (inverse * inverse * inverse)

    def sums(step, b):
        for u in range(per):
            c = step * per + u
            total = None
            for at in range(0, len(blocks), wide):
                terms = jnp.concatenate(
                    [sum_rows[n][beside(c, k)] for k, n in blocks[at : at + wide]], axis=1
                )
                low = u * tall + at * LANES
                w = heavy[b][low : low + wide * LANES]
                head = w.astype(bf16)
                tail = (w - head.astype(f32)).astype(bf16)
                part = lax.dot_general(
                    terms, jnp.concatenate([head, tail], axis=1), NN, preferred_element_type=f32
                )
                part = part[:, :LANES] + part[:, LANES:]
                total = part if total is None else total + part
            out[c] = total

    steps = count // per
    distances(0, 0)
    distances(1, 1)
    weights(0)

    def body(i, _):
        for b in range(2):
            step = 2 * i + b
            sums(step, b)
            weights(1 - b)
            distances(jnp.minimum(step + 2, steps - 1), b)
        return 0

    lax.fori_loop(0, steps // 2, body, 0, unroll=8)


def copy_kernel(source_ref, target_ref):
    target_ref[...] = source_ref[...]


def join_kernel(n_dom, me_ref, *refs):
    pieces, shells_ref = refs[:n_dom], refs[n_dom]
    turn = me_ref[0] * (LANES // n_dom)
    for comp in range(4):
        shells_ref[comp] = pltpu.roll(merged(pieces, comp, n_dom), turn, 1)


def speeds_kernel(n_dom, me_ref, shells_ref, *refs):
    pieces, planes_ref = refs[:n_dom], refs[n_dom]
    turn = me_ref[0] * (LANES // n_dom)
    planes_ref[:4] = shells_ref[:, :CELLS]
    for comp in range(3):
        planes_ref[4 + comp] = pltpu.roll(merged(pieces, comp, n_dom), turn, 1)


def own_rows_kernel(shells_ref, near_ref, far_ref, sum_ref, rows):
    build(shells_ref, (0, CELLS), rows, far_ref, sum_ref, near_ref)


def own_kernel(cells, near_ref, far_ref, sum_ref, out_ref, *work):
    pair_loop(
        cells, 2, 1, 3, [far_ref], [sum_ref], near_ref, out_ref, work[0:2], work[2:4]
    )


def side_kernel(cells, up_ref, down_ref, near_ref, own_low, own_high, shells_ref, accel_ref, *refs):
    low, high = cells
    count = high - low
    rows, far_rows, sum_rows, out, work = refs[0], refs[1:3], refs[3:5], refs[5], refs[6:]
    for side, there_ref in enumerate((up_ref, down_ref)):
        build(there_ref, cells, rows, far_rows[side], sum_rows[side])
    pair_loop(cells, 1, 6, 6, far_rows, sum_rows, near_ref, out, work[0:2], work[2:4])
    both = out[...] + jnp.concatenate([own_low[...], own_high[...]], axis=0)[low:high]
    both = (both[:, :8] + both[:, 8:]).reshape(count * 8, LANES)
    rows[: count * 8] = both + pltpu.roll(both, count * 8 - 4, 0)
    total = [rows[pl.ds(comp, count, stride=8), :] for comp in range(4)]
    live = shells_ref[3, low:high] > 0
    for comp in range(3):
        centre_at = shells_ref[comp, low:high] * math.sqrt(scale)
        accel_ref[comp] = jnp.where(live, total[comp] - centre_at * total[3], 0.0)


def kick_kernel(planes_ref, *refs):
    accels, out_ref = refs[:-1], refs[-1]
    for comp in range(4):
        out_ref[comp, 0] = planes_ref[comp]
    low = 0
    for accel_ref in accels:
        high = low + accel_ref.shape[1]
        for comp in range(3):
            accel = accel_ref[comp]
            out_ref[4 + comp, 0, low:high] = planes_ref[4 + comp, low:high] + kick_step * accel
            out_ref[7 + comp, 0, low:high] = accel
        low = high


def place_kernel(planes_ref, out_ref):
    for comp in range(4):
        out_ref[comp, 0] = planes_ref[comp]
    out_ref[4:] = jnp.zeros((6, 1) + planes_ref.shape[1:], f32)


def last_kick_kernel(low, _, planes_ref, accel_ref, out_ref, kicked, sem):
    high = low + accel_ref.shape[1]
    for comp in range(3):
        accel = accel_ref[comp]
        kicked[comp, 0] = planes_ref[4 + comp, low:high] + kick_step * accel
        kicked[3 + comp, 0] = accel
    copy = pltpu.make_async_copy(kicked, out_ref.at[4:10, :, low:high], sem)
    copy.start()
    copy.wait()


def call(
    kernel, n_smem, n_vmem, out_shape, scratch=(), name=None, cost=None, n_any=0, n_same=0, vmem_mib=48
):
    smem = pl.BlockSpec(memory_space=pltpu.SMEM)
    vmem = pl.BlockSpec(memory_space=pltpu.VMEM)
    here = pl.BlockSpec(memory_space=pltpu.HBM)
    return pl.pallas_call(
        kernel,
        in_specs=[smem] * n_smem + [here] * n_any + [vmem] * n_vmem,
        out_specs=jax.tree.map(lambda _: here if n_same else vmem, out_shape),
        out_shape=out_shape,
        scratch_shapes=scratch,
        name=name,
        compiler_params=pltpu.CompilerParams(vmem_limit_bytes=vmem_mib << 20),
        cost_estimate=cost,
        input_output_aliases={i: i for i in range(n_same)},
    )


def sent(value, n_slab, n_dom, by_slab, by_dom):
    pairs = [
        (s * n_dom + d, (s + by_slab) % n_slab * n_dom + (d + by_dom) % n_dom)
        for s in range(n_slab)
        for d in range(n_dom)
    ]
    return lax.ppermute(value, ("slab", "dom"), pairs)


def per_device(positions, velocities, masses, owner_cell, counts):
    n_slab, n_dom = lax.axis_size("slab"), lax.axis_size("dom")
    rows = positions.shape[1]
    lanes = LANES // n_dom
    targets = n_dom * CELLS
    half = 4 * lanes // LANES
    tall = CELLS + EDGES
    me = lax.axis_index("dom").astype(jnp.int32).reshape(1)
    shape = lambda *dims, dtype=f32: jax.ShapeDtypeStruct(dims, dtype)

    whole = call(
        functools.partial(pack_kernel, n_dom),
        2,
        0,
        [shape(half, tall, LANES)] * n_dom + [shape(half, CELLS, LANES)] * n_dom,
        [
            pltpu.VMEM((3, rows), f32),
            pltpu.VMEM((3, rows), f32),
            pltpu.VMEM((1, rows), f32),
            pltpu.VMEM((1, rows), jnp.int32),
            pltpu.VMEM((1, rows), jnp.int32),
            pltpu.VMEM((1, rows), jnp.int32),
            pltpu.VMEM((8 * lanes, targets), f32),
            pltpu.SemaphoreType.DMA((4,)),
        ],
        name="pack",
        n_any=4,
        vmem_mib=63,
    )(me, counts, positions, velocities, masses.reshape(1, rows), owner_cell.reshape(1, rows))

    def swapped(parts):
        return [parts[0]] + [
            sent(parts[-k % n_dom], n_slab, n_dom, 0, -k) for k in range(1, n_dom)
        ]

    places, speeds = swapped(whole[:n_dom]), swapped(whole[n_dom:])
    places[0] = call(copy_kernel, 0, 1, shape(half, tall, LANES), name="own_piece")(places[0])
    shells = call(
        functools.partial(join_kernel, n_dom), 1, n_dom, shape(4, tall, LANES), name="join"
    )(me, *places)
    below, above = (sent(shells, n_slab, n_dom, side, 0) for side in (1, -1))
    near, far_rows, sum_rows = call(
        own_rows_kernel,
        0,
        1,
        [
            shape(CELLS, FEATURES, LANES, dtype=bf16),
            shape(tall, FEATURES, LANES, dtype=bf16),
            shape(tall, 16, LANES, dtype=bf16),
        ],
        [pltpu.VMEM((tall * 8, LANES), f32)],
        name="own_rows",
        cost=pl.CostEstimate(flops=1_000_000_000, bytes_accessed=1_000_000, transcendentals=0),
    )(shells)

    def pair_work(size):
        return [pltpu.VMEM((size, LANES), f32)] * 4

    def own_sums(far_rows, *cells):
        return call(
            functools.partial(own_kernel, cells),
            0,
            3,
            shape(cells[1] - cells[0], 16, LANES),
            pair_work(768),
            name="own_slab",
            cost=pl.CostEstimate(flops=4_000_000_000, bytes_accessed=1_000_000, transcendentals=0),
        )(near, far_rows, sum_rows)

    low_sums = own_sums(far_rows, 0, CELLS // 2)
    kept, low_sums = lax.optimization_barrier((shells, low_sums))
    planes = call(
        functools.partial(speeds_kernel, n_dom),
        1,
        1 + n_dom,
        shape(7, CELLS, LANES),
        name="speeds",
    )(me, kept, *speeds)
    early = sent(planes, n_slab, n_dom, n_slab // 2, 0)

    far_rows, _ = lax.optimization_barrier((far_rows, planes))
    high_sums = own_sums(far_rows, CELLS // 2, CELLS)

    def row_work(copies):
        return (
            [pltpu.VMEM((tall * 8, LANES), f32)]
            + [pltpu.VMEM((tall, FEATURES, LANES), bf16)] * copies
            + [pltpu.VMEM((tall, 16, LANES), bf16)] * copies
        )

    accel = call(
        functools.partial(side_kernel, (0, CELLS)),
        0,
        6,
        shape(3, CELLS, LANES),
        row_work(2) + [pltpu.VMEM((CELLS, 16, LANES), f32)] + pair_work(768),
        name="side_slabs",
        cost=pl.CostEstimate(flops=8_000_000_000, bytes_accessed=1_000_000, transcendentals=0),
    )(below, above, near, low_sums, high_sums, shells)
    later = sent(accel, n_slab, n_dom, n_slab // 2, 0)
    out = shape(10, 1, CELLS, LANES)
    state = call(kick_kernel, 0, 2, out, name="state")(planes, accel)
    part = call(place_kernel, 0, 1, out, name="buddy")(early)
    buddy = call(
        functools.partial(last_kick_kernel, 0),
        0,
        2,
        out,
        [pltpu.VMEM((6, 1, CELLS, LANES), f32), pltpu.SemaphoreType.DMA],
        name="buddy_end",
        n_any=1,
        n_same=1,
    )(part, early, later)
    return state, buddy


def solution(mesh):
    placed = (
        P(None, ("slab", "dom")),
        P(None, ("slab", "dom")),
        P(("slab", "dom")),
        P(("slab", "dom"), None),
        P(("slab", "dom")),
    )
    return jax.shard_map(
        per_device,
        mesh=mesh,
        in_specs=placed,
        out_specs=(P(None, "slab", "dom", None), P(None, "slab", "dom", None)),
        check_vma=False,
    )
```

```python
import functools
import math

import jax
import jax.numpy as jnp
from jax import lax
from jax.experimental import pallas as pl
from jax.experimental.pallas import tpu as pltpu
from jax.sharding import PartitionSpec as P

CELLS = 64
LANES = 128

drift_step = 0.5
kick_step = 0.5
soften = 0.25
reach = 4.0
coupling = 0.25

scale = math.log2(math.e) / reach
fold = scale**1.5 * math.exp(soften / reach)

f32 = jnp.float32
bf16 = jnp.bfloat16
NN = (((1,), (0,)), ((), ()))
NT = (((1,), (1,)), ((), ()))
TN = (((0,), (0,)), ((), ()))
FEATURES = 32
EDGES = 8


def split(value, pieces):
    parts = []
    for _ in range(pieces):
        head = value.astype(bf16).astype(f32)
        parts.append(head)
        value = value - head
    return parts


def pack_kernel(n_dom, me_ref, count_ref, pos_any, vel_any, mass_any, owner_any, *refs):
    outs, refs = refs[: 2 * n_dom], refs[2 * n_dom :]
    pos_ref, vel_ref, mass_ref, owner_ref, rank_ref, target_ref, total_ref, sems = refs
    copies = [
        pltpu.make_async_copy(source, target, sems.at[i])
        for i, (source, target) in enumerate(
            [(owner_any, owner_ref), (pos_any, pos_ref), (vel_any, vel_ref), (mass_any, mass_ref)]
        )
    ]
    for copy in copies:
        copy.start()
    rows = pos_ref.shape[1]
    targets, lanes = n_dom * CELLS, LANES // n_dom
    part = lanes // 2
    chunk = 256
    before = (
        lax.broadcasted_iota(jnp.int32, (chunk, chunk + LANES), 0)
        < lax.broadcasted_iota(jnp.int32, (chunk, chunk + LANES), 1)
    ).astype(f32).astype(bf16)
    carry = jnp.zeros((targets, LANES), f32)
    number = lax.broadcasted_iota(jnp.int32, (targets, chunk), 0)
    copies[0].wait()
    for at in range(0, rows, chunk):
        target = owner_ref[:, at : at + chunk] - me_ref[0] * CELLS
        target = jnp.where(target < 0, target + targets, target)
        place = lax.broadcasted_iota(jnp.int32, (1, chunk), 1) + at
        target = jnp.where(place < count_ref[0], target, -1)
        target_ref[:, at : at + chunk] = target
        same = number == target
        hot = jnp.where(same, 1.0, 0.0).astype(bf16)
        seen = lax.dot_general(hot, before, NN, preferred_element_type=f32)
        wide = jnp.concatenate([carry] * (chunk // LANES), axis=1)
        rank = jnp.sum(jnp.where(same, seen[:, :chunk] + wide, 0.0), axis=0, keepdims=True)
        rank_ref[:, at : at + chunk] = rank.astype(jnp.int32)
        carry = carry + seen[:, chunk:]
    for copy in copies[1:]:
        copy.wait()
    step = 1024
    row = lax.broadcasted_iota(jnp.int32, (part, step), 0)
    column = lax.broadcasted_iota(jnp.int32, (2 * targets, step), 0)
    for at in range(0, rows, step):
        span = slice(at, at + step)
        rank, target = rank_ref[:, span], target_ref[:, span]
        upper = rank >= part
        mark = row == jnp.where(upper, rank - part, rank)
        place = jnp.where(upper & (target >= 0), target + targets, target)
        hot = jnp.where(column == place, 1.0, 0.0).astype(bf16)
        values = [pos_ref[i : i + 1, span] + drift_step * vel_ref[i : i + 1, span] for i in range(3)]
        values += [mass_ref[:, span]]
        values += [vel_ref[i : i + 1, span] for i in range(3)]
        pieces = [split(value, 2) for value in values]
        left = [
            jnp.concatenate([jnp.where(mark, piece[k], 0.0).astype(bf16) for piece in pieces], axis=0)
            for k in range(2)
        ]
        found = lax.dot_general(
            jnp.concatenate(left, axis=1),
            jnp.concatenate([hot] * 2, axis=1),
            NT,
            preferred_element_type=f32,
        )
        for comp in range(7):
            for half in range(2):
                low = comp * lanes + half * part
                value = found[comp * part : (comp + 1) * part, half * targets : (half + 1) * targets]
                if at == 0:
                    total_ref[low : low + part] = value
                else:
                    total_ref[low : low + part] += value
    total_ref[7 * lanes :] = jnp.zeros((lanes, targets), f32)
    groups = 8 * lanes // LANES
    packed = [
        jnp.concatenate(
            [
                total_ref[g * LANES : (g + 1) * LANES, t : t + LANES].T
                for t in range(0, targets, LANES)
            ],
            axis=0,
        )
        for g in range(groups)
    ]
    for by in range(n_dom):
        low, high = by * CELLS, (by + 1) * CELLS
        edge_high, edge_low = high % targets, (low - 1) % targets
        for g in range(groups // 2):
            edges = jnp.concatenate(
                [
                    packed[g][edge_high : edge_high + 1],
                    packed[g][edge_low : edge_low + 1],
                    jnp.zeros((EDGES - 2, LANES), f32),
                ],
                axis=0,
            )
            outs[by][g] = jnp.concatenate([packed[g][low:high], edges], axis=0)
            outs[n_dom + by][g] = packed[groups // 2 + g][low:high]


def merged(pieces, comp, n_dom):
    lanes = LANES // n_dom
    group, inside = comp // n_dom, comp % n_dom
    plane = None
    for k, piece in enumerate(pieces):
        value = piece[group]
        shift = ((k - inside) % n_dom) * lanes
        if shift:
            value = pltpu.roll(value, shift, 1)
        if plane is None:
            plane = value
        else:
            lane = lax.broadcasted_iota(jnp.int32, value.shape, 1)
            plane = jnp.where(lane // lanes == k, value, plane)
    return plane


def build(shells_ref, cells, rows_ref, far_ref, sum_ref, near_ref=None):
    root = math.sqrt(scale)
    low, high = cells
    needed = [c % (CELLS + 2) for c in range(low - 1, high + 1)]
    groups_at = sorted({c // 8 * 8 for c in needed})
    rows_ref[...] = jnp.zeros_like(rows_ref)
    for at in groups_at:
        for comp in range(4):
            rows_ref[pl.ds(at * 8 + comp, 8, stride=8), :] = shells_ref[comp, at : at + 8, :]
    for at in groups_at:
        value = rows_ref[at * 8 : (at + 8) * 8]
        row = lax.broadcasted_iota(jnp.int32, value.shape, 0) % 8

        def spread(array):
            total = jnp.sum(array.reshape(8, 8, LANES), axis=1, keepdims=True)
            return jnp.broadcast_to(total, (8, 8, LANES)).reshape(64, LANES)

        mass = spread(jnp.where(row == 3, value, 0.0)) * (coupling * fold / root)
        place = jnp.where(row < 3, value * root, 0.0)
        norm = spread(place * place)
        h, m, l = split(place, 3)
        down = lambda array, by: pltpu.roll(array, by, 0)

        def ends(array, first):
            parts = split(array, 3)
            ones = (row >= 3 - first) & (row < 6 - first)
            kept = jnp.where(ones, 1.0, 0.0)
            for i in range(3):
                kept = jnp.where(row == first + i, parts[i], kept)
            return kept

        def put(ref, groups):
            both = [
                jnp.concatenate(
                    [groups[i].reshape(8, 8, LANES), groups[i + 1].reshape(8, 8, LANES)], axis=1
                )
                for i in range(0, len(groups), 2)
            ]
            count = min(8, ref.shape[0] - at)
            if count > 0:
                value = jnp.concatenate(both, axis=1).astype(bf16)
                ref[at : at + count] = value[:count]

        h3, m3, l3 = down(h, 3), down(m, 3), down(l, 3)
        put(far_ref, [h + m3, h + l3, h + m3, ends(norm, 3)])
        if near_ref is not None:
            near = [-2.0 * (h + h3), -2.0 * (m + h3), -2.0 * (l + m3)]
            put(near_ref, near + [ends(norm + scale * soften, 0)])
        terms = split(mass * jnp.where(row == 3, 1.0, place), 3)
        put(sum_ref, [terms[0] + down(terms[1], 4), terms[2]])


def pair_loop(cells, per, apart, wide, far_rows, sum_rows, centre, out, dist, heavy):
    blocks = [(k, n) for k in range(3) for n in range(len(far_rows))]
    tall = LANES * len(blocks)
    first, count = cells[0], cells[1] - cells[0]

    def beside(c, k):
        at = c + first + k - 1
        return jnp.where(at < 0, CELLS + 1, at) if k == 0 else at

    def distances(step, b):
        for u in range(per):
            c = step * per + u
            for at in range(0, len(blocks), apart):
                others = jnp.concatenate(
                    [far_rows[n][beside(c, k)] for k, n in blocks[at : at + apart]], axis=1
                )
                low = u * tall + at * LANES
                dist[b][low : low + apart * LANES] = lax.dot_general(
                    others, centre[c + first], TN, preferred_element_type=f32
                )

    def weights(b):
        for at in range(0, per * tall, 64):
            s = dist[b][at : at + 64]
            inverse = lax.rsqrt(s)
            heavy[b][at : at + 64] = jnp.exp2(-s) * (inverse * inverse * inverse)

    def sums(step, b):
        for u in range(per):
            c = step * per + u
            total = None
            for at in range(0, len(blocks), wide):
                terms = jnp.concatenate(
                    [sum_rows[n][beside(c, k)] for k, n in blocks[at : at + wide]], axis=1
                )
                low = u * tall + at * LANES
                w = heavy[b][low : low + wide * LANES]
                head = w.astype(bf16)
                tail = (w - head.astype(f32)).astype(bf16)
                part = lax.dot_general(
                    terms, jnp.concatenate([head, tail], axis=1), NN, preferred_element_type=f32
                )
                part = part[:, :LANES] + part[:, LANES:]
                total = part if total is None else total + part
            out[c] = total

    steps = count // per
    distances(0, 0)
    distances(1, 1)
    weights(0)

    def body(i, _):
        for b in range(2):
            step = 2 * i + b
            sums(step, b)
            weights(1 - b)
            distances(jnp.minimum(step + 2, steps - 1), b)
        return 0

    unroll = max(u for u in range(1, 9) if steps // 2 % u == 0)
    lax.fori_loop(0, steps // 2, body, 0, unroll=unroll)


def copy_kernel(source_ref, target_ref):
    target_ref[...] = source_ref[...]


def join_kernel(n_dom, me_ref, *refs):
    pieces, shells_ref = refs[:n_dom], refs[n_dom]
    turn = me_ref[0] * (LANES // n_dom)
    for comp in range(4):
        shells_ref[comp] = pltpu.roll(merged(pieces, comp, n_dom), turn, 1)


def speeds_kernel(n_dom, me_ref, shells_ref, *refs):
    pieces, planes_ref = refs[:n_dom], refs[n_dom]
    turn = me_ref[0] * (LANES // n_dom)
    planes_ref[:4] = shells_ref[:, :CELLS]
    for comp in range(3):
        planes_ref[4 + comp] = pltpu.roll(merged(pieces, comp, n_dom), turn, 1)


def first_own_kernel(cells, shells_ref, near_ref, far_ref, sum_ref, out_ref, rows, *work):
    build(shells_ref, (0, CELLS), rows, far_ref, sum_ref, near_ref)
    own_kernel(cells, near_ref, far_ref, sum_ref, out_ref, *work)


def own_kernel(cells, near_ref, far_ref, sum_ref, out_ref, *work):
    pair_loop(
        cells, 2, 1, 3, [far_ref], [sum_ref], near_ref, out_ref, work[0:2], work[2:4]
    )


def side_kernel(cells, up_ref, down_ref, near_ref, own_low, own_high, shells_ref, accel_ref, *refs):
    low, high = cells
    count = high - low
    rows, far_rows, sum_rows, out, work = refs[0], refs[1:3], refs[3:5], refs[5], refs[6:]
    for side, there_ref in enumerate((up_ref, down_ref)):
        build(there_ref, cells, rows, far_rows[side], sum_rows[side])
    pair_loop(cells, 1, 6, 6, far_rows, sum_rows, near_ref, out, work[0:2], work[2:4])
    both = out[...] + jnp.concatenate([own_low[...], own_high[...]], axis=0)[low:high]
    both = (both[:, :8] + both[:, 8:]).reshape(count * 8, LANES)
    rows[: count * 8] = both + pltpu.roll(both, count * 8 - 4, 0)
    total = [rows[pl.ds(comp, count, stride=8), :] for comp in range(4)]
    live = shells_ref[3, low:high] > 0
    for comp in range(3):
        centre_at = shells_ref[comp, low:high] * math.sqrt(scale)
        accel_ref[comp] = jnp.where(live, total[comp] - centre_at * total[3], 0.0)


def kick_kernel(planes_ref, *refs):
    accels, out_ref = refs[:-1], refs[-1]
    for comp in range(4):
        out_ref[comp, 0] = planes_ref[comp]
    low = 0
    for accel_ref in accels:
        high = low + accel_ref.shape[1]
        for comp in range(3):
            accel = accel_ref[comp]
            out_ref[4 + comp, 0, low:high] = planes_ref[4 + comp, low:high] + kick_step * accel
            out_ref[7 + comp, 0, low:high] = accel
        low = high


def place_kernel(planes_ref, out_ref):
    for comp in range(4):
        out_ref[comp, 0] = planes_ref[comp]
    out_ref[4:] = jnp.zeros((6, 1) + planes_ref.shape[1:], f32)


def last_kick_kernel(low, _, planes_ref, accel_ref, out_ref, kicked, sem):
    high = low + accel_ref.shape[1]
    for comp in range(3):
        accel = accel_ref[comp]
        kicked[comp, 0] = planes_ref[4 + comp, low:high] + kick_step * accel
        kicked[3 + comp, 0] = accel
    copy = pltpu.make_async_copy(kicked, out_ref.at[4:10, :, low:high], sem)
    copy.start()
    copy.wait()


def call(
    kernel, n_smem, n_vmem, out_shape, scratch=(), name=None, cost=None, n_any=0, n_same=0, vmem_mib=48
):
    smem = pl.BlockSpec(memory_space=pltpu.SMEM)
    vmem = pl.BlockSpec(memory_space=pltpu.VMEM)
    here = pl.BlockSpec(memory_space=pltpu.HBM)
    return pl.pallas_call(
        kernel,
        in_specs=[smem] * n_smem + [here] * n_any + [vmem] * n_vmem,
        out_specs=jax.tree.map(lambda _: here if n_same else vmem, out_shape),
        out_shape=out_shape,
        scratch_shapes=scratch,
        name=name,
        compiler_params=pltpu.CompilerParams(vmem_limit_bytes=vmem_mib << 20),
        cost_estimate=cost,
        input_output_aliases={i: i for i in range(n_same)},
    )


def sent(value, n_slab, n_dom, by_slab, by_dom):
    pairs = [
        (s * n_dom + d, (s + by_slab) % n_slab * n_dom + (d + by_dom) % n_dom)
        for s in range(n_slab)
        for d in range(n_dom)
    ]
    return lax.ppermute(value, ("slab", "dom"), pairs)


def per_device(positions, velocities, masses, owner_cell, counts):
    n_slab, n_dom = lax.axis_size("slab"), lax.axis_size("dom")
    rows = positions.shape[1]
    lanes = LANES // n_dom
    targets = n_dom * CELLS
    half = 4 * lanes // LANES
    tall = CELLS + EDGES
    me = lax.axis_index("dom").astype(jnp.int32).reshape(1)
    shape = lambda *dims, dtype=f32: jax.ShapeDtypeStruct(dims, dtype)

    whole = call(
        functools.partial(pack_kernel, n_dom),
        2,
        0,
        [shape(half, tall, LANES)] * n_dom + [shape(half, CELLS, LANES)] * n_dom,
        [
            pltpu.VMEM((3, rows), f32),
            pltpu.VMEM((3, rows), f32),
            pltpu.VMEM((1, rows), f32),
            pltpu.VMEM((1, rows), jnp.int32),
            pltpu.VMEM((1, rows), jnp.int32),
            pltpu.VMEM((1, rows), jnp.int32),
            pltpu.VMEM((8 * lanes, targets), f32),
            pltpu.SemaphoreType.DMA((4,)),
        ],
        name="pack",
        n_any=4,
        vmem_mib=63,
    )(me, counts, positions, velocities, masses.reshape(1, rows), owner_cell.reshape(1, rows))

    def swapped(parts):
        return [parts[0]] + [
            sent(parts[-k % n_dom], n_slab, n_dom, 0, -k) for k in range(1, n_dom)
        ]

    places, speeds = swapped(whole[:n_dom]), swapped(whole[n_dom:])
    places[0] = call(copy_kernel, 0, 1, shape(half, tall, LANES), name="own_piece")(places[0])
    shells = call(
        functools.partial(join_kernel, n_dom), 1, n_dom, shape(4, tall, LANES), name="join"
    )(me, *places)
    below, above = (sent(shells, n_slab, n_dom, side, 0) for side in (1, -1))

    def pair_work(size):
        return [pltpu.VMEM((size, LANES), f32)] * 4

    cut = CELLS // 4
    near, far_rows, sum_rows, low_sums = call(
        functools.partial(first_own_kernel, (0, cut)),
        0,
        1,
        [
            shape(CELLS, FEATURES, LANES, dtype=bf16),
            shape(tall, FEATURES, LANES, dtype=bf16),
            shape(tall, 16, LANES, dtype=bf16),
            shape(cut, 16, LANES),
        ],
        [pltpu.VMEM((tall * 8, LANES), f32)] + pair_work(768),
        name="own_slab",
        cost=pl.CostEstimate(flops=8_000_000_000, bytes_accessed=1_000_000, transcendentals=0),
    )(shells)
    kept, low_sums = lax.optimization_barrier((shells, low_sums))
    planes = call(
        functools.partial(speeds_kernel, n_dom),
        1,
        1 + n_dom,
        shape(7, CELLS, LANES),
        name="speeds",
    )(me, kept, *speeds)
    early = sent(planes, n_slab, n_dom, n_slab // 2, 0)

    far_rows, _ = lax.optimization_barrier((far_rows, planes))
    high_sums = call(
        functools.partial(own_kernel, (cut, CELLS)),
        0,
        3,
        shape(CELLS - cut, 16, LANES),
        pair_work(768),
        name="own_slab",
        cost=pl.CostEstimate(flops=8_000_000_000, bytes_accessed=1_000_000, transcendentals=0),
    )(near, far_rows, sum_rows)

    def row_work(copies):
        return (
            [pltpu.VMEM((tall * 8, LANES), f32)]
            + [pltpu.VMEM((tall, FEATURES, LANES), bf16)] * copies
            + [pltpu.VMEM((tall, 16, LANES), bf16)] * copies
        )

    accel = call(
        functools.partial(side_kernel, (0, CELLS)),
        0,
        6,
        shape(3, CELLS, LANES),
        row_work(2) + [pltpu.VMEM((CELLS, 16, LANES), f32)] + pair_work(768),
        name="side_slabs",
        cost=pl.CostEstimate(flops=8_000_000_000, bytes_accessed=1_000_000, transcendentals=0),
    )(below, above, near, low_sums, high_sums, shells)
    later = sent(accel, n_slab, n_dom, n_slab // 2, 0)
    out = shape(10, 1, CELLS, LANES)
    state = call(kick_kernel, 0, 2, out, name="state")(planes, accel)
    part = call(place_kernel, 0, 1, out, name="buddy")(early)
    buddy = call(
        functools.partial(last_kick_kernel, 0),
        0,
        2,
        out,
        [pltpu.VMEM((6, 1, CELLS, LANES), f32), pltpu.SemaphoreType.DMA],
        name="buddy_end",
        n_any=1,
        n_same=1,
    )(part, early, later)
    return state, buddy


def solution(mesh):
    placed = (
        P(None, ("slab", "dom")),
        P(None, ("slab", "dom")),
        P(("slab", "dom")),
        P(("slab", "dom"), None),
        P(("slab", "dom")),
    )
    return jax.shard_map(
        per_device,
        mesh=mesh,
        in_specs=placed,
        out_specs=(P(None, "slab", "dom", None), P(None, "slab", "dom", None)),
        check_vma=False,
    )
```
